128 devices in a mesh: lat: 8 (over y, z_hi), lon: 16 (over x, z_lo, core).
Axes of the slice: x: 4, y: 4, z: 4 (z_hi: 2, z_lo: 2; z = z_hi * 2 + z_lo), core: 2. Of those that a mesh axis runs over, the one named last changes fastest.
Arguments:
- coarse: bfloat16 [73, 32, 128], P(None, 'lat', 'lon'), may hold values from -6 to 6
- row_src: int32 [256], P('lat'), may hold values from 0 to 30, as said below
- row_frac: float32 [256], P('lat'), may hold values from 0 to 1
- col_src: int32 [2048], P('lon'), may hold values from 0 to 127, as said below
- col_frac: float32 [2048], P('lon'), may hold values from 0 to 1
- embed_weight: bfloat16 [73, 128], replicated, may hold values from -0.75 to 0.75
- conv1_weight: bfloat16 [3, 3, 128, 128], replicated, may hold values from -0.1875 to 0.1875
- conv2_weight: bfloat16 [3, 3, 128, 128], replicated, may hold values from -0.1875 to 0.1875
- cotangent: bfloat16 [256, 2048, 128], P('lat', 'lon'), may hold values from -6 to 6
Outputs:
- features: bfloat16 [256, 2048, 128], P('lat', 'lon')
- grad_embed: float32 [73, 128], replicated
- grad_conv1: float32 [3, 3, 128, 128], replicated
- grad_conv2: float32 [3, 3, 128, 128], replicated
The draws below stay inside these ranges and needn't reach their ends.
Inputs may be any that keep to these rules, and one draw needn't show every extreme that they name: row_src[r] differs from (r * 32) // 256 by at most 1; both bounds are reached. col_src[c] differs cyclically (mod 128) from (c * 128) // 2048 by at most 1; both bounds are reached.
All inputs are finite; a program needn't handle non-finite values.
Results may differ from the reference program's by a relative error of at most 0.0062.
Values may be sent and summed in bfloat16 or wider, within the bound.
A program may use at most 128 MiB of HBM per device.

```python
import math
import jax
import jax.numpy as jnp
from jax import lax

CH_IN = 73
HID = 128
ROWS = 32
COLS = 128
CR_DEV = 4
CC_DEV = 8
FROWS = 256
FCOLS = 2048
CROWS = 32
CCOLS = 128


def draw_row_src(key, part):
    key = jax.random.fold_in(key, 11)
    line = jnp.arange(FROWS, dtype=jnp.int32)
    base = line * CROWS // FROWS
    offset = jax.random.randint(key, (FROWS,), -1, 2, dtype=jnp.int32)
    picked = jnp.clip(base + offset, 0, CROWS - 2)
    picked = picked.at[0].set(0)
    picked = picked.at[FROWS - 1].set(CROWS - 2)
    tiles = jnp.arange(1, FROWS // ROWS, dtype=jnp.int32)
    edge_value = tiles * CR_DEV - 1
    picked = picked.at[tiles * ROWS].set(edge_value)
    picked = picked.at[tiles * ROWS + 1].set(edge_value)
    return picked.astype(jnp.int32)


def draw_col_src(key, part):
    key = jax.random.fold_in(key, 23)
    line = jnp.arange(FCOLS, dtype=jnp.int32)
    base = line * CCOLS // FCOLS
    offset = jax.random.randint(key, (FCOLS,), -1, 2, dtype=jnp.int32)
    picked = jnp.mod(base + offset, CCOLS)
    picked = picked.at[2].set(0)
    picked = picked.at[FCOLS - 1].set(CCOLS - 1)
    tiles = jnp.arange(0, FCOLS // COLS, dtype=jnp.int32)
    edge_value = jnp.mod(tiles * CC_DEV - 1, CCOLS)
    picked = picked.at[tiles * COLS].set(edge_value)
    picked = picked.at[tiles * COLS + 1].set(edge_value)
    return picked.astype(jnp.int32)


def levels(rng, dims, split, low, largest):
    loudness = 1.0
    for position, blocks in split:
        heights = jax.random.uniform(jax.random.fold_in(jax.random.fold_in(rng, 6), position), (blocks,), jnp.float32, low / len(split), largest / len(split))
        loudness = loudness * jnp.repeat(jnp.exp(heights), dims[position] // blocks).reshape((-1,) + (1,) * (len(dims) - 1 - position))
    return loudness


def scatter_about(own_key, extent, spread, bound, shards=(), kind=jnp.bfloat16):
    drawn = spread * jax.random.normal(own_key, extent, jnp.float32)
    if shards:
        drawn = drawn * levels(own_key, extent, shards, -0.22, 0.18)
    return jnp.clip(drawn, -bound, bound).astype(kind)


def setup_inputs(seed: int = 0) -> dict:
    seeds = jax.random.split(jax.random.key(seed), 10)
    coarse = scatter_about(seeds[0], (CH_IN, CROWS, CCOLS), 1.0, 6.0, ((1, 8), (2, 16)))
    row_src = draw_row_src(jax.random.fold_in(seeds[9], 71), 0)
    row_frac = jnp.clip(1.0 * jax.random.uniform(seeds[2], (FROWS,), jnp.float32) ** levels(seeds[2], (FROWS,), ((0, 8),), -0.2, 0.2), 0.0, 1.0)
    col_src = draw_col_src(jax.random.fold_in(seeds[9], 71), 0)
    col_frac = jnp.clip(1.0 * jax.random.uniform(seeds[4], (FCOLS,), jnp.float32) ** levels(seeds[4], (FCOLS,), ((0, 16),), -0.2, 0.2), 0.0, 1.0)
    embed_weight = scatter_about(seeds[5], (CH_IN, HID), CH_IN ** -0.5, 0.75)
    conv1_weight = scatter_about(seeds[6], (3, 3, HID, HID), (9 * HID) ** -0.5, 0.1875)
    conv2_weight = scatter_about(seeds[7], (3, 3, HID, HID), (9 * HID) ** -0.5, 0.1875)
    cotangent = scatter_about(seeds[8], (FROWS, FCOLS, HID), 1.0, 6.0, ((0, 8), (1, 16)))
    return {"coarse": coarse, "row_src": row_src, "row_frac": row_frac, "col_src": col_src, "col_frac": col_frac, "embed_weight": embed_weight, "conv1_weight": conv1_weight, "conv2_weight": conv2_weight, "cotangent": cotangent}


def pad_grid(field):
    wrapped = jnp.concatenate([field[:, -1:], field, field[:, :1]], axis=1)
    return jnp.pad(wrapped, ((1, 1), (0, 0), (0, 0)))

def convolve(padded, weight, span_rows, span_cols):
    channels = weight.shape[2]
    total = jnp.zeros((span_rows * span_cols, weight.shape[3]), jnp.float32)
    for tap_row in range(3):
        for tap_col in range(3):
            window = padded[tap_row:tap_row + span_rows, tap_col:tap_col + span_cols].reshape(-1, channels)
            total = total + jnp.dot(window, weight[tap_row, tap_col], preferred_element_type=jnp.float32)
    return total.reshape(span_rows, span_cols, -1)

def convolve_back(padded, weight, span_rows, span_cols):
    channels = weight.shape[3]
    total = jnp.zeros((span_rows * span_cols, weight.shape[2]), jnp.float32)
    for tap_row in range(3):
        for tap_col in range(3):
            window = padded[2 - tap_row:2 - tap_row + span_rows, 2 - tap_col:2 - tap_col + span_cols].reshape(-1, channels)
            total = total + jnp.dot(window, weight[tap_row, tap_col].T, preferred_element_type=jnp.float32)
    return total.reshape(span_rows, span_cols, -1)

def weight_grads(padded, delta, span_rows, span_cols):
    channels = padded.shape[2]
    flat_delta = delta.reshape(-1, delta.shape[2])
    blocks = []
    for tap_row in range(3):
        line = []
        for tap_col in range(3):
            window = padded[tap_row:tap_row + span_rows, tap_col:tap_col + span_cols].reshape(-1, channels)
            line.append(lax.dot_general(window, flat_delta, (((0,), (0,)), ((), ())), preferred_element_type=jnp.float32))
        blocks.append(jnp.stack(line))
    return jnp.stack(blocks)

def reference(coarse, row_src, row_frac, col_src, col_frac, embed_weight, conv1_weight, conv2_weight, cotangent):
    span_rows = cotangent.shape[0]
    span_cols = cotangent.shape[1]
    coarse_f = coarse.astype(jnp.float32)
    row_mixed = (1.0 - row_frac)[None, :, None] * coarse_f[:, row_src, :] + row_frac[None, :, None] * coarse_f[:, row_src + 1, :]
    next_col = jnp.mod(col_src + 1, coarse.shape[2]).astype(jnp.int32)
    fine_input = ((1.0 - col_frac)[None, None, :] * row_mixed[:, :, col_src] + col_frac[None, None, :] * row_mixed[:, :, next_col]).astype(jnp.bfloat16)
    lifted = jnp.einsum('krc,kh->rch', fine_input.astype(jnp.float32), embed_weight.astype(jnp.float32)).astype(jnp.bfloat16)
    lifted_pad = pad_grid(lifted)
    pre_first = convolve(lifted_pad, conv1_weight, span_rows, span_cols)
    hidden = jax.nn.silu(pre_first).astype(jnp.bfloat16)
    hidden_pad = pad_grid(hidden)
    features = (lifted.astype(jnp.float32) + convolve(hidden_pad, conv2_weight, span_rows, span_cols)).astype(jnp.bfloat16)
    norm_scale = 1.0 / math.sqrt(span_rows * span_cols)
    grad_conv2 = weight_grads(hidden_pad, cotangent, span_rows, span_cols) * norm_scale
    cot_pad = pad_grid(cotangent)
    back_hidden = convolve_back(cot_pad, conv2_weight, span_rows, span_cols)
    sig = jax.nn.sigmoid(pre_first)
    delta = (back_hidden * sig * (1.0 + pre_first * (1.0 - sig))).astype(jnp.bfloat16)
    grad_conv1 = weight_grads(lifted_pad, delta, span_rows, span_cols) * norm_scale
    back_lifted = (cotangent.astype(jnp.float32) + convolve_back(pad_grid(delta), conv1_weight, span_rows, span_cols)).astype(jnp.bfloat16)
    grad_embed = jnp.einsum('krc,rch->kh', fine_input.astype(jnp.float32), back_lifted.astype(jnp.float32)) * norm_scale
    return (features, grad_embed, grad_conv1, grad_conv2)
```

```python
import functools
import math

import jax
import jax.numpy as jnp
from jax import lax
from jax.experimental import pallas as pl
from jax.experimental.pallas import tpu as pltpu
from jax.sharding import PartitionSpec as P

MESH = pl.DeviceIdType.MESH
BF = jnp.bfloat16
F32 = jnp.float32

ROWS = 32
COLS = 128
WIDE = 144
HID = 128
CROW = 4
CCOL = 8
CELLS = CROW * CCOL
PACK = 48
LO_J = 2
NUM_J = 9
PIECE = 5
TILES = 72
DIRS = [(dy, dx) for dy in (-1, 0, 1) for dx in (-1, 0, 1) if (dy, dx) != (0, 0)]


def dot(a, b):
    return jnp.dot(a, b, preferred_element_type=F32)


def dot_t(a, b):
    return lax.dot_general(a, b, (((0,), (0,)), ((), ())), preferred_element_type=F32)


def halves(x):
    hi = x.astype(BF)
    return hi, (x - hi.astype(F32)).astype(BF)


def spread_taps(w_ref, out_ref, back):
    zero = jnp.zeros((HID, HID), BF)
    for b in range(3):
        for a in range(3):
            block = w_ref[2 - a, 2 - b].T if back else w_ref[a, b]
            for s in range(2):
                k = a + s
                out_ref[pl.ds((k * 3 + b) * HID, HID), pl.ds(s * HID, HID)] = block
        out_ref[pl.ds(b * HID, HID), pl.ds(HID, HID)] = zero
        out_ref[pl.ds((9 + b) * HID, HID), pl.ds(0, HID)] = zero


def store_shifted(ref, pair, side, x):
    axis = x.ndim - 2
    ref[pair, side, :, pl.ds(HID, HID)] = x.astype(BF)
    ref[pair, side, :, pl.ds(0, HID)] = pltpu.roll(x, 1, axis).astype(BF)
    ref[pair, side, :, pl.ds(2 * HID, HID)] = pltpu.roll(x, WIDE - 1, axis).astype(BF)


def four_rows(ref, first, count, width):
    rows = [
        ref[pl.ds(first + k // 2, count), k % 2, pl.ds(0, width), :].reshape(count * width, 3 * HID)
        for k in range(4)
    ]
    return jnp.concatenate(rows, axis=-1)


def coarse_setup(lat, lon, nb_ref, cells_ref, rowmix_ref, colmix_ref):
    for block in range(9):
        dy, dx = block // 3, block % 3
        cells_ref[pl.ds(dy * CROW, CROW), pl.ds(dx * CCOL, CCOL), :] = (
            nb_ref[block, pl.ds(0, CELLS), :].astype(F32).reshape(CROW, CCOL, HID)
        )

    def line(block):
        return nb_ref[block, pl.ds(CELLS, 16), :].astype(F32)

    lane = lax.broadcasted_iota(jnp.int32, (16, HID), 1)
    rows = jnp.where(
        lane < 2,
        pltpu.roll(line(1), 98, 1),
        jnp.where(lane < 34, pltpu.roll(line(4), 2, 1), pltpu.roll(line(7), 34, 1)),
    )
    lane = lane[0:1]
    frac = rows[1:2] + rows[2:3] + rows[3:4]
    start = ((lane + 30) // 8 - 1).astype(F32)
    place = rows[0:1] - (lat * CROW - CROW).astype(F32) - start
    fine_row = lat * ROWS + lane - 2
    inside = ((fine_row >= 0) & (fine_row < 8 * ROWS)).astype(F32)
    for m in range(4):
        weight = jnp.where(place == float(m), 1.0 - frac, 0.0) + jnp.where(
            place == float(m - 1), frac, 0.0
        )
        rowmix_ref[pl.ds(m, 1), :] = weight * inside

    lane = lax.broadcasted_iota(jnp.int32, (16, HID), 1)
    edge = jnp.where(lane < 8, line(5), pltpu.roll(line(3), 16, 1))
    tables = []
    for part in (line(4), edge):
        frac = part[5:6] + part[6:7] + part[7:8]
        spot = part[4:5] - (lon * CCOL - CCOL).astype(F32)
        spot = jnp.where(spot < 0.0, spot + 128.0, spot)
        spot = jnp.where(spot >= 128.0, spot - 128.0, spot)
        cell = lax.broadcasted_iota(jnp.int32, (32, HID), 0).astype(F32)
        tables.append(
            jnp.where(cell == spot, 1.0 - frac, 0.0) + jnp.where(cell == spot + 1.0, frac, 0.0)
        )
    hi, lo = halves(jnp.concatenate(tables, axis=-1))
    colmix_ref[pl.ds(0, 32), :] = hi
    colmix_ref[pl.ds(32, 32), :] = lo


def lift(embed_ref, cells_ref, rowmix_ref, colmix_ref, mid_ref, l3_ref):
    window = cells_ref[...].reshape(12 * 24, HID).astype(BF)
    lifted = dot(window, embed_ref[...]).reshape(12, 24, HID)
    wide = jnp.concatenate([lifted[LO_J + j] for j in range(NUM_J)], axis=-1)
    wide = jnp.concatenate([wide, jnp.zeros((8, NUM_J * HID), F32)], axis=0)
    hi, lo = halves(wide)
    mixer = jnp.concatenate([colmix_ref[...], colmix_ref[pl.ds(0, 32), :]], axis=0)
    mid = dot_t(mixer, jnp.concatenate([hi, hi, lo], axis=0))
    mid_ref[...] = mid[0:WIDE]
    mix = rowmix_ref[...]
    for i in range(ROWS + 4):
        first = (i + 30) // 8 - 1 - LO_J
        total = None
        for m in range(4):
            weight = mix[m : m + 1, i : i + 1]
            term = weight * mid_ref[:, pl.ds((first + m) * HID, HID)]
            total = term if total is None else total + term
        store_shifted(l3_ref, i // 2, i % 2, total)


def spread_cot(lat, cot_ref, rowhalo_ref, colhalo_ref, c3_ref):
    near = lax.broadcasted_iota(jnp.int32, (16, HID), 0) < 8

    def put(i, own, scale):
        right = colhalo_ref[1, i].astype(F32)
        left = colhalo_ref[0, i].astype(F32)
        x = jnp.concatenate([own.astype(F32), jnp.where(near, right, left)], axis=0)
        if scale is not None:
            x = x * scale
        return x

    top = (lat > 0).astype(F32)
    bottom = (lat < 7).astype(F32)
    for t in range(2):
        store_shifted(c3_ref, 0, t, put(t, rowhalo_ref[0, t], top))
        store_shifted(c3_ref, 17, t, put(34 + t, rowhalo_ref[1, t], bottom))

    def step(q, carry):
        for t in range(2):
            r = 2 * q + t
            store_shifted(c3_ref, q + 1, t, put(r + 2, cot_ref[r], None))
        return carry

    lax.fori_loop(0, ROWS // 2, step, 0)


def middle(lat, first, count, l3_ref, c3_ref, w1_ref, w2t_ref, h3_ref, d3_ref):
    pre_all = dot(four_rows(l3_ref, first, count, WIDE), w1_ref[...])
    back_all = dot(four_rows(c3_ref, first, count, WIDE), w2t_ref[...])
    top = (lat > 0).astype(F32)
    bottom = (lat < 7).astype(F32)
    for p in range(count):
        for s in range(2):
            pre = pre_all[p * WIDE : (p + 1) * WIDE, s * HID : (s + 1) * HID]
            back = back_all[p * WIDE : (p + 1) * WIDE, s * HID : (s + 1) * HID]
            sig = 0.5 + 0.5 * jnp.tanh(0.5 * pre)
            hidden = pre * sig
            delta = back * (sig + hidden * (1.0 - sig))
            if first + p == 0 and s == 0:
                hidden, delta = hidden * top, delta * top
            if first + p == 16 and s == 1:
                hidden, delta = hidden * bottom, delta * bottom
            store_shifted(h3_ref, first + p, s, hidden)
            store_shifted(d3_ref, first + p, s, delta)


def rows_from(ref, start, lanes):
    q, odd = start // 2, start % 2
    if odd == 0:
        return ref[pl.ds(q, 16), :, pl.ds(0, COLS), lanes].reshape(ROWS * COLS, -1)
    parts = [ref[pl.ds(q, 16), 1, pl.ds(0, COLS), lanes], ref[pl.ds(q + 1, 16), 0, pl.ds(0, COLS), lanes]]
    return jnp.stack(parts, axis=1).reshape(ROWS * COLS, -1)


def weight_grad(v_ref, v_start, u_ref, u_start, out_ref):
    centre = pl.ds(HID, HID)
    left = jnp.concatenate([rows_from(v_ref, v_start + a, centre) for a in range(3)], axis=-1)
    right = rows_from(u_ref, u_start, pl.ds(0, 3 * HID))
    grad = dot_t(left, right)
    for a in range(3):
        for b in range(3):
            block = grad[a * HID : (a + 1) * HID, (2 - b) * HID : (3 - b) * HID]
            out_ref[pl.ds((a * 3 + b) * 8, 8)] = block.reshape(8, 16, HID).astype(BF)


def back_to_embed(first, count, d3_ref, w1t_ref, cot_ref, rowmix_ref, colmix_ref, down_ref):
    y = dot(four_rows(d3_ref, first, count, COLS), w1t_ref[...])
    rows = []
    for p in range(count):
        for s in range(2):
            part = y[p * COLS : (p + 1) * COLS, s * HID : (s + 1) * HID]
            rows.append((cot_ref[2 * (first + p) + s].astype(F32) + part).astype(BF))
    low = dot(colmix_ref[:, pl.ds(0, COLS)], jnp.concatenate(rows, axis=-1))
    low = low[0:32] + low[32:64]
    mix = rowmix_ref[...]
    sums = {}
    for n in range(2 * count):
        i = 2 * first + n + 2
        base = (i + 30) // 8 - 1
        part = low[:, n * HID : (n + 1) * HID]
        for m in range(4):
            term = mix[m : m + 1, i : i + 1] * part
            sums[base + m] = term if base + m not in sums else sums[base + m] + term
    for j, value in sums.items():
        down_ref[j] = down_ref[j] + value


def embed_grad(cells_ref, down_ref, out_ref):
    window = cells_ref[...].reshape(12 * 24, HID).astype(BF)
    down = jnp.concatenate([down_ref[j, pl.ds(0, 24), :] for j in range(12)], axis=0)
    hi, lo = halves(down)
    grad = dot_t(window, hi) + dot_t(window, lo)
    out_ref[...] = grad[0:80].reshape(PIECE, 16, HID).astype(BF)


def features_of(first, count, h3_ref, l3_ref, w2_ref, feat_ref):
    y = dot(four_rows(h3_ref, first, count, COLS), w2_ref[...])
    for p in range(count):
        for s in range(2):
            part = y[p * COLS : (p + 1) * COLS, s * HID : (s + 1) * HID]
            own = l3_ref[first + p + 1, s, pl.ds(0, COLS), pl.ds(HID, HID)].astype(F32)
            feat_ref[2 * (first + p) + s] = (own + part).astype(BF)


def ring(lat, lon, axis, step):
    if axis == "lat":
        return lax.rem(lat + step, 8), lon
    return lat, lax.rem(lon + step, 16)


class Exchange:
    def __init__(self, copies):
        self.copies = copies

    def start(self):
        for c in self.copies:
            c.start()

    def arrive(self):
        for c in self.copies:
            c.wait_recv()

    def sent(self):
        for c in self.copies:
            c.wait_send()


def remote(src, dst, send, recv, target):
    return pltpu.make_async_remote_copy(
        src_ref=src, dst_ref=dst, send_sem=send, recv_sem=recv, device_id=target, device_id_type=MESH
    )


class GradSum:
    def __init__(self, lat, lon, part, got, mine, other, final, sems):
        self.lat, self.lon = lat, lon
        self.part, self.got, self.mine, self.other, self.final = part, got, mine, other, final
        s_send, s_recv, l_send, l_recv, g_send, g_recv = sems
        spots = [ring(lat, lon, "lon", d) for d in range(1, 16)]
        own = pl.ds(lon * PIECE, PIECE)
        self.scatter = Exchange(
            [
                remote(part.at[pl.ds(t[1] * PIECE, PIECE)], got.at[n], s_send.at[n], s_recv.at[n], t)
                for n, t in enumerate(spots)
            ]
        )
        self.lats = Exchange(
            [
                remote(mine, other.at[d - 1], l_send.at[d - 1], l_recv.at[d - 1], ring(lat, lon, "lat", d))
                for d in range(1, 8)
            ]
        )
        self.gather = Exchange(
            [remote(final.at[own], final.at[own], g_send.at[n], g_recv.at[n], t) for n, t in enumerate(spots)]
        )

    def begin(self):
        self.scatter.start()

    def second(self):
        self.scatter.arrive()
        total = self.part[pl.ds(self.lon * PIECE, PIECE)].astype(F32)
        for n in range(15):
            total = total + self.got[n].astype(F32)
        self.mine[...] = total.astype(BF)
        self.lats.start()

    def third(self):
        self.lats.arrive()
        total = self.mine[...].astype(F32)
        for n in range(7):
            total = total + self.other[n].astype(F32)
        self.final[pl.ds(self.lon * PIECE, PIECE)] = total.astype(BF)
        self.gather.start()

    def finish(self, out_ref, scale):
        self.gather.arrive()
        for t in range(9):
            block = self.final[pl.ds(t * 8, 8)].astype(F32) * scale
            out_ref[t // 3, t % 3] = block.reshape(HID, HID)
        for e in (self.scatter, self.lats, self.gather):
            e.sent()


class SmallSum:
    def __init__(self, lat, lon, parts, slots, sems):
        self.parts, self.slots = parts, slots
        mate = lon + 1 - 2 * lax.rem(lon, 2)
        groups = [
            [ring(lat, lon, "lat", d) for d in range(1, 8)],
            [(lat, mate)],
            [ring(lat, lon, "lon", 2 * d) for d in range(1, 8)],
        ]
        self.steps = []
        base = 0
        for g, targets in enumerate(groups):
            copies = []
            for n, t in enumerate(targets):
                copies.append(remote(parts.at[g], slots.at[base + n], sems[0].at[base + n], sems[1].at[base + n], t))
            self.steps.append((base, len(targets), Exchange(copies)))
            base += len(targets)

    def begin(self, g):
        self.steps[g][2].start()

    def total(self, g):
        base, count, exchange = self.steps[g]
        exchange.arrive()
        total = self.parts[g].astype(F32)
        for n in range(count):
            total = total + self.slots[base + n].astype(F32)
        return total

    def pass_on(self, g):
        self.parts[g + 1] = self.total(g).astype(BF)
        self.begin(g + 1)

    def finish(self, out_ref, scale):
        out_ref[...] = (self.total(2) * scale).reshape(PIECE * 16, HID)
        for _, _, exchange in self.steps:
            exchange.sent()


def kernel(
    pack_ref, embed_ref, conv1_ref, conv2_ref, cot_ref,
    feat_ref, gemb_ref, g1_ref, g2_ref,
    nb_ref, rowhalo_ref, colhalo_ref, cells_ref, rowmix_ref, colmix_ref, mid_ref, down_ref,
    w1_ref, w2_ref, w1t_ref, w2t_ref, l3_ref, c3_ref, h3_ref, d3_ref,
    part1, got1, mine1, other1, final1, part2, got2, mine2, other2, final2, eparts, eslots,
    halo_send, halo_recv, cot_send, cot_recv, *sems,
):
    lat = lax.axis_index("lat")
    lon = lax.axis_index("lon")
    scale = 1.0 / math.sqrt(8 * ROWS * 16 * COLS)

    partners = [ring(lat, lon, "lat", d) for d in range(1, 8)]
    partners += [ring(lat, lon, "lon", d) for d in range(1, 16)]
    diagonal = {}
    for dy, dx in DIRS:
        spot = (lax.rem(lat + dy + 8, 8), lax.rem(lon + dx + 16, 16))
        diagonal[dy, dx] = spot
        if dy != 0 and dx != 0:
            partners.append(spot)
    barrier = pltpu.get_barrier_semaphore()
    for spot in partners:
        pl.semaphore_signal(barrier, inc=1, device_id=spot, device_id_type=MESH)
    pl.semaphore_wait(barrier, len(partners))

    packs, edges = [], []
    for n, (dy, dx) in enumerate(DIRS):
        slot = (1 - dy) * 3 + 1 - dx
        packs.append(remote(pack_ref, nb_ref.at[slot], halo_send.at[n], halo_recv.at[n], diagonal[dy, dx]))
        rows = {-1: pl.ds(0, 2), 0: pl.ds(0, ROWS), 1: pl.ds(ROWS - 2, 2)}[dy]
        if dx == 0:
            src = cot_ref.at[rows]
            dst = rowhalo_ref.at[0 if dy == 1 else 1]
        else:
            src = cot_ref.at[rows, pl.ds(0 if dx == -1 else COLS - 16, 16)]
            land = {1: pl.ds(0, 2), 0: pl.ds(2, ROWS), -1: pl.ds(ROWS + 2, 2)}[dy]
            dst = colhalo_ref.at[1 if dx == -1 else 0, land]
        edges.append(remote(src, dst, cot_send.at[n], cot_recv.at[n], diagonal[dy, dx]))
    packs, edges = Exchange(packs), Exchange(edges)
    packs.start()
    edges.start()

    sum1 = GradSum(lat, lon, part1, got1, mine1, other1, final1, sems[0:6])
    sum2 = GradSum(lat, lon, part2, got2, mine2, other2, final2, sems[6:12])
    small = SmallSum(lat, lon, eparts, eslots, sems[12:14])

    nb_ref[4] = pack_ref[...]
    spread_taps(conv1_ref, w1_ref, False)
    spread_taps(conv2_ref, w2_ref, False)
    spread_taps(conv1_ref, w1t_ref, True)
    spread_taps(conv2_ref, w2t_ref, True)
    down_ref[...] = jnp.zeros_like(down_ref)
    part1[pl.ds(TILES, 8)] = jnp.zeros((8, 16, HID), BF)
    part2[pl.ds(TILES, 8)] = jnp.zeros((8, 16, HID), BF)

    packs.arrive()
    coarse_setup(lat, lon, nb_ref, cells_ref, rowmix_ref, colmix_ref)
    lift(embed_ref, cells_ref, rowmix_ref, colmix_ref, mid_ref, l3_ref)
    edges.arrive()
    spread_cot(lat, cot_ref, rowhalo_ref, colhalo_ref, c3_ref)
    middle(lat, 0, 9, l3_ref, c3_ref, w1_ref, w2t_ref, h3_ref, d3_ref)
    middle(lat, 9, 8, l3_ref, c3_ref, w1_ref, w2t_ref, h3_ref, d3_ref)

    weight_grad(h3_ref, 0, c3_ref, 2, part2)
    sum2.begin()
    weight_grad(l3_ref, 1, d3_ref, 1, part1)
    sum1.begin()
    back_to_embed(0, 16, d3_ref, w1t_ref, cot_ref, rowmix_ref, colmix_ref, down_ref)
    embed_grad(cells_ref, down_ref, eparts.at[0])
    small.begin(0)
    sum2.second()
    features_of(0, 8, h3_ref, l3_ref, w2_ref, feat_ref)
    small.pass_on(0)
    sum1.second()
    features_of(8, 8, h3_ref, l3_ref, w2_ref, feat_ref)
    sum2.third()
    small.pass_on(1)
    sum1.third()
    sum2.finish(g2_ref, scale)
    small.finish(gemb_ref, scale)
    sum1.finish(g1_ref, scale)
    packs.sent()
    edges.sent()


def pack_block(coarse, row_src, row_frac, col_src, col_frac):
    def three(x):
        hi = x.astype(BF).astype(F32)
        mid = (x - hi).astype(BF).astype(F32)
        return [hi, mid, x - hi - mid]

    lines = [row_src.astype(F32)] + three(row_frac)
    lines = [jnp.pad(v, (0, HID - ROWS)) for v in lines]
    lines += [col_src.astype(F32)] + three(col_frac)
    lines = jnp.stack(lines + [jnp.zeros((HID,), F32)] * 8).astype(BF)
    cells = jnp.transpose(coarse, (1, 2, 0)).reshape(CELLS, -1)
    cells = jnp.pad(cells, ((0, 0), (0, HID - cells.shape[1])))
    return jnp.concatenate([cells, lines], axis=0)


def scratch_list():
    dma = pltpu.SemaphoreType.DMA
    wide = [pltpu.VMEM((12 * HID, 2 * HID), BF)] * 4
    grad = [
        pltpu.VMEM((80, 16, HID), BF),
        pltpu.VMEM((15, PIECE, 16, HID), BF),
        pltpu.VMEM((PIECE, 16, HID), BF),
        pltpu.VMEM((7, PIECE, 16, HID), BF),
        pltpu.VMEM((80, 16, HID), BF),
    ]
    return (
        [
            pltpu.VMEM((9, PACK, HID), BF),
            pltpu.VMEM((2, 2, COLS, HID), BF),
            pltpu.VMEM((2, ROWS + 4, 16, HID), BF),
            pltpu.VMEM((12, 24, HID), F32),
            pltpu.VMEM((8, HID), F32),
            pltpu.VMEM((64, 2 * HID), BF),
            pltpu.VMEM((WIDE, NUM_J * HID), F32),
            pltpu.VMEM((12, 32, HID), F32),
        ]
        + wide
        + [
            pltpu.VMEM((18, 2, WIDE, 3 * HID), BF),
            pltpu.VMEM((18, 2, WIDE, 3 * HID), BF),
            pltpu.VMEM((17, 2, WIDE, 3 * HID), BF),
            pltpu.VMEM((17, 2, WIDE, 3 * HID), BF),
        ]
        + grad
        + grad
        + [pltpu.VMEM((3, PIECE, 16, HID), BF), pltpu.VMEM((15, PIECE, 16, HID), BF)]
        + [dma((8,))] * 4
        + [dma((15,)), dma((15,)), dma((7,)), dma((7,)), dma((15,)), dma((15,))] * 2
        + [dma((15,))] * 2
    )


def on_device(coarse, row_src, row_frac, col_src, col_frac, embed_weight, conv1_weight, conv2_weight, cotangent):
    pack = pack_block(coarse, row_src, row_frac, col_src, col_frac)
    embed = jnp.pad(embed_weight, ((0, HID - embed_weight.shape[0]), (0, 0)))
    vmem = pl.BlockSpec(memory_space=pltpu.VMEM)
    conv = jax.ShapeDtypeStruct((3, 3, HID, HID), F32)
    features, grad_embed, grad_conv1, grad_conv2 = pl.pallas_call(
        kernel,
        out_shape=[
            jax.ShapeDtypeStruct((ROWS, COLS, HID), BF),
            jax.ShapeDtypeStruct((PIECE * 16, HID), F32),
            conv,
            conv,
        ],
        in_specs=[vmem] * 5,
        out_specs=[vmem] * 4,
        scratch_shapes=scratch_list(),
        compiler_params=pltpu.CompilerParams(
            collective_id=0, has_side_effects=True, vmem_limit_bytes=56 * 2**20
        ),
    )(pack, embed, conv1_weight, conv2_weight, cotangent)
    return (features, grad_embed[: coarse.shape[0]], grad_conv1, grad_conv2)


def solution(mesh):
    in_specs = (
        P(None, "lat", "lon"),
        P("lat"),
        P("lat"),
        P("lon"),
        P("lon"),
        P(),
        P(),
        P(),
        P("lat", "lon", None),
    )
    out_specs = (P("lat", "lon", None), P(), P(), P())
    return jax.shard_map(
        on_device, mesh=mesh, in_specs=in_specs, out_specs=out_specs, check_vma=False
    )
```

```python
import functools
import math

import jax
import jax.numpy as jnp
from jax import lax
from jax.experimental import pallas as pl
from jax.experimental.pallas import tpu as pltpu
from jax.sharding import PartitionSpec as P

MESH = pl.DeviceIdType.MESH
BF = jnp.bfloat16
F32 = jnp.float32

ROWS = 32
COLS = 128
WIDE = 144
HID = 128
CROW = 4
CCOL = 8
CELLS = CROW * CCOL
PACK = 48
LO_J = 2
NUM_J = 9
TILES = 72
HALF = 36
PIECE = 3
EMBED_TILES = 5
DIRS = [(dy, dx) for dy in (-1, 0, 1) for dx in (-1, 0, 1) if (dy, dx) != (0, 0)]


def dot(a, b):
    return jnp.dot(a, b, preferred_element_type=F32)


def dot_t(a, b):
    return lax.dot_general(a, b, (((0,), (0,)), ((), ())), preferred_element_type=F32)


def halves(x):
    hi = x.astype(BF)
    return hi, (x - hi.astype(F32)).astype(BF)


def spread_taps(w_ref, out_ref, back):
    zero = jnp.zeros((HID, HID), BF)
    for b in range(3):
        for a in range(3):
            block = w_ref[2 - a, 2 - b].T if back else w_ref[a, b]
            for s in range(2):
                k = a + s
                out_ref[pl.ds((k * 3 + b) * HID, HID), pl.ds(s * HID, HID)] = block
        out_ref[pl.ds(b * HID, HID), pl.ds(HID, HID)] = zero
        out_ref[pl.ds((9 + b) * HID, HID), pl.ds(0, HID)] = zero


def store_shifted(ref, pair, side, x):
    axis = x.ndim - 2
    ref[pair, side, :, pl.ds(HID, HID)] = x.astype(BF)
    ref[pair, side, :, pl.ds(0, HID)] = pltpu.roll(x, 1, axis).astype(BF)
    ref[pair, side, :, pl.ds(2 * HID, HID)] = pltpu.roll(x, WIDE - 1, axis).astype(BF)


def four_rows(ref, first, count, width, start=0):
    rows = [
        ref[pl.ds(first + k // 2, count), k % 2, pl.ds(start, width), :].reshape(count * width, 3 * HID)
        for k in range(4)
    ]
    return jnp.concatenate(rows, axis=-1)


def coarse_setup(lat, lon, nb_ref, cells_ref, rowmix_ref, colmix_ref):
    for block in range(9):
        dy, dx = block // 3, block % 3
        cells_ref[pl.ds(dy * CROW, CROW), pl.ds(dx * CCOL, CCOL), :] = (
            nb_ref[block, pl.ds(0, CELLS), :].astype(F32).reshape(CROW, CCOL, HID)
        )

    def line(block):
        return nb_ref[block, pl.ds(CELLS, 16), :].astype(F32)

    lane = lax.broadcasted_iota(jnp.int32, (16, HID), 1)
    rows = jnp.where(
        lane < 2,
        pltpu.roll(line(1), 98, 1),
        jnp.where(lane < 34, pltpu.roll(line(4), 2, 1), pltpu.roll(line(7), 34, 1)),
    )
    lane = lane[0:1]
    frac = rows[1:2] + rows[2:3] + rows[3:4]
    start = ((lane + 30) // 8 - 1).astype(F32)
    place = rows[0:1] - (lat * CROW - CROW).astype(F32) - start
    fine_row = lat * ROWS + lane - 2
    inside = ((fine_row >= 0) & (fine_row < 8 * ROWS)).astype(F32)
    for m in range(4):
        weight = jnp.where(place == float(m), 1.0 - frac, 0.0) + jnp.where(
            place == float(m - 1), frac, 0.0
        )
        rowmix_ref[pl.ds(m, 1), :] = weight * inside

    lane = lax.broadcasted_iota(jnp.int32, (16, HID), 1)
    edge = jnp.where(lane < 8, line(5), pltpu.roll(line(3), 16, 1))
    tables = []
    for part in (line(4), edge):
        frac = part[5:6] + part[6:7] + part[7:8]
        spot = part[4:5] - (lon * CCOL - CCOL).astype(F32)
        spot = jnp.where(spot < 0.0, spot + 128.0, spot)
        spot = jnp.where(spot >= 128.0, spot - 128.0, spot)
        cell = lax.broadcasted_iota(jnp.int32, (32, HID), 0).astype(F32)
        tables.append(
            jnp.where(cell == spot, 1.0 - frac, 0.0) + jnp.where(cell == spot + 1.0, frac, 0.0)
        )
    hi, lo = halves(jnp.concatenate(tables, axis=-1))
    colmix_ref[pl.ds(0, 32), :] = hi
    colmix_ref[pl.ds(32, 32), :] = lo


def lift(embed_ref, cells_ref, rowmix_ref, colmix_ref, mid_ref, l3_ref):
    cells = [cells_ref[LO_J + j] for j in range(NUM_J)]
    wide = jnp.concatenate(cells, axis=-1)
    wide = jnp.concatenate([wide, jnp.zeros((8, NUM_J * HID), F32)], axis=0).astype(BF)
    mid = dot_t(colmix_ref[...], jnp.concatenate([wide, wide], axis=0))
    mid_ref[...] = mid[0:WIDE]
    mix = rowmix_ref[...]
    for start in range(0, ROWS + 4, 12):
        rows = []
        for i in range(start, start + 12):
            first = (i + 30) // 8 - 1 - LO_J
            total = None
            for m in range(4):
                weight = mix[m : m + 1, i : i + 1]
                term = weight * mid_ref[:, pl.ds((first + m) * HID, HID)]
                total = term if total is None else total + term
            rows.append(total.astype(BF))
        lifted = dot(jnp.concatenate(rows, axis=0), embed_ref[...])
        for n in range(12):
            i = start + n
            store_shifted(l3_ref, i // 2, i % 2, lifted[n * WIDE : (n + 1) * WIDE])


def spread_own(cot_ref, c3_ref):
    def step(q, carry):
        for t in range(2):
            x = cot_ref[2 * q + t].astype(F32)
            own = pl.ds(0, COLS)
            c3_ref[q + 1, t, own, pl.ds(HID, HID)] = cot_ref[2 * q + t]
            c3_ref[q + 1, t, own, pl.ds(0, HID)] = pltpu.roll(x, 1, 0).astype(BF)
            c3_ref[q + 1, t, own, pl.ds(2 * HID, HID)] = pltpu.roll(x, COLS - 1, 0).astype(BF)
        return carry

    lax.fori_loop(0, ROWS // 2, step, 0)


def close_edges(lat, cot_ref, rowhalo_ref, colhalo_ref, c3_ref):
    near = lax.broadcasted_iota(jnp.int32, (16, HID), 0) < 8

    def beside(i):
        return jnp.where(near, colhalo_ref[1, i].astype(F32), colhalo_ref[0, i].astype(F32))

    top = (lat > 0).astype(F32)
    bottom = (lat < 7).astype(F32)
    for t in range(2):
        x = jnp.concatenate([rowhalo_ref[0, t].astype(F32), beside(t)], axis=0)
        store_shifted(c3_ref, 0, t, x * top)
        x = jnp.concatenate([rowhalo_ref[1, t].astype(F32), beside(ROWS + 2 + t)], axis=0)
        store_shifted(c3_ref, 17, t, x * bottom)

    def step(q, carry):
        for t in range(2):
            r = 2 * q + t
            last = cot_ref[r, pl.ds(COLS - 16, 16)].astype(F32)
            first = cot_ref[r, pl.ds(0, 16)].astype(F32)
            x = jnp.concatenate([last, beside(r + 2), first], axis=0)
            west = pltpu.roll(x, 1, 0).astype(BF)
            east = pltpu.roll(x, 47, 0).astype(BF)
            wide = pl.ds(COLS, 16)
            c3_ref[q + 1, t, wide, pl.ds(HID, HID)] = x[16:32].astype(BF)
            c3_ref[q + 1, t, wide, pl.ds(0, HID)] = west[16:32]
            c3_ref[q + 1, t, pl.ds(0, 16), pl.ds(0, HID)] = west[32:48]
            c3_ref[q + 1, t, pl.ds(COLS - 16, 32), pl.ds(2 * HID, HID)] = east[0:32]
        return carry

    lax.fori_loop(0, ROWS // 2, step, 0)


def back_inside(c3_ref, w2t_ref, back_ref):
    y = dot(four_rows(c3_ref, 1, 15, 96, 16), w2t_ref[...])
    back_ref[pl.ds(1, 15), pl.ds(16, 96), :] = y.reshape(15, 96, 2 * HID)


def back_around(c3_ref, w2t_ref, back_ref):
    parts = [
        four_rows(c3_ref, 1, 15, 16, 0),
        four_rows(c3_ref, 1, 15, 32, COLS - 16),
        four_rows(c3_ref, 0, 1, WIDE),
        four_rows(c3_ref, 16, 1, WIDE),
    ]
    y = dot(jnp.concatenate(parts, axis=0), w2t_ref[...])
    back_ref[pl.ds(1, 15), pl.ds(0, 16), :] = y[0:240].reshape(15, 16, 2 * HID)
    back_ref[pl.ds(1, 15), pl.ds(COLS - 16, 32), :] = y[240:720].reshape(15, 32, 2 * HID)
    back_ref[0] = y[720 : 720 + WIDE]
    back_ref[16] = y[720 + WIDE : 720 + 2 * WIDE]


def middle(lat, first, count, l3_ref, back_ref, w1_ref, h3_ref, d3_ref):
    pre_all = dot(four_rows(l3_ref, first, count, WIDE), w1_ref[...])
    top = (lat > 0).astype(F32)
    bottom = (lat < 7).astype(F32)
    for p in range(count):
        for s in range(2):
            pre = pre_all[p * WIDE : (p + 1) * WIDE, s * HID : (s + 1) * HID]
            back = back_ref[first + p, :, pl.ds(s * HID, HID)]
            sig = 0.5 + 0.5 * jnp.tanh(0.5 * pre)
            hidden = pre * sig
            delta = back * (sig + hidden * (1.0 - sig))
            if first + p == 0 and s == 0:
                hidden, delta = hidden * top, delta * top
            if first + p == 16 and s == 1:
                hidden, delta = hidden * bottom, delta * bottom
            store_shifted(h3_ref, first + p, s, hidden)
            store_shifted(d3_ref, first + p, s, delta)


def rows_from(ref, start, lanes):
    q, odd = start // 2, start % 2
    if odd == 0:
        return ref[pl.ds(q, 16), :, pl.ds(0, COLS), lanes].reshape(ROWS * COLS, -1)
    parts = [ref[pl.ds(q, 16), 1, pl.ds(0, COLS), lanes], ref[pl.ds(q + 1, 16), 0, pl.ds(0, COLS), lanes]]
    return jnp.stack(parts, axis=1).reshape(ROWS * COLS, -1)


def weight_grad(v_ref, v_start, u_ref, u_start, out_ref):
    centre = pl.ds(HID, HID)
    left = jnp.concatenate([rows_from(v_ref, v_start + a, centre) for a in range(3)], axis=-1)
    right = rows_from(u_ref, u_start, pl.ds(0, 3 * HID))
    grad = dot_t(left, right)
    for a in range(3):
        for b in range(3):
            block = grad[a * HID : (a + 1) * HID, (2 - b) * HID : (3 - b) * HID]
            out_ref[pl.ds((a * 3 + b) * 8, 8)] = block.reshape(8, 16, HID).astype(BF)


def back_to_embed(first, count, d3_ref, w1t_ref, cot_ref, rowmix_ref, colmix_ref, down_ref):
    y = dot(four_rows(d3_ref, first, count, COLS), w1t_ref[...])
    rows = []
    for p in range(count):
        for s in range(2):
            part = y[p * COLS : (p + 1) * COLS, s * HID : (s + 1) * HID]
            rows.append((cot_ref[2 * (first + p) + s].astype(F32) + part).astype(BF))
    low = dot(colmix_ref[:, pl.ds(0, COLS)], jnp.concatenate(rows, axis=-1))
    low = low[0:32] + low[32:64]
    mix = rowmix_ref[...]
    sums = {}
    for n in range(2 * count):
        i = 2 * first + n + 2
        base = (i + 30) // 8 - 1
        part = low[:, n * HID : (n + 1) * HID]
        for m in range(4):
            term = mix[m : m + 1, i : i + 1] * part
            sums[base + m] = term if base + m not in sums else sums[base + m] + term
    for j, value in sums.items():
        down_ref[j] = down_ref[j] + value


def embed_grad(cells_ref, down_ref, out_ref):
    window = cells_ref[...].reshape(12 * 24, HID).astype(BF)
    down = jnp.concatenate([down_ref[j, pl.ds(0, 24), :] for j in range(12)], axis=0)
    hi, lo = halves(down)
    grad = dot_t(window, hi) + dot_t(window, lo)
    out_ref[...] = grad[0 : EMBED_TILES * 16].reshape(EMBED_TILES, 16, HID).astype(BF)


def features_of(first, count, h3_ref, l3_ref, w2_ref, feat_ref):
    y = dot(four_rows(h3_ref, first, count, COLS), w2_ref[...])
    for p in range(count):
        for s in range(2):
            part = y[p * COLS : (p + 1) * COLS, s * HID : (s + 1) * HID]
            own = l3_ref[first + p + 1, s, pl.ds(0, COLS), pl.ds(HID, HID)].astype(F32)
            feat_ref[2 * (first + p) + s] = (own + part).astype(BF)


class Place:
    def __init__(self):
        self.lat = lax.axis_index("lat")
        self.lon = lax.axis_index("lon")
        self.core = lax.rem(self.lon, 2)
        self.z = lax.rem(self.lat, 2) * 2 + lax.rem(self.lon // 2, 2)
        self.plane = self.lon // 4 * 4 + self.lat // 2
        self.mate = (self.lat, self.lon + 1 - 2 * self.core)
        self.planes = [lax.rem(self.plane + d, 16) for d in range(1, 16)]
        self.plane_mates = [self.spot(q, self.z) for q in self.planes]
        self.z_mates = [self.spot(self.plane, lax.rem(self.z + d, 4)) for d in range(1, 4)]
        self.around = [(lax.rem(self.lat + dy + 8, 8), lax.rem(self.lon + dx + 16, 16)) for dy, dx in DIRS]

    def spot(self, plane, z):
        return (lax.rem(plane, 4) * 2 + z // 2, plane // 4 * 4 + lax.rem(z, 2) * 2 + self.core)


class Exchange:
    def __init__(self, copies):
        self.copies = copies

    def start(self):
        for c in self.copies:
            c.start()

    def arrive(self):
        for c in self.copies:
            c.wait_recv()

    def sent(self):
        for c in self.copies:
            c.wait_send()


def remote(src, dst, send, recv, target):
    return pltpu.make_async_remote_copy(
        src_ref=src, dst_ref=dst, send_sem=send, recv_sem=recv, device_id=target, device_id_type=MESH
    )


class GradSum:
    def __init__(self, place, part, paired, half, got, mine, other, final, twin, sems):
        self.part, self.paired, self.half, self.got = part, paired, half, got
        self.mine, self.other, self.final, self.twin = mine, other, final, twin
        a_sem, s_send, s_recv, z_send, z_recv, g_send, g_recv = sems
        self.keep = place.core * HALF
        self.own = pl.ds(place.plane * PIECE, PIECE)
        away = part.at[pl.ds(HALF - self.keep, HALF)]
        self.pair = Exchange([remote(away, paired, a_sem.at[0], a_sem.at[1], place.mate)])
        self.scatter = Exchange(
            [
                remote(half.at[pl.ds(q * PIECE, PIECE)], got.at[n], s_send.at[n], s_recv.at[n], t)
                for n, (q, t) in enumerate(zip(place.planes, place.plane_mates))
            ]
        )
        self.column = Exchange(
            [remote(mine, other.at[n], z_send.at[n], z_recv.at[n], t) for n, t in enumerate(place.z_mates)]
        )
        self.gather = Exchange(
            [
                remote(final.at[self.own], final.at[self.own], g_send.at[n], g_recv.at[n], t)
                for n, t in enumerate(place.plane_mates)
            ]
        )
        self.swap = Exchange([remote(final.at[pl.ds(0, HALF)], twin, a_sem.at[2], a_sem.at[3], place.mate)])

    def step_pair(self):
        self.pair.start()

    def step_scatter(self):
        self.pair.arrive()
        total = self.part[pl.ds(self.keep, HALF)].astype(F32) + self.paired[...].astype(F32)
        self.half[pl.ds(0, HALF)] = total.astype(BF)
        self.half[pl.ds(HALF, 16 * PIECE - HALF)] = jnp.zeros((16 * PIECE - HALF, 16, HID), BF)
        self.scatter.start()

    def step_column(self):
        self.scatter.arrive()
        total = self.half[self.own].astype(F32)
        for n in range(15):
            total = total + self.got[n].astype(F32)
        self.mine[...] = total.astype(BF)
        self.column.start()

    def step_gather(self):
        self.column.arrive()
        total = self.mine[...].astype(F32)
        for n in range(3):
            total = total + self.other[n].astype(F32)
        self.final[self.own] = total.astype(BF)
        self.gather.start()

    def step_swap(self, out_ref, scale):
        self.gather.arrive()
        self.swap.start()
        out_ref[pl.ds(self.keep, HALF)] = self.final[pl.ds(0, HALF)].astype(F32) * scale

    def finish(self, out_ref, scale):
        self.swap.arrive()
        out_ref[pl.ds(HALF - self.keep, HALF)] = self.twin[...].astype(F32) * scale
        for e in (self.pair, self.scatter, self.column, self.gather, self.swap):
            e.sent()


class SmallSum:
    def __init__(self, place, parts, slots, sems):
        self.parts, self.slots = parts, slots
        self.steps = []
        base = 0
        for g, targets in enumerate([[place.mate], place.z_mates, place.plane_mates]):
            copies = []
            for n, t in enumerate(targets):
                copies.append(remote(parts.at[g], slots.at[base + n], sems[0].at[base + n], sems[1].at[base + n], t))
            self.steps.append((base, len(targets), Exchange(copies)))
            base += len(targets)

    def begin(self, g):
        self.steps[g][2].start()

    def total(self, g):
        base, count, exchange = self.steps[g]
        exchange.arrive()
        total = self.parts[g].astype(F32)
        for n in range(count):
            total = total + self.slots[base + n].astype(F32)
        return total

    def pass_on(self, g):
        self.parts[g + 1] = self.total(g).astype(BF)
        self.begin(g + 1)

    def finish(self, out_ref, scale):
        out_ref[...] = (self.total(2) * scale).reshape(EMBED_TILES * 16, HID)
        for _, _, exchange in self.steps:
            exchange.sent()


def pack_block(coarse_ref, row_src_ref, row_frac_ref, col_src_ref, col_frac_ref, lines_ref, pack_ref):
    pack_ref[...] = jnp.zeros_like(pack_ref)
    pack_ref[pl.ds(0, CELLS), pl.ds(0, coarse_ref.shape[1])] = coarse_ref[...]
    lines_ref[...] = jnp.zeros_like(lines_ref)
    for row, src_ref, frac_ref in ((0, row_src_ref, row_frac_ref), (4, col_src_ref, col_frac_ref)):
        lanes = pl.ds(0, src_ref.shape[1])
        lines_ref[pl.ds(row, 1), lanes] = src_ref[...].astype(F32)
        left = frac_ref[...]
        for n in range(1, 4):
            term = left.astype(BF).astype(F32)
            lines_ref[pl.ds(row + n, 1), lanes] = term
            left = left - term
    pack_ref[pl.ds(CELLS, 16), :] = lines_ref[...].astype(BF)


def kernel(
    coarse_hbm, row_src_hbm, row_frac_hbm, col_src_hbm, col_frac_hbm, embed_hbm, conv1_hbm, conv2_hbm, cot_hbm,
    feat_ref, gemb_ref, g1_ref, g2_ref,
    coarse_ref, row_src_ref, row_frac_ref, col_src_ref, col_frac_ref, embed_in_ref, conv1_ref, conv2_ref, cot_ref,
    lines_ref, pack_ref, embed_ref,
    nb_ref, rowhalo_ref, colhalo_ref, cells_ref, rowmix_ref, colmix_ref, mid_ref, down_ref,
    w1_ref, w2_ref, w1t_ref, w2t_ref, l3_ref, c3_ref, h3_ref, d3_ref, back_ref,
    part1, paired1, half1, got1, mine1, other1, final1, twin1,
    part2, paired2, half2, got2, mine2, other2, final2, twin2, eparts, eslots,
    load_sem, halo_send, halo_recv, cot_send, cot_recv, *sems,
):
    place = Place()
    lat, lon = place.lat, place.lon
    scale = 1.0 / math.sqrt(8 * ROWS * 16 * COLS)

    barrier = pltpu.get_barrier_semaphore()
    partners = [place.mate] + place.around + place.z_mates + place.plane_mates
    for spot in partners:
        pl.semaphore_signal(barrier, inc=1, device_id=spot, device_id_type=MESH)

    pairs = [
        (coarse_hbm, coarse_ref), (row_src_hbm, row_src_ref), (row_frac_hbm, row_frac_ref),
        (col_src_hbm, col_src_ref), (col_frac_hbm, col_frac_ref), (cot_hbm, cot_ref),
        (conv2_hbm, conv2_ref), (conv1_hbm, conv1_ref), (embed_hbm, embed_in_ref),
    ]
    loads = [pltpu.make_async_copy(src, dst, load_sem.at[n]) for n, (src, dst) in enumerate(pairs)]
    for load in loads:
        load.start()

    packs, edges = [], []
    for n, (dy, dx) in enumerate(DIRS):
        slot = (1 - dy) * 3 + 1 - dx
        packs.append(remote(pack_ref, nb_ref.at[slot], halo_send.at[n], halo_recv.at[n], place.around[n]))
        rows = {-1: pl.ds(0, 2), 0: pl.ds(0, ROWS), 1: pl.ds(ROWS - 2, 2)}[dy]
        if dx == 0:
            src = cot_ref.at[rows]
            dst = rowhalo_ref.at[0 if dy == 1 else 1]
        else:
            src = cot_ref.at[rows, pl.ds(0 if dx == -1 else COLS - 16, 16)]
            land = {1: pl.ds(0, 2), 0: pl.ds(2, ROWS), -1: pl.ds(ROWS + 2, 2)}[dy]
            dst = colhalo_ref.at[1 if dx == -1 else 0, land]
        edges.append(remote(src, dst, cot_send.at[n], cot_recv.at[n], place.around[n]))
    packs, edges = Exchange(packs), Exchange(edges)
    sum1 = GradSum(place, part1, paired1, half1, got1, mine1, other1, final1, twin1, sems[0:7])
    sum2 = GradSum(place, part2, paired2, half2, got2, mine2, other2, final2, twin2, sems[7:14])
    small = SmallSum(place, eparts, eslots, sems[14:16])

    for load in loads[0:5]:
        load.wait()
    pack_block(coarse_ref, row_src_ref, row_frac_ref, col_src_ref, col_frac_ref, lines_ref, pack_ref)
    loads[5].wait()
    pl.semaphore_wait(barrier, len(partners))
    packs.start()
    edges.start()

    nb_ref[4] = pack_ref[...]
    for load in loads[6:9]:
        load.wait()
    spread_taps(conv2_ref, w2t_ref, True)
    spread_own(cot_ref, c3_ref)
    back_inside(c3_ref, w2t_ref, back_ref)
    spread_taps(conv1_ref, w1_ref, False)
    spread_taps(conv2_ref, w2_ref, False)
    spread_taps(conv1_ref, w1t_ref, True)
    embed_ref[...] = jnp.zeros_like(embed_ref)
    embed_ref[pl.ds(0, embed_in_ref.shape[0]), :] = embed_in_ref[...]
    down_ref[...] = jnp.zeros_like(down_ref)

    packs.arrive()
    coarse_setup(lat, lon, nb_ref, cells_ref, rowmix_ref, colmix_ref)
    lift(embed_ref, cells_ref, rowmix_ref, colmix_ref, mid_ref, l3_ref)
    edges.arrive()
    close_edges(lat, cot_ref, rowhalo_ref, colhalo_ref, c3_ref)
    back_around(c3_ref, w2t_ref, back_ref)
    middle(lat, 0, 9, l3_ref, back_ref, w1_ref, h3_ref, d3_ref)
    middle(lat, 9, 8, l3_ref, back_ref, w1_ref, h3_ref, d3_ref)

    weight_grad(h3_ref, 0, c3_ref, 2, part2)
    sum2.step_pair()
    weight_grad(l3_ref, 1, d3_ref, 1, part1)
    sum1.step_pair()
    sum2.step_scatter()
    back_to_embed(0, 8, d3_ref, w1t_ref, cot_ref, rowmix_ref, colmix_ref, down_ref)
    sum1.step_scatter()
    back_to_embed(8, 8, d3_ref, w1t_ref, cot_ref, rowmix_ref, colmix_ref, down_ref)
    embed_grad(cells_ref, down_ref, eparts.at[0])
    small.begin(0)
    features_of(0, 8, h3_ref, l3_ref, w2_ref, feat_ref)
    small.pass_on(0)
    sum2.step_column()
    features_of(8, 8, h3_ref, l3_ref, w2_ref, feat_ref)
    sum1.step_column()
    small.pass_on(1)
    sum2.step_gather()
    sum1.step_gather()
    small.finish(gemb_ref, scale)
    sum2.step_swap(g2_ref, scale)
    sum1.step_swap(g1_ref, scale)
    sum2.finish(g2_ref, scale)
    sum1.finish(g1_ref, scale)
    packs.sent()
    edges.sent()


def scratch_list(channels=73):
    dma = pltpu.SemaphoreType.DMA
    line = lambda n, kind: pltpu.VMEM((1, n), kind)
    tiles = lambda *n: pltpu.VMEM((*n, 16, HID), BF)
    grad = [
        tiles(TILES), tiles(HALF), tiles(16 * PIECE), tiles(15, PIECE),
        tiles(PIECE), tiles(3, PIECE), tiles(16 * PIECE), tiles(HALF),
    ]
    return (
        [
            pltpu.VMEM((CELLS, channels), BF),
            line(ROWS, jnp.int32), line(ROWS, F32), line(COLS, jnp.int32), line(COLS, F32),
            pltpu.VMEM((channels, HID), BF),
            pltpu.VMEM((3, 3, HID, HID), BF),
            pltpu.VMEM((3, 3, HID, HID), BF),
            pltpu.VMEM((ROWS, COLS, HID), BF),
            pltpu.VMEM((16, HID), F32),
            pltpu.VMEM((PACK, HID), BF),
            pltpu.VMEM((HID, HID), BF),
            pltpu.VMEM((9, PACK, HID), BF),
            pltpu.VMEM((2, 2, COLS, HID), BF),
            pltpu.VMEM((2, ROWS + 4, 16, HID), BF),
            pltpu.VMEM((12, 24, HID), F32),
            pltpu.VMEM((8, HID), F32),
            pltpu.VMEM((64, 2 * HID), BF),
            pltpu.VMEM((WIDE, NUM_J * HID), F32),
            pltpu.VMEM((12, 32, HID), F32),
        ]
        + [pltpu.VMEM((12 * HID, 2 * HID), BF)] * 4
        + [pltpu.VMEM((18, 2, WIDE, 3 * HID), BF)] * 2
        + [pltpu.VMEM((17, 2, WIDE, 3 * HID), BF)] * 2
        + [pltpu.VMEM((17, WIDE, 2 * HID), F32)]
        + grad
        + grad
        + [tiles(3, EMBED_TILES), tiles(19, EMBED_TILES)]
        + [dma((9,))]
        + [dma((8,))] * 4
        + [dma((4,)), dma((15,)), dma((15,)), dma((3,)), dma((3,)), dma((15,)), dma((15,))] * 2
        + [dma((19,))] * 2
    )


def on_device(coarse, row_src, row_frac, col_src, col_frac, embed_weight, conv1_weight, conv2_weight, cotangent):
    channels = coarse.shape[0]
    cells = jnp.transpose(coarse, (1, 2, 0)).reshape(CELLS, channels)
    lines = [v.reshape(1, -1) for v in (row_src, row_frac, col_src, col_frac)]
    features, grad_embed, grad_conv1, grad_conv2 = pl.pallas_call(
        kernel,
        out_shape=[
            pltpu.VMEM((ROWS, COLS, HID), BF),
            pltpu.VMEM((EMBED_TILES * 16, HID), F32),
            pltpu.VMEM((TILES, 16, HID), F32),
            pltpu.VMEM((TILES, 16, HID), F32),
        ],
        in_specs=[pl.BlockSpec(memory_space=pl.ANY)] * 9,
        out_specs=[pl.BlockSpec(memory_space=pltpu.VMEM)] * 4,
        scratch_shapes=scratch_list(channels),
        compiler_params=pltpu.CompilerParams(
            collective_id=0, has_side_effects=True, vmem_limit_bytes=56 * 2**20
        ),
    )(cells, *lines, embed_weight, conv1_weight, conv2_weight, cotangent)
    taps = (3, 3, HID, HID)
    return (features, grad_embed[:channels], grad_conv1.reshape(taps), grad_conv2.reshape(taps))


def solution(mesh):
    in_specs = (
        P(None, "lat", "lon"),
        P("lat"),
        P("lat"),
        P("lon"),
        P("lon"),
        P(),
        P(),
        P(),
        P("lat", "lon", None),
    )
    out_specs = (P("lat", "lon", None), P(), P(), P())
    return jax.shard_map(
        on_device, mesh=mesh, in_specs=in_specs, out_specs=out_specs, check_vma=False
    )
```

```python
import functools
import math

import jax
import jax.numpy as jnp
from jax import lax
from jax.experimental import pallas as pl
from jax.experimental.pallas import tpu as pltpu
from jax.sharding import PartitionSpec as P

MESH = pl.DeviceIdType.MESH
BF = jnp.bfloat16
F32 = jnp.float32

ROWS = 32
COLS = 128
WIDE = 144
HID = 128
CROW = 4
CCOL = 8
CELLS = CROW * CCOL
PACK = 48
LO_J = 2
NUM_J = 9
TILES = 72
HALF = 36
PIECE = 3
EMBED_TILES = 5
DIRS = [(dy, dx) for dy in (-1, 0, 1) for dx in (-1, 0, 1) if (dy, dx) != (0, 0)]


def dot(a, b):
    return jnp.dot(a, b, preferred_element_type=F32)


def dot_t(a, b):
    return lax.dot_general(a, b, (((0,), (0,)), ((), ())), preferred_element_type=F32)


def halves(x):
    hi = x.astype(BF)
    return hi, (x - hi.astype(F32)).astype(BF)


def spread_taps(w_ref, out_ref, back):
    zero = jnp.zeros((HID, HID), BF)
    for b in range(3):
        for a in range(3):
            block = w_ref[2 - a, 2 - b].T if back else w_ref[a, b]
            for s in range(2):
                k = a + s
                out_ref[pl.ds((k * 3 + b) * HID, HID), pl.ds(s * HID, HID)] = block
        out_ref[pl.ds(b * HID, HID), pl.ds(HID, HID)] = zero
        out_ref[pl.ds((9 + b) * HID, HID), pl.ds(0, HID)] = zero


def store_shifted(ref, pair, side, x):
    axis = x.ndim - 2
    ref[pair, side, :, pl.ds(HID, HID)] = x.astype(BF)
    ref[pair, side, :, pl.ds(0, HID)] = pltpu.roll(x, 1, axis).astype(BF)
    ref[pair, side, :, pl.ds(2 * HID, HID)] = pltpu.roll(x, WIDE - 1, axis).astype(BF)


def four_rows(ref, first, count, width, start=0):
    rows = [
        ref[pl.ds(first + k // 2, count), k % 2, pl.ds(start, width), :].reshape(count * width, 3 * HID)
        for k in range(4)
    ]
    return jnp.concatenate(rows, axis=-1)


def coarse_setup(lat, lon, nb_ref, cells_ref, rowmix_ref, colmix_ref):
    for block in range(9):
        dy, dx = block // 3, block % 3
        cells_ref[pl.ds(dy * CROW, CROW), pl.ds(dx * CCOL, CCOL), :] = (
            nb_ref[block, pl.ds(0, CELLS), :].astype(F32).reshape(CROW, CCOL, HID)
        )

    def line(block):
        return nb_ref[block, pl.ds(CELLS, 16), :].astype(F32)

    lane = lax.broadcasted_iota(jnp.int32, (16, HID), 1)
    rows = jnp.where(
        lane < 2,
        pltpu.roll(line(1), 98, 1),
        jnp.where(lane < 34, pltpu.roll(line(4), 2, 1), pltpu.roll(line(7), 34, 1)),
    )
    lane = lane[0:1]
    frac = rows[1:2] + rows[2:3] + rows[3:4]
    start = ((lane + 30) // 8 - 1).astype(F32)
    place = rows[0:1] - (lat * CROW - CROW).astype(F32) - start
    fine_row = lat * ROWS + lane - 2
    inside = ((fine_row >= 0) & (fine_row < 8 * ROWS)).astype(F32)
    for m in range(4):
        weight = jnp.where(place == float(m), 1.0 - frac, 0.0) + jnp.where(
            place == float(m - 1), frac, 0.0
        )
        rowmix_ref[pl.ds(m, 1), :] = weight * inside

    lane = lax.broadcasted_iota(jnp.int32, (16, HID), 1)
    edge = jnp.where(lane < 8, line(5), pltpu.roll(line(3), 16, 1))
    tables = []
    for part in (line(4), edge):
        frac = part[5:6] + part[6:7] + part[7:8]
        spot = part[4:5] - (lon * CCOL - CCOL).astype(F32)
        spot = jnp.where(spot < 0.0, spot + 128.0, spot)
        spot = jnp.where(spot >= 128.0, spot - 128.0, spot)
        cell = lax.broadcasted_iota(jnp.int32, (32, HID), 0).astype(F32)
        tables.append(
            jnp.where(cell == spot, 1.0 - frac, 0.0) + jnp.where(cell == spot + 1.0, frac, 0.0)
        )
    hi, lo = halves(jnp.concatenate(tables, axis=-1))
    colmix_ref[pl.ds(0, 32), :] = hi
    colmix_ref[pl.ds(32, 32), :] = lo


def lift(embed_ref, cells_ref, rowmix_ref, colmix_ref, mid_ref, l3_ref):
    cells = [cells_ref[LO_J + j] for j in range(NUM_J)]
    wide = jnp.concatenate(cells, axis=-1)
    wide = jnp.concatenate([wide, jnp.zeros((8, NUM_J * HID), F32)], axis=0).astype(BF)
    mid = dot_t(colmix_ref[...], jnp.concatenate([wide, wide], axis=0))
    mid_ref[...] = mid[0:WIDE]
    mix = rowmix_ref[...]
    for start in range(0, ROWS + 4, 12):
        rows = []
        for i in range(start, start + 12):
            first = (i + 30) // 8 - 1 - LO_J
            total = None
            for m in range(4):
                weight = mix[m : m + 1, i : i + 1]
                term = weight * mid_ref[:, pl.ds((first + m) * HID, HID)]
                total = term if total is None else total + term
            rows.append(total.astype(BF))
        lifted = dot(jnp.concatenate(rows, axis=0), embed_ref[...])
        for n in range(12):
            i = start + n
            store_shifted(l3_ref, i // 2, i % 2, lifted[n * WIDE : (n + 1) * WIDE])


def spread_own(cot_ref, c3_ref):
    def step(q, carry):
        for t in range(2):
            x = cot_ref[2 * q + t].astype(F32)
            own = pl.ds(0, COLS)
            c3_ref[q + 1, t, own, pl.ds(HID, HID)] = cot_ref[2 * q + t]
            c3_ref[q + 1, t, own, pl.ds(0, HID)] = pltpu.roll(x, 1, 0).astype(BF)
            c3_ref[q + 1, t, own, pl.ds(2 * HID, HID)] = pltpu.roll(x, COLS - 1, 0).astype(BF)
        return carry

    lax.fori_loop(0, ROWS // 2, step, 0)


def gather_columns(cot_ref, colpack_ref):
    spot = lax.broadcasted_iota(jnp.int32, (16, HID), 0) // 2
    for side, start in ((0, 0), (1, COLS - 16)):
        for g in range(ROWS // 8):
            total = None
            for n in range(8):
                x = cot_ref[8 * g + n, pl.ds(start, 16)].astype(F32)
                shift = (2 * n + 2 * side) % 16
                x = pltpu.roll(x, shift, 0) if shift else x
                total = x if n == 0 else jnp.where(spot == n, x, total)
            colpack_ref[side, g] = total.astype(BF)


def beside(colhalo_ref, tile, n):
    near = lax.broadcasted_iota(jnp.int32, (16, HID), 0) < 8
    right = colhalo_ref[1, tile].astype(F32)
    left = colhalo_ref[0, tile].astype(F32)
    right = pltpu.roll(right, 16 - 2 * n, 0) if n else right
    left = pltpu.roll(left, 14 - 2 * n, 0) if n < 7 else left
    return jnp.where(near, right, left)


def close_columns(cot_ref, colhalo_ref, c3_ref):
    def step(g, carry):
        for n in range(8):
            r = 8 * g + n
            last = cot_ref[r, pl.ds(COLS - 16, 16)].astype(F32)
            first = cot_ref[r, pl.ds(0, 16)].astype(F32)
            x = jnp.concatenate([last, beside(colhalo_ref, g, n), first], axis=0)
            west = pltpu.roll(x, 1, 0).astype(BF)
            east = pltpu.roll(x, 47, 0).astype(BF)
            wide = pl.ds(COLS, 16)
            q, t = 4 * g + n // 2 + 1, n % 2
            c3_ref[q, t, wide, pl.ds(HID, HID)] = x[16:32].astype(BF)
            c3_ref[q, t, wide, pl.ds(0, HID)] = west[16:32]
            c3_ref[q, t, pl.ds(0, 16), pl.ds(0, HID)] = west[32:48]
            c3_ref[q, t, pl.ds(COLS - 16, 32), pl.ds(2 * HID, HID)] = east[0:32]
        return carry

    lax.fori_loop(0, ROWS // 8, step, 0)


def close_rows(lat, rowhalo_ref, colhalo_ref, c3_ref):
    top = (lat > 0).astype(F32)
    bottom = (lat < 7).astype(F32)
    for t in range(2):
        x = jnp.concatenate([rowhalo_ref[0, t].astype(F32), beside(colhalo_ref, 4, 6 + t)], axis=0)
        store_shifted(c3_ref, 0, t, x * top)
        x = jnp.concatenate([rowhalo_ref[1, t].astype(F32), beside(colhalo_ref, 5, t)], axis=0)
        store_shifted(c3_ref, 17, t, x * bottom)


def back_inside(c3_ref, w2t_ref, back_ref):
    y = dot(four_rows(c3_ref, 1, 15, 96, 16), w2t_ref[...])
    back_ref[pl.ds(1, 15), pl.ds(16, 96), :] = y.reshape(15, 96, 2 * HID)


def back_around(c3_ref, w2t_ref, back_ref):
    parts = [
        four_rows(c3_ref, 1, 15, 16, 0),
        four_rows(c3_ref, 1, 15, 32, COLS - 16),
        four_rows(c3_ref, 0, 1, WIDE),
        four_rows(c3_ref, 16, 1, WIDE),
    ]
    y = dot(jnp.concatenate(parts, axis=0), w2t_ref[...])
    back_ref[pl.ds(1, 15), pl.ds(0, 16), :] = y[0:240].reshape(15, 16, 2 * HID)
    back_ref[pl.ds(1, 15), pl.ds(COLS - 16, 32), :] = y[240:720].reshape(15, 32, 2 * HID)
    back_ref[0] = y[720 : 720 + WIDE]
    back_ref[16] = y[720 + WIDE : 720 + 2 * WIDE]


def make_hidden(lat, l3_ref, w1_ref, h3_ref, slope_ref):
    def finish(pre_all, first, count):
        for p in range(count):
            for s in range(2):
                pre = pre_all[p * WIDE : (p + 1) * WIDE, s * HID : (s + 1) * HID]
                sig = 0.5 + 0.5 * jnp.tanh(0.5 * pre)
                hidden = pre * sig
                slope = sig + hidden * (1.0 - sig)
                if first + p == 0 and s == 0:
                    inside = (lat > 0).astype(F32)
                    hidden, slope = hidden * inside, slope * inside
                if first + p == 16 and s == 1:
                    inside = (lat < 7).astype(F32)
                    hidden, slope = hidden * inside, slope * inside
                h3_ref[first + p, s, :, pl.ds(HID, HID)] = hidden.astype(BF)
                slope_ref[first + p, :, pl.ds(s * HID, HID)] = slope

    waiting = None
    for first in range(0, 17, 3):
        count = min(3, 17 - first)
        pre_all = dot(four_rows(l3_ref, first, count, WIDE), w1_ref[...])
        if waiting is not None:
            finish(*waiting)
        waiting = (pre_all, first, count)
    finish(*waiting)


def shift_hidden(h3_ref):
    def step(p, carry):
        for s in range(2):
            x = h3_ref[p, s, :, pl.ds(HID, HID)].astype(F32)
            h3_ref[p, s, :, pl.ds(0, HID)] = pltpu.roll(x, 1, 0).astype(BF)
            h3_ref[p, s, :, pl.ds(2 * HID, HID)] = pltpu.roll(x, WIDE - 1, 0).astype(BF)
        return carry

    lax.fori_loop(0, 17, step, 0)


def make_delta(back_ref, slope_ref, d3_ref):
    def step(p, carry):
        for s in range(2):
            lanes = pl.ds(s * HID, HID)
            store_shifted(d3_ref, p, s, back_ref[p, :, lanes] * slope_ref[p, :, lanes])
        return carry

    lax.fori_loop(0, 17, step, 0)


def rows_from(ref, start, lanes):
    q, odd = start // 2, start % 2
    if odd == 0:
        return ref[pl.ds(q, 16), :, pl.ds(0, COLS), lanes].reshape(ROWS * COLS, -1)
    parts = [ref[pl.ds(q, 16), 1, pl.ds(0, COLS), lanes], ref[pl.ds(q + 1, 16), 0, pl.ds(0, COLS), lanes]]
    return jnp.stack(parts, axis=1).reshape(ROWS * COLS, -1)


def weight_grad(v_ref, v_start, u_ref, u_start, out_ref):
    centre = pl.ds(HID, HID)
    left = jnp.concatenate([rows_from(v_ref, v_start + a, centre) for a in range(3)], axis=-1)
    right = rows_from(u_ref, u_start, pl.ds(0, 3 * HID))
    grad = dot_t(left, right)
    for a in range(3):
        for b in range(3):
            block = grad[a * HID : (a + 1) * HID, (2 - b) * HID : (3 - b) * HID]
            out_ref[pl.ds((a * 3 + b) * 8, 8)] = block.reshape(8, 16, HID).astype(BF)


def back_to_embed(first, count, d3_ref, w1t_ref, cot_ref, rowmix_ref, colmix_ref, down_ref):
    y = dot(four_rows(d3_ref, first, count, COLS), w1t_ref[...])
    rows = []
    for p in range(count):
        for s in range(2):
            part = y[p * COLS : (p + 1) * COLS, s * HID : (s + 1) * HID]
            rows.append((cot_ref[2 * (first + p) + s].astype(F32) + part).astype(BF))
    low = dot(colmix_ref[:, pl.ds(0, COLS)], jnp.concatenate(rows, axis=-1))
    low = low[0:32] + low[32:64]
    mix = rowmix_ref[...]
    sums = {}
    for n in range(2 * count):
        i = 2 * first + n + 2
        base = (i + 30) // 8 - 1
        part = low[:, n * HID : (n + 1) * HID]
        for m in range(4):
            term = mix[m : m + 1, i : i + 1] * part
            sums[base + m] = term if base + m not in sums else sums[base + m] + term
    for j, value in sums.items():
        down_ref[j] = down_ref[j] + value


def embed_grad(cells_ref, down_ref, out_ref):
    window = cells_ref[...].reshape(12 * 24, HID).astype(BF)
    down = jnp.concatenate([down_ref[j, pl.ds(0, 24), :] for j in range(12)], axis=0)
    hi, lo = halves(down)
    grad = dot_t(window, hi) + dot_t(window, lo)
    out_ref[...] = grad[0 : EMBED_TILES * 16].reshape(EMBED_TILES, 16, HID).astype(BF)


def features_of(first, count, h3_ref, l3_ref, w2_ref, feat_ref):
    y = dot(four_rows(h3_ref, first, count, COLS), w2_ref[...])
    for p in range(count):
        for s in range(2):
            part = y[p * COLS : (p + 1) * COLS, s * HID : (s + 1) * HID]
            own = l3_ref[first + p + 1, s, pl.ds(0, COLS), pl.ds(HID, HID)].astype(F32)
            feat_ref[2 * (first + p) + s] = (own + part).astype(BF)


class Place:
    def __init__(self):
        self.lat = lax.axis_index("lat")
        self.lon = lax.axis_index("lon")
        self.core = lax.rem(self.lon, 2)
        self.z = lax.rem(self.lat, 2) * 2 + lax.rem(self.lon // 2, 2)
        self.plane = self.lon // 4 * 4 + self.lat // 2
        self.mate = (self.lat, self.lon + 1 - 2 * self.core)
        self.planes = [lax.rem(self.plane + d, 16) for d in range(1, 16)]
        self.plane_mates = [self.spot(q, self.z) for q in self.planes]
        self.z_mates = [self.spot(self.plane, lax.rem(self.z + d, 4)) for d in range(1, 4)]
        self.around = [(lax.rem(self.lat + dy + 8, 8), lax.rem(self.lon + dx + 16, 16)) for dy, dx in DIRS]

    def spot(self, plane, z):
        return (lax.rem(plane, 4) * 2 + z // 2, plane // 4 * 4 + lax.rem(z, 2) * 2 + self.core)


class Exchange:
    def __init__(self, copies, span, sems):
        self.copies = copies
        self.whole = [pltpu.make_async_copy(span, span, sem) for sem in sems]

    def start(self):
        for c in self.copies:
            c.start()

    def arrive(self):
        self.whole[1].wait()

    def sent(self):
        self.whole[0].wait()


def remote(src, dst, sems, target):
    return pltpu.make_async_remote_copy(
        src_ref=src, dst_ref=dst, send_sem=sems[0], recv_sem=sems[1], device_id=target, device_id_type=MESH
    )


class GradSum:
    def __init__(self, place, part, paired, half, got, mine, other, final, twin, sems):
        self.part, self.paired, self.half, self.got = part, paired, half, got
        self.mine, self.other, self.final, self.twin = mine, other, final, twin
        pairs = [(sems.at[2 * n], sems.at[2 * n + 1]) for n in range(5)]
        self.keep = place.core * HALF
        self.own = pl.ds(place.plane * PIECE, PIECE)
        away = part.at[pl.ds(HALF - self.keep, HALF)]
        self.pair = Exchange([remote(away, paired, pairs[0], place.mate)], paired, pairs[0])
        self.scatter = Exchange(
            [
                remote(half.at[pl.ds(q * PIECE, PIECE)], got.at[n], pairs[1], t)
                for n, (q, t) in enumerate(zip(place.planes, place.plane_mates))
            ],
            got,
            pairs[1],
        )
        self.column = Exchange(
            [remote(mine, other.at[n], pairs[2], t) for n, t in enumerate(place.z_mates)], other, pairs[2]
        )
        self.gather = Exchange(
            [remote(final.at[self.own], final.at[self.own], pairs[3], t) for t in place.plane_mates],
            final.at[pl.ds(0, 15 * PIECE)],
            pairs[3],
        )
        self.swap = Exchange([remote(final.at[pl.ds(0, HALF)], twin, pairs[4], place.mate)], twin, pairs[4])

    def step_pair(self):
        self.pair.start()

    def step_scatter(self):
        self.pair.arrive()
        total = self.part[pl.ds(self.keep, HALF)].astype(F32) + self.paired[...].astype(F32)
        self.half[pl.ds(0, HALF)] = total.astype(BF)
        self.half[pl.ds(HALF, 16 * PIECE - HALF)] = jnp.zeros((16 * PIECE - HALF, 16, HID), BF)
        self.scatter.start()

    def step_column(self):
        self.scatter.arrive()
        total = self.half[self.own].astype(F32)
        for n in range(15):
            total = total + self.got[n].astype(F32)
        self.mine[...] = total.astype(BF)
        self.column.start()

    def step_gather(self):
        self.column.arrive()
        total = self.mine[...].astype(F32)
        for n in range(3):
            total = total + self.other[n].astype(F32)
        self.final[self.own] = total.astype(BF)
        self.gather.start()

    def step_swap(self, full_ref, out_ref, sem, scale):
        self.gather.arrive()
        self.swap.start()
        self.outs = [
            pltpu.make_async_copy(full_ref.at[part], out_ref.at[part], sem.at[n])
            for n, part in enumerate((pl.ds(self.keep, HALF), pl.ds(HALF - self.keep, HALF)))
        ]
        full_ref[pl.ds(self.keep, HALF)] = self.final[pl.ds(0, HALF)].astype(F32) * scale
        self.outs[0].start()

    def finish(self, full_ref, scale):
        self.swap.arrive()
        full_ref[pl.ds(HALF - self.keep, HALF)] = self.twin[...].astype(F32) * scale
        self.outs[1].start()

    def drain(self):
        for e in (self.pair, self.scatter, self.column, self.gather, self.swap):
            e.sent()
        for out in self.outs:
            out.wait()


class SmallSum:
    def __init__(self, place, parts, slots, sems):
        self.parts, self.slots = parts, slots
        self.keep = pl.ds(place.core * 2, 3)
        self.away = pl.ds(2 - place.core * 2, 3)
        self.steps = []
        base = 0
        for g, targets in enumerate([[place.mate], place.z_mates, place.plane_mates, [place.mate]]):
            size = EMBED_TILES if g == 0 else 3
            pair = (sems.at[2 * g], sems.at[2 * g + 1])
            copies = []
            for n, t in enumerate(targets, base):
                copies.append(remote(parts.at[g, pl.ds(0, size)], slots.at[n, pl.ds(0, size)], pair, t))
            span = slots.at[pl.ds(base, len(targets)), pl.ds(0, size)]
            self.steps.append((base, len(targets), Exchange(copies, span, pair)))
            base += len(targets)

    def begin(self):
        self.steps[0][2].start()

    def pass_on(self, g):
        base, count, exchange = self.steps[g]
        exchange.arrive()
        here = self.keep if g == 0 else pl.ds(0, 3)
        total = self.parts[g, here].astype(F32)
        for n in range(count):
            total = total + self.slots[base + n, here].astype(F32)
        self.parts[g + 1, pl.ds(0, 3)] = total.astype(BF)
        self.steps[g + 1][2].start()

    def finish(self, out_ref, scale):
        base, _, exchange = self.steps[3]
        exchange.arrive()
        out_ref[self.away] = self.slots[base, pl.ds(0, 3)].astype(F32) * scale
        out_ref[self.keep] = self.parts[3, pl.ds(0, 3)].astype(F32) * scale
        for _, _, exchange in self.steps:
            exchange.sent()


def pack_block(coarse_ref, row_src_ref, row_frac_ref, col_src_ref, col_frac_ref, lines_ref, pack_ref):
    pack_ref[...] = jnp.zeros_like(pack_ref)
    pack_ref[pl.ds(0, CELLS), pl.ds(0, coarse_ref.shape[1])] = coarse_ref[...]
    lines_ref[...] = jnp.zeros_like(lines_ref)
    for row, src_ref, frac_ref in ((0, row_src_ref, row_frac_ref), (4, col_src_ref, col_frac_ref)):
        lanes = pl.ds(0, src_ref.shape[1])
        lines_ref[pl.ds(row, 1), lanes] = src_ref[...].astype(F32)
        left = frac_ref[...]
        for n in range(1, 4):
            term = left.astype(BF).astype(F32)
            lines_ref[pl.ds(row + n, 1), lanes] = term
            left = left - term
    pack_ref[pl.ds(CELLS, 16), :] = lines_ref[...].astype(BF)


def kernel(
    coarse_hbm, row_src_hbm, row_frac_hbm, col_src_hbm, col_frac_hbm, embed_hbm, conv1_hbm, conv2_hbm, cot_hbm,
    feat_out, gemb_out, g1_out, g2_out,
    feat_ref, gemb_ref, g1_ref, g2_ref, out_sem,
    coarse_ref, row_src_ref, row_frac_ref, col_src_ref, col_frac_ref, embed_in_ref, conv1_ref, conv2_ref, cot_ref,
    lines_ref, pack_ref, embed_ref,
    nb_ref, rowhalo_ref, colpack_ref, colhalo_ref, cells_ref, rowmix_ref, colmix_ref, mid_ref, down_ref,
    w1_ref, w2_ref, w1t_ref, w2t_ref, l3_ref, c3_ref, h3_ref, d3_ref, back_ref, slope_ref,
    part1, paired1, half1, got1, mine1, other1, final1, twin1,
    part2, paired2, half2, got2, mine2, other2, final2, twin2, eparts, eslots,
    load_sem, halo_sem, sum_sem,
):
    place = Place()
    lat, lon = place.lat, place.lon
    scale = 1.0 / math.sqrt(8 * ROWS * 16 * COLS)

    def apart(stage, *args):
        @pl.when(lat < 8)
        def _():
            stage(*args)

    barrier = pltpu.get_barrier_semaphore()
    partners = [place.mate] + place.around + place.z_mates + place.plane_mates
    for spot in partners:
        pl.semaphore_signal(barrier, inc=1, device_id=spot, device_id_type=MESH)

    pairs = [
        (coarse_hbm, coarse_ref), (row_src_hbm, row_src_ref), (row_frac_hbm, row_frac_ref),
        (col_src_hbm, col_src_ref), (col_frac_hbm, col_frac_ref), (cot_hbm, cot_ref),
        (conv2_hbm, conv2_ref), (conv1_hbm, conv1_ref), (embed_hbm, embed_in_ref),
    ]
    loads = [pltpu.make_async_copy(src, dst, load_sem.at[n]) for n, (src, dst) in enumerate(pairs)]
    for load in loads:
        load.start()

    packs, columns, rows, corners = [], [], [], []
    pairs = [(halo_sem.at[2 * n], halo_sem.at[2 * n + 1]) for n in range(4)]
    for n, (dy, dx) in enumerate(DIRS):
        slot = (1 - dy) * 3 + 1 - dx
        packs.append(remote(pack_ref, nb_ref.at[slot], pairs[0], place.around[n]))
        if dx == 0:
            src = cot_ref.at[pl.ds(0 if dy == -1 else ROWS - 2, 2)]
            rows.append(remote(src, rowhalo_ref.at[0 if dy == 1 else 1], pairs[2], place.around[n]))
        else:
            side = 0 if dx == -1 else 1
            src = colpack_ref.at[side, {-1: pl.ds(0, 1), 0: pl.ds(0, 4), 1: pl.ds(3, 1)}[dy]]
            dst = colhalo_ref.at[1 - side, {1: pl.ds(4, 1), 0: pl.ds(0, 4), -1: pl.ds(5, 1)}[dy]]
            if dy == 0:
                columns.append(remote(src, dst, pairs[1], place.around[n]))
            else:
                corners.append(remote(src, dst, pairs[3], place.around[n]))
    packs = Exchange(packs, nb_ref.at[pl.ds(0, 8)], pairs[0])
    columns = Exchange(columns, colhalo_ref.at[:, pl.ds(0, 4)], pairs[1])
    rows = Exchange(rows, rowhalo_ref, pairs[2])
    corners = Exchange(corners, colhalo_ref.at[:, pl.ds(4, 2)], pairs[3])
    sum1 = GradSum(place, part1, paired1, half1, got1, mine1, other1, final1, twin1, sum_sem.at[pl.ds(0, 10)])
    sum2 = GradSum(place, part2, paired2, half2, got2, mine2, other2, final2, twin2, sum_sem.at[pl.ds(10, 10)])
    small = SmallSum(place, eparts, eslots, sum_sem.at[pl.ds(20, 8)])

    for load in loads[0:5]:
        load.wait()
    pack_block(coarse_ref, row_src_ref, row_frac_ref, col_src_ref, col_frac_ref, lines_ref, pack_ref)
    loads[5].wait()
    pl.semaphore_wait(barrier, len(partners))
    packs.start()
    gather_columns(cot_ref, colpack_ref)
    columns.start()

    nb_ref[4] = pack_ref[...]
    for load in loads[6:9]:
        load.wait()
    spread_taps(conv2_ref, w2t_ref, True)
    spread_own(cot_ref, c3_ref)
    apart(back_inside, c3_ref, w2t_ref, back_ref)
    spread_taps(conv1_ref, w1_ref, False)
    spread_taps(conv2_ref, w2_ref, False)
    spread_taps(conv1_ref, w1t_ref, True)
    embed_ref[...] = jnp.zeros_like(embed_ref)
    embed_ref[pl.ds(0, embed_in_ref.shape[0]), :] = embed_in_ref[...]
    down_ref[...] = jnp.zeros_like(down_ref)

    packs.arrive()
    corners.start()
    rows.start()
    coarse_setup(lat, lon, nb_ref, cells_ref, rowmix_ref, colmix_ref)
    lift(embed_ref, cells_ref, rowmix_ref, colmix_ref, mid_ref, l3_ref)
    apart(make_hidden, lat, l3_ref, w1_ref, h3_ref, slope_ref)
    columns.arrive()
    close_columns(cot_ref, colhalo_ref, c3_ref)
    apart(weight_grad, h3_ref, 0, c3_ref, 2, part2)
    sum2.step_pair()
    corners.arrive()
    rows.arrive()
    close_rows(lat, rowhalo_ref, colhalo_ref, c3_ref)
    apart(back_around, c3_ref, w2t_ref, back_ref)
    sum2.step_scatter()
    make_delta(back_ref, slope_ref, d3_ref)
    apart(weight_grad, l3_ref, 1, d3_ref, 1, part1)
    sum1.step_pair()
    apart(back_to_embed, 0, 8, d3_ref, w1t_ref, cot_ref, rowmix_ref, colmix_ref, down_ref)
    sum1.step_scatter()
    apart(back_to_embed, 8, 8, d3_ref, w1t_ref, cot_ref, rowmix_ref, colmix_ref, down_ref)
    embed_grad(cells_ref, down_ref, eparts.at[0])
    small.begin()
    sum2.step_column()
    shift_hidden(h3_ref)
    small.pass_on(0)
    done = [
        pltpu.make_async_copy(feat_ref.at[pl.ds(n * 16, 16)], feat_out.at[pl.ds(n * 16, 16)], out_sem.at[n])
        for n in range(2)
    ]
    apart(features_of, 0, 8, h3_ref, l3_ref, w2_ref, feat_ref)
    done[0].start()
    apart(features_of, 8, 8, h3_ref, l3_ref, w2_ref, feat_ref)
    done[1].start()
    sum2.step_gather()
    sum1.step_column()
    small.pass_on(1)
    sum1.step_gather()
    sum2.step_swap(g2_ref, g2_out, out_sem.at[pl.ds(2, 2)], scale)
    small.pass_on(2)
    sum2.finish(g2_ref, scale)
    small.finish(gemb_ref, scale)
    done.append(pltpu.make_async_copy(gemb_ref, gemb_out, out_sem.at[4]))
    done[2].start()
    sum1.step_swap(g1_ref, g1_out, out_sem.at[pl.ds(5, 2)], scale)
    sum1.finish(g1_ref, scale)
    for exchange in (packs, columns, rows, corners):
        exchange.sent()
    for copy in done:
        copy.wait()
    sum2.drain()
    sum1.drain()


def write_out(*refs):
    count = (len(refs) - 1) // 2
    copies = [pltpu.make_async_copy(refs[n], refs[count + n], refs[-1].at[n]) for n in range(count)]
    for copy in copies:
        copy.start()
    for copy in copies:
        copy.wait()


RESULTS = [
    ((ROWS, COLS, HID), BF),
    ((EMBED_TILES, 16, HID), F32),
    ((TILES, 16, HID), F32),
    ((TILES, 16, HID), F32),
]


def scratch_list(channels=73):
    dma = pltpu.SemaphoreType.DMA
    line = lambda n, kind: pltpu.VMEM((1, n), kind)
    tiles = lambda *n: pltpu.VMEM((*n, 16, HID), BF)
    grad = [
        tiles(TILES), tiles(HALF), tiles(16 * PIECE), tiles(15, PIECE),
        tiles(PIECE), tiles(3, PIECE), tiles(16 * PIECE), tiles(HALF),
    ]
    return (
        [pltpu.VMEM(shape, kind) for shape, kind in RESULTS]
        + [dma((7,))]
        + [
            pltpu.VMEM((CELLS, channels), BF),
            line(ROWS, jnp.int32), line(ROWS, F32), line(COLS, jnp.int32), line(COLS, F32),
            pltpu.VMEM((channels, HID), BF),
            pltpu.VMEM((3, 3, HID, HID), BF),
            pltpu.VMEM((3, 3, HID, HID), BF),
            pltpu.VMEM((ROWS, COLS, HID), BF),
            pltpu.VMEM((16, HID), F32),
            pltpu.VMEM((PACK, HID), BF),
            pltpu.VMEM((HID, HID), BF),
            pltpu.VMEM((9, PACK, HID), BF),
            pltpu.VMEM((2, 2, COLS, HID), BF),
            tiles(2, 4),
            tiles(2, 6),
            pltpu.VMEM((12, 24, HID), F32),
            pltpu.VMEM((8, HID), F32),
            pltpu.VMEM((64, 2 * HID), BF),
            pltpu.VMEM((WIDE, NUM_J * HID), F32),
            pltpu.VMEM((12, 32, HID), F32),
        ]
        + [pltpu.VMEM((12 * HID, 2 * HID), BF)] * 4
        + [pltpu.VMEM((18, 2, WIDE, 3 * HID), BF)] * 2
        + [pltpu.VMEM((17, 2, WIDE, 3 * HID), BF)] * 2
        + [pltpu.VMEM((17, WIDE, 2 * HID), F32)] * 2
        + grad
        + grad
        + [tiles(4, EMBED_TILES), tiles(20, EMBED_TILES)]
        + [dma((9,))]
        + [dma((8,)), dma((28,))]
    )


def on_device(coarse, row_src, row_frac, col_src, col_frac, embed_weight, conv1_weight, conv2_weight, cotangent):
    channels = coarse.shape[0]
    cells = jnp.transpose(coarse, (1, 2, 0)).reshape(CELLS, channels)
    lines = [v.reshape(1, -1) for v in (row_src, row_frac, col_src, col_frac)]
    results = pl.pallas_call(
        kernel,
        out_shape=[pltpu.VMEM(shape, kind) for shape, kind in RESULTS],
        in_specs=[pl.BlockSpec(memory_space=pl.ANY)] * 9,
        out_specs=[pl.BlockSpec(memory_space=pl.ANY)] * 4,
        scratch_shapes=scratch_list(channels),
        compiler_params=pltpu.CompilerParams(
            collective_id=0, has_side_effects=True, vmem_limit_bytes=56 * 2**20
        ),
    )(cells, *lines, embed_weight, conv1_weight, conv2_weight, cotangent)
    features, grad_embed, grad_conv1, grad_conv2 = pl.pallas_call(
        write_out,
        out_shape=[jax.ShapeDtypeStruct(shape, kind) for shape, kind in RESULTS],
        in_specs=[pl.BlockSpec(memory_space=pl.ANY)] * 4,
        out_specs=[pl.BlockSpec(memory_space=pl.ANY)] * 4,
        scratch_shapes=[pltpu.SemaphoreType.DMA((4,))],
    )(*[pltpu.with_memory_space_constraint(r, pltpu.VMEM) for r in results])
    taps = (3, 3, HID, HID)
    grad_embed = grad_embed.reshape(EMBED_TILES * 16, HID)[:channels]
    return (features, grad_embed, grad_conv1.reshape(taps), grad_conv2.reshape(taps))


def solution(mesh):
    in_specs = (
        P(None, "lat", "lon"),
        P("lat"),
        P("lat"),
        P("lon"),
        P("lon"),
        P(),
        P(),
        P(),
        P("lat", "lon", None),
    )
    out_specs = (P("lat", "lon", None), P(), P(), P())
    return jax.shard_map(
        on_device, mesh=mesh, in_specs=in_specs, out_specs=out_specs, check_vma=False
    )
```

```python
import functools
import math

import jax
import jax.numpy as jnp
from jax import lax
from jax.experimental import pallas as pl
from jax.experimental.pallas import tpu as pltpu
from jax.sharding import PartitionSpec as P

MESH = pl.DeviceIdType.MESH
BF = jnp.bfloat16
F32 = jnp.float32

ROWS = 32
COLS = 128
WIDE = 144
HID = 128
CROW = 4
CCOL = 8
CELLS = CROW * CCOL
PACK = 48
TILES = 72
HALF = 36
PIECE = 3
OWNERS = 12


def owner_rank(plane):
    x, y = plane // 4, lax.rem(plane, 4)
    return x != y, jnp.minimum(x * 3 + y - (y > x).astype(jnp.int32), OWNERS - 1)

EMBED_TILES = 5
DIRS = [(dy, dx) for dy in (-1, 0, 1) for dx in (-1, 0, 1) if (dy, dx) != (0, 0)]


def dot(a, b):
    return jnp.dot(a, b, preferred_element_type=F32)


def dot_t(a, b):
    return lax.dot_general(a, b, (((0,), (0,)), ((), ())), preferred_element_type=F32)


def halves(x):
    hi = x.astype(BF)
    return hi, (x - hi.astype(F32)).astype(BF)


def spread_taps(w_ref, out_ref, back):
    zero = jnp.zeros((HID, HID), BF)
    for b in range(3):
        for a in range(3):
            block = w_ref[2 - a, 2 - b].T if back else w_ref[a, b]
            for s in range(2):
                k = a + s
                out_ref[pl.ds((k * 3 + b) * HID, HID), pl.ds(s * HID, HID)] = block
        out_ref[pl.ds(b * HID, HID), pl.ds(HID, HID)] = zero
        out_ref[pl.ds((9 + b) * HID, HID), pl.ds(0, HID)] = zero


def store_shifted(ref, pair, side, x):
    axis = x.ndim - 2
    ref[pair, side, :, pl.ds(HID, HID)] = x.astype(BF)
    ref[pair, side, :, pl.ds(0, HID)] = pltpu.roll(x, 1, axis).astype(BF)
    ref[pair, side, :, pl.ds(2 * HID, HID)] = pltpu.roll(x, WIDE - 1, axis).astype(BF)


def four_rows(ref, first, count, width, start=0):
    rows = [
        ref[pl.ds(first + k // 2, count), k % 2, pl.ds(start, width), :].reshape(count * width, 3 * HID)
        for k in range(4)
    ]
    return jnp.concatenate(rows, axis=-1)


def coarse_setup(lat, lon, nb_ref, cells_ref, rowmix_ref, colmix_ref):
    for block in range(9):
        dy, dx = block // 3, block % 3
        cells_ref[pl.ds(dy * CROW, CROW), pl.ds(dx * CCOL, CCOL), :] = (
            nb_ref[block, pl.ds(0, CELLS), :].astype(F32).reshape(CROW, CCOL, HID)
        )

    def line(block):
        return nb_ref[block, pl.ds(CELLS, 16), :].astype(F32)

    lane = lax.broadcasted_iota(jnp.int32, (16, HID), 1)
    rows = jnp.where(
        lane < 2,
        pltpu.roll(line(1), 98, 1),
        jnp.where(lane < 34, pltpu.roll(line(4), 2, 1), pltpu.roll(line(7), 34, 1)),
    )
    lane = lane[0:1]
    frac = rows[1:2] + rows[2:3] + rows[3:4]
    start = ((lane + 30) // 8 - 1).astype(F32)
    place = rows[0:1] - (lat * CROW - CROW).astype(F32) - start
    fine_row = lat * ROWS + lane - 2
    inside = ((fine_row >= 0) & (fine_row < 8 * ROWS)).astype(F32)
    for m in range(4):
        weight = jnp.where(place == float(m), 1.0 - frac, 0.0) + jnp.where(
            place == float(m - 1), frac, 0.0
        )
        rowmix_ref[pl.ds(m, 1), :] = weight * inside

    lane = lax.broadcasted_iota(jnp.int32, (16, HID), 1)
    edge = jnp.where(lane < 8, line(5), pltpu.roll(line(3), 16, 1))
    tables = []
    for part in (line(4), edge):
        frac = part[5:6] + part[6:7] + part[7:8]
        spot = part[4:5] - (lon * CCOL - CCOL).astype(F32)
        spot = jnp.where(spot < 0.0, spot + 128.0, spot)
        spot = jnp.where(spot >= 128.0, spot - 128.0, spot)
        cell = lax.broadcasted_iota(jnp.int32, (32, HID), 0).astype(F32)
        tables.append(
            jnp.where(cell == spot, 1.0 - frac, 0.0) + jnp.where(cell == spot + 1.0, frac, 0.0)
        )
    hi, lo = halves(jnp.concatenate(tables, axis=-1))
    colmix_ref[pl.ds(0, 32), :] = hi
    colmix_ref[pl.ds(32, 32), :] = lo


def spread_own(cot_ref, c3_ref):
    def step(q, carry):
        for t in range(2):
            x = cot_ref[2 * q + t].astype(F32)
            own = pl.ds(0, COLS)
            c3_ref[q + 1, t, own, pl.ds(HID, HID)] = cot_ref[2 * q + t]
            c3_ref[q + 1, t, own, pl.ds(0, HID)] = pltpu.roll(x, 1, 0).astype(BF)
            c3_ref[q + 1, t, own, pl.ds(2 * HID, HID)] = pltpu.roll(x, COLS - 1, 0).astype(BF)
        return carry

    lax.fori_loop(0, ROWS // 2, step, 0)


def gather_columns(cot_ref, colpack_ref):
    spot = lax.broadcasted_iota(jnp.int32, (16, HID), 0) // 2
    for side, start in ((0, 0), (1, COLS - 16)):
        for g in range(ROWS // 8):
            total = None
            for n in range(8):
                x = cot_ref[8 * g + n, pl.ds(start, 16)].astype(F32)
                shift = (2 * n + 2 * side) % 16
                x = pltpu.roll(x, shift, 0) if shift else x
                total = x if n == 0 else jnp.where(spot == n, x, total)
            colpack_ref[side, g] = total.astype(BF)


def beside(colhalo_ref, tile, n):
    near = lax.broadcasted_iota(jnp.int32, (16, HID), 0) < 8
    right = colhalo_ref[1, tile].astype(F32)
    left = colhalo_ref[0, tile].astype(F32)
    right = pltpu.roll(right, 16 - 2 * n, 0) if n else right
    left = pltpu.roll(left, 14 - 2 * n, 0) if n < 7 else left
    return jnp.where(near, right, left)


def close_columns(cot_ref, colhalo_ref, c3_ref):
    def step(g, carry):
        for n in range(8):
            r = 8 * g + n
            last = cot_ref[r, pl.ds(COLS - 16, 16)].astype(F32)
            first = cot_ref[r, pl.ds(0, 16)].astype(F32)
            x = jnp.concatenate([last, beside(colhalo_ref, g, n), first], axis=0)
            west = pltpu.roll(x, 1, 0).astype(BF)
            east = pltpu.roll(x, 47, 0).astype(BF)
            wide = pl.ds(COLS, 16)
            q, t = 4 * g + n // 2 + 1, n % 2
            c3_ref[q, t, wide, pl.ds(HID, HID)] = x[16:32].astype(BF)
            c3_ref[q, t, wide, pl.ds(0, HID)] = west[16:32]
            c3_ref[q, t, pl.ds(0, 16), pl.ds(0, HID)] = west[32:48]
            c3_ref[q, t, pl.ds(COLS - 16, 32), pl.ds(2 * HID, HID)] = east[0:32]
        return carry

    lax.fori_loop(0, ROWS // 8, step, 0)


def close_rows(lat, rowhalo_ref, colhalo_ref, c3_ref):
    top = (lat > 0).astype(F32)
    bottom = (lat < 7).astype(F32)
    for t in range(2):
        x = jnp.concatenate([rowhalo_ref[0, t].astype(F32), beside(colhalo_ref, 4, 6 + t)], axis=0)
        store_shifted(c3_ref, 0, t, x * top)
        x = jnp.concatenate([rowhalo_ref[1, t].astype(F32), beside(colhalo_ref, 5, t)], axis=0)
        store_shifted(c3_ref, 17, t, x * bottom)


def back_inside(c3_ref, w2t_ref, back_ref):
    y = dot(four_rows(c3_ref, 1, 15, 96, 16), w2t_ref[...])
    back_ref[pl.ds(1, 15), pl.ds(16, 96), :] = y.reshape(15, 96, 2 * HID)


def back_around(c3_ref, w2t_ref, back_ref):
    parts = [
        four_rows(c3_ref, 1, 15, 16, 0),
        four_rows(c3_ref, 1, 15, 32, COLS - 16),
        four_rows(c3_ref, 0, 1, WIDE),
        four_rows(c3_ref, 16, 1, WIDE),
    ]
    y = dot(jnp.concatenate(parts, axis=0), w2t_ref[...])
    back_ref[pl.ds(1, 15), pl.ds(0, 16), :] = y[0:240].reshape(15, 16, 2 * HID)
    back_ref[pl.ds(1, 15), pl.ds(COLS - 16, 32), :] = y[240:720].reshape(15, 32, 2 * HID)
    back_ref[0] = y[720 : 720 + WIDE]
    back_ref[16] = y[720 + WIDE : 720 + 2 * WIDE]


def lift_and_hide(lat, embed_ref, cells_ref, rowmix_ref, colmix_ref, w1_ref, l3_ref, h3_ref, slope_ref):
    hi, lo = colmix_ref[pl.ds(0, 32), :], colmix_ref[pl.ds(32, 32), :]
    mixer = jnp.concatenate([hi, lo, hi], axis=0).T[0:WIDE]
    mix = rowmix_ref[...]
    step = 6

    def lift(start):
        rows = []
        for i in range(start, start + step):
            first = (i + 30) // 8 - 1
            total = None
            for m in range(4):
                term = mix[m : m + 1, i : i + 1] * cells_ref[first + m]
                total = term if total is None else total + term
            rows.append(total)
        wide = jnp.concatenate(rows, axis=-1)
        wide = jnp.concatenate([wide, jnp.zeros((8, step * HID), F32)], axis=0)
        hi, lo = halves(wide)
        fine = dot(mixer, jnp.concatenate([hi, hi, lo], axis=0)).astype(BF)
        fine = jnp.concatenate([fine[:, n * HID : (n + 1) * HID] for n in range(step)], axis=0)
        lifted = dot(fine, embed_ref[...])
        for n in range(step):
            i = start + n
            store_shifted(l3_ref, i // 2, i % 2, lifted[n * WIDE : (n + 1) * WIDE])

    def finish(pre_all, first, count):
        for p in range(count):
            for s in range(2):
                pre = pre_all[p * WIDE : (p + 1) * WIDE, s * HID : (s + 1) * HID]
                sig = 0.5 + 0.5 * jnp.tanh(0.5 * pre)
                hidden = pre * sig
                slope = sig + hidden * (1.0 - sig)
                if first + p == 0 and s == 0:
                    inside = (lat > 0).astype(F32)
                    hidden, slope = hidden * inside, slope * inside
                if first + p == 16 and s == 1:
                    inside = (lat < 7).astype(F32)
                    hidden, slope = hidden * inside, slope * inside
                h3_ref[first + p, s, :, pl.ds(HID, HID)] = hidden.astype(BF)
                slope_ref[first + p, :, pl.ds(s * HID, HID)] = slope

    waiting = None
    lift(0)
    lift(step)
    for first in range(0, 17, 3):
        count = min(3, 17 - first)
        pre_all = dot(four_rows(l3_ref, first, count, WIDE), w1_ref[...])
        if 2 * first + 2 * step < ROWS + 4:
            lift(2 * first + 2 * step)
        if waiting is not None:
            finish(*waiting)
        waiting = (pre_all, first, count)
    finish(*waiting)


def shift_hidden(h3_ref):
    def step(p, carry):
        for s in range(2):
            x = h3_ref[p, s, :, pl.ds(HID, HID)].astype(F32)
            h3_ref[p, s, :, pl.ds(0, HID)] = pltpu.roll(x, 1, 0).astype(BF)
            h3_ref[p, s, :, pl.ds(2 * HID, HID)] = pltpu.roll(x, WIDE - 1, 0).astype(BF)
        return carry

    lax.fori_loop(0, 17, step, 0)


def make_delta(back_ref, slope_ref, d3_ref, first, count):
    for p in range(first, first + count):
        for s in range(2):
            lanes = pl.ds(s * HID, HID)
            store_shifted(d3_ref, p, s, back_ref[p, :, lanes] * slope_ref[p, :, lanes])


def rows_from(ref, start, lanes, count=ROWS):
    q, odd, half = start // 2, start % 2, count // 2
    if odd == 0:
        return ref[pl.ds(q, half), :, pl.ds(0, COLS), lanes].reshape(count * COLS, -1)
    parts = [
        ref[pl.ds(q, half), 1, pl.ds(0, COLS), lanes],
        ref[pl.ds(q + 1, half), 0, pl.ds(0, COLS), lanes],
    ]
    return jnp.stack(parts, axis=1).reshape(count * COLS, -1)


def tap_products(v_ref, v_start, u_ref, u_start, count=ROWS):
    turned = []
    for n in range(v_start, v_start + count + 2):
        turned.append(v_ref[n // 2, n % 2, pl.ds(0, COLS), pl.ds(HID, HID)].T)
    left = [jnp.concatenate(turned[a : a + count], axis=1) for a in range(3)]
    wide = dot(jnp.concatenate(left, axis=0), rows_from(u_ref, u_start, pl.ds(0, 2 * HID), count))
    left = [jnp.concatenate(turned[a : a + count : 2], axis=1) for a in range(4)]
    right = []
    for n in (u_start, u_start + 1):
        rows = u_ref[pl.ds(n // 2, count // 2), n % 2, pl.ds(0, COLS), pl.ds(2 * HID, HID)]
        right.append(rows.reshape(count // 2 * COLS, HID))
    last = dot(jnp.concatenate(left, axis=0), jnp.concatenate(right, axis=-1))
    blocks = []
    for a in range(3):
        line = wide[a * HID : (a + 1) * HID]
        third = last[a * HID : (a + 1) * HID, 0:HID] + last[(a + 1) * HID : (a + 2) * HID, HID : 2 * HID]
        blocks.append([line[:, 0:HID], line[:, HID : 2 * HID], third])
    return blocks


def store_taps(blocks, out_ref):
    for a in range(3):
        for b in range(3):
            out_ref[pl.ds((a * 3 + b) * 8, 8)] = blocks[a][2 - b].reshape(8, 16, HID).astype(BF)


def weight_grad(v_ref, v_start, u_ref, u_start, out_ref):
    store_taps(tap_products(v_ref, v_start, u_ref, u_start), out_ref)


def delta_and_grad(back_ref, slope_ref, d3_ref, l3_ref, out_ref):
    make_delta(back_ref, slope_ref, d3_ref, 0, 9)
    one = tap_products(l3_ref, 1, d3_ref, 1, 16)
    make_delta(back_ref, slope_ref, d3_ref, 9, 8)
    two = tap_products(l3_ref, 17, d3_ref, 17, 16)
    store_taps([[x + y for x, y in zip(*lines)] for lines in zip(one, two)], out_ref)


def back_to_embed(first, count, d3_ref, w1t_ref, cot_ref, rowmix_ref, colmix_ref, down_ref):
    y = dot(four_rows(d3_ref, first, count, COLS), w1t_ref[...])
    rows = []
    for p in range(count):
        for s in range(2):
            part = y[p * COLS : (p + 1) * COLS, s * HID : (s + 1) * HID]
            rows.append((cot_ref[2 * (first + p) + s].astype(F32) + part).astype(BF))
    low = dot(colmix_ref[:, pl.ds(0, COLS)], jnp.concatenate(rows, axis=-1))
    low = low[0:32] + low[32:64]
    mix = rowmix_ref[...]
    sums = {}
    for n in range(2 * count):
        i = 2 * first + n + 2
        base = (i + 30) // 8 - 1
        part = low[:, n * HID : (n + 1) * HID]
        for m in range(4):
            term = mix[m : m + 1, i : i + 1] * part
            sums[base + m] = term if base + m not in sums else sums[base + m] + term
    for j, value in sums.items():
        down_ref[j] = down_ref[j] + value


def embed_grad(cells_ref, down_ref, out_ref):
    window = cells_ref[...].reshape(12 * 24, HID).astype(BF)
    down = jnp.concatenate([down_ref[j, pl.ds(0, 24), :] for j in range(12)], axis=0)
    hi, lo = halves(down)
    grad = dot_t(window, hi) + dot_t(window, lo)
    out_ref[...] = grad[0 : EMBED_TILES * 16].reshape(EMBED_TILES, 16, HID).astype(BF)


def features_of(first, count, h3_ref, l3_ref, w2_ref, feat_ref):
    y = dot(four_rows(h3_ref, first, count, COLS), w2_ref[...])
    for p in range(count):
        for s in range(2):
            part = y[p * COLS : (p + 1) * COLS, s * HID : (s + 1) * HID]
            own = l3_ref[first + p + 1, s, pl.ds(0, COLS), pl.ds(HID, HID)].astype(F32)
            feat_ref[2 * (first + p) + s] = (own + part).astype(BF)


class Place:
    def __init__(self):
        self.lat = lax.axis_index("lat")
        self.lon = lax.axis_index("lon")
        self.core = lax.rem(self.lon, 2)
        self.z = lax.rem(self.lat, 2) * 2 + lax.rem(self.lon // 2, 2)
        self.plane = self.lon // 4 * 4 + self.lat // 2
        self.mate = (self.lat, self.lon + 1 - 2 * self.core)
        self.planes = [lax.rem(self.plane + d, 16) for d in range(1, 16)]
        self.plane_mates = [self.spot(q, self.z) for q in self.planes]
        x, y = self.plane // 4, lax.rem(self.plane, 4)
        self.x_mates = [self.spot(lax.rem(x + d, 4) * 4 + y, self.z) for d in range(1, 4)]
        self.y_mates = [self.spot(x * 4 + lax.rem(y + d, 4), self.z) for d in range(1, 4)]
        self.z_mates = [self.spot(self.plane, lax.rem(self.z + d, 4)) for d in range(1, 4)]
        self.around = [(lax.rem(self.lat + dy + 8, 8), lax.rem(self.lon + dx + 16, 16)) for dy, dx in DIRS]

    def spot(self, plane, z):
        return (lax.rem(plane, 4) * 2 + z // 2, plane // 4 * 4 + lax.rem(z, 2) * 2 + self.core)


class Exchange:
    def __init__(self, copies, span, sems):
        self.copies = copies
        self.whole = [pltpu.make_async_copy(span, span, sem) for sem in sems]

    def start(self):
        for c in self.copies:
            c.start()

    def arrive(self):
        self.whole[1].wait()

    def sent(self):
        self.whole[0].wait()


def remote(src, dst, sems, target):
    return pltpu.make_async_remote_copy(
        src_ref=src, dst_ref=dst, send_sem=sems[0], recv_sem=sems[1], device_id=target, device_id_type=MESH
    )


class GradSum:
    def __init__(self, place, part, paired, half, got, mine, other, final, twin, sems):
        self.part, self.paired, self.half, self.got = part, paired, half, got
        self.mine, self.other, self.final, self.twin = mine, other, final, twin
        pairs = [(sems.at[2 * n], sems.at[2 * n + 1]) for n in range(5)]
        self.place = place
        self.owner, rank = owner_rank(place.plane)
        self.keep = place.core * HALF
        self.own = pl.ds(rank * PIECE, PIECE)
        away = part.at[pl.ds(HALF - self.keep, HALF)]
        self.pair = Exchange([remote(away, paired, pairs[0], place.mate)], paired, pairs[0])
        self.scatter_sems, self.gather_sems = pairs[1], pairs[3]
        self.column = Exchange(
            [remote(mine, other.at[n], pairs[2], t) for n, t in enumerate(place.z_mates)], other, pairs[2]
        )
        self.swap = Exchange([remote(final, twin, pairs[4], place.mate)], twin, pairs[4])

    def take(self, ref, count, sem):
        span = ref.at[pl.ds(0, count * PIECE)]
        pltpu.make_async_copy(span, span, sem).wait()

    def take_others(self, ref, sem):
        @pl.when(self.owner)
        def _():
            self.take(ref, OWNERS - 1, sem)

        @pl.when(jnp.logical_not(self.owner))
        def _():
            self.take(ref, OWNERS, sem)

    def step_pair(self):
        self.pair.start()

    def step_scatter(self):
        self.pair.arrive()
        total = self.part[pl.ds(self.keep, HALF)].astype(F32) + self.paired[...].astype(F32)
        self.half[...] = total.astype(BF)
        for n, (q, t) in enumerate(zip(self.place.planes, self.place.plane_mates)):
            owner, rank = owner_rank(q)

            @pl.when(owner)
            def _():
                piece = self.half.at[pl.ds(rank * PIECE, PIECE)]
                remote(piece, self.got.at[pl.ds(n * PIECE, PIECE)], self.scatter_sems, t).start()

    def step_column(self):
        @pl.when(self.owner)
        def _():
            self.take(self.got, 15, self.scatter_sems[1])
            total = self.half[self.own].astype(F32)
            for n in range(15):
                total = total + self.got[pl.ds(n * PIECE, PIECE)].astype(F32)
            self.mine[...] = total.astype(BF)
            self.column.start()

    def step_gather(self):
        @pl.when(self.owner)
        def _():
            self.column.arrive()
            total = self.mine[...].astype(F32)
            for n in range(3):
                total = total + self.other[n].astype(F32)
            self.final[self.own] = total.astype(BF)
            for t in self.place.plane_mates:
                remote(self.final.at[self.own], self.final.at[self.own], self.gather_sems, t).start()

    def step_swap(self, full_ref, out_ref, sem, scale):
        self.take_others(self.final, self.gather_sems[1])
        self.swap.start()
        self.outs = [
            pltpu.make_async_copy(full_ref.at[part], out_ref.at[part], sem.at[n])
            for n, part in enumerate((pl.ds(self.keep, HALF), pl.ds(HALF - self.keep, HALF)))
        ]
        full_ref[pl.ds(self.keep, HALF)] = self.final[...].astype(F32) * scale
        self.outs[0].start()

    def finish(self, full_ref, scale):
        self.swap.arrive()
        full_ref[pl.ds(HALF - self.keep, HALF)] = self.twin[...].astype(F32) * scale
        self.outs[1].start()

    def drain(self):
        self.pair.sent()
        self.swap.sent()
        self.take_others(self.half, self.scatter_sems[0])

        @pl.when(self.owner)
        def _():
            self.column.sent()
            self.take(self.got, 15, self.gather_sems[0])

        for out in self.outs:
            out.wait()


class SmallSum:
    def __init__(self, place, parts, slots, sems):
        self.parts, self.slots = parts, slots
        self.keep = pl.ds(place.core * 2, 3)
        self.away = pl.ds(2 - place.core * 2, 3)
        self.steps = []
        base = 0
        for g, targets in enumerate([[place.mate], place.z_mates, place.x_mates, place.y_mates, [place.mate]]):
            size = EMBED_TILES if g == 0 else 3
            pair = (sems.at[2 * g], sems.at[2 * g + 1])
            copies = []
            for n, t in enumerate(targets, base):
                copies.append(remote(parts.at[g, pl.ds(0, size)], slots.at[n, pl.ds(0, size)], pair, t))
            span = slots.at[pl.ds(base, len(targets)), pl.ds(0, size)]
            self.steps.append((base, len(targets), Exchange(copies, span, pair)))
            base += len(targets)

    def begin(self):
        self.steps[0][2].start()

    def pass_on(self, g):
        base, count, exchange = self.steps[g]
        exchange.arrive()
        here = self.keep if g == 0 else pl.ds(0, 3)
        total = self.parts[g, here].astype(F32)
        for n in range(count):
            total = total + self.slots[base + n, here].astype(F32)
        self.parts[g + 1, pl.ds(0, 3)] = total.astype(BF)
        self.steps[g + 1][2].start()

    def finish(self, out_ref, scale):
        base, _, exchange = self.steps[4]
        exchange.arrive()
        out_ref[self.away] = self.slots[base, pl.ds(0, 3)].astype(F32) * scale
        out_ref[self.keep] = self.parts[4, pl.ds(0, 3)].astype(F32) * scale
        for _, _, exchange in self.steps:
            exchange.sent()


def pack_block(coarse_ref, row_src_ref, row_frac_ref, col_src_ref, col_frac_ref, lines_ref, pack_ref):
    pack_ref[...] = jnp.zeros_like(pack_ref)
    pack_ref[pl.ds(0, CELLS), pl.ds(0, coarse_ref.shape[1])] = coarse_ref[...]
    lines_ref[...] = jnp.zeros_like(lines_ref)
    for row, src_ref, frac_ref in ((0, row_src_ref, row_frac_ref), (4, col_src_ref, col_frac_ref)):
        lanes = pl.ds(0, src_ref.shape[1])
        lines_ref[pl.ds(row, 1), lanes] = src_ref[...].astype(F32)
        left = frac_ref[...]
        for n in range(1, 4):
            term = left.astype(BF).astype(F32)
            lines_ref[pl.ds(row + n, 1), lanes] = term
            left = left - term
    pack_ref[pl.ds(CELLS, 16), :] = lines_ref[...].astype(BF)


def kernel(
    coarse_hbm, row_src_hbm, row_frac_hbm, col_src_hbm, col_frac_hbm, embed_hbm, conv1_hbm, conv2_hbm, cot_hbm,
    feat_out, gemb_out, g1_out, g2_out,
    feat_ref, gemb_ref, g1_ref, g2_ref, out_sem,
    coarse_ref, row_src_ref, row_frac_ref, col_src_ref, col_frac_ref, embed_in_ref, conv1_ref, conv2_ref, cot_ref,
    lines_ref, pack_ref, embed_ref,
    nb_ref, rowhalo_ref, colpack_ref, colhalo_ref, cells_ref, rowmix_ref, colmix_ref, down_ref,
    w1_ref, w2_ref, w1t_ref, w2t_ref, l3_ref, c3_ref, h3_ref, d3_ref, back_ref, slope_ref,
    part1, paired1, half1, got1, mine1, other1, final1, twin1,
    part2, paired2, half2, got2, mine2, other2, final2, twin2, eparts, eslots,
    load_sem, halo_sem, sum_sem,
):
    place = Place()
    lat, lon = place.lat, place.lon
    scale = 1.0 / math.sqrt(8 * ROWS * 16 * COLS)

    def apart(stage, *args):
        @pl.when(lat < 8)
        def _():
            stage(*args)

    barrier = pltpu.get_barrier_semaphore()
    partners = [place.mate] + place.around + place.z_mates + place.plane_mates
    for spot in partners:
        pl.semaphore_signal(barrier, inc=1, device_id=spot, device_id_type=MESH)

    pairs = [
        (coarse_hbm, coarse_ref), (row_src_hbm, row_src_ref), (row_frac_hbm, row_frac_ref),
        (col_src_hbm, col_src_ref), (col_frac_hbm, col_frac_ref), (cot_hbm, cot_ref),
        (conv2_hbm, conv2_ref), (conv1_hbm, conv1_ref), (embed_hbm, embed_in_ref),
    ]
    loads = [pltpu.make_async_copy(src, dst, load_sem.at[n]) for n, (src, dst) in enumerate(pairs)]
    for load in loads:
        load.start()

    packs, columns, rows, corners = [], [], [], []
    pairs = [(halo_sem.at[2 * n], halo_sem.at[2 * n + 1]) for n in range(4)]
    for n, (dy, dx) in enumerate(DIRS):
        slot = (1 - dy) * 3 + 1 - dx
        packs.append(remote(pack_ref, nb_ref.at[slot], pairs[0], place.around[n]))
        if dx == 0:
            src = cot_ref.at[pl.ds(0 if dy == -1 else ROWS - 2, 2)]
            rows.append(remote(src, rowhalo_ref.at[0 if dy == 1 else 1], pairs[2], place.around[n]))
        else:
            side = 0 if dx == -1 else 1
            src = colpack_ref.at[side, {-1: pl.ds(0, 1), 0: pl.ds(0, 4), 1: pl.ds(3, 1)}[dy]]
            dst = colhalo_ref.at[1 - side, {1: pl.ds(4, 1), 0: pl.ds(0, 4), -1: pl.ds(5, 1)}[dy]]
            if dy == 0:
                columns.append(remote(src, dst, pairs[1], place.around[n]))
            else:
                corners.append(remote(src, dst, pairs[3], place.around[n]))
    packs = Exchange(packs, nb_ref.at[pl.ds(0, 8)], pairs[0])
    columns = Exchange(columns, colhalo_ref.at[:, pl.ds(0, 4)], pairs[1])
    rows = Exchange(rows, rowhalo_ref, pairs[2])
    corners = Exchange(corners, colhalo_ref.at[:, pl.ds(4, 2)], pairs[3])
    sum1 = GradSum(place, part1, paired1, half1, got1, mine1, other1, final1, twin1, sum_sem.at[pl.ds(0, 10)])
    sum2 = GradSum(place, part2, paired2, half2, got2, mine2, other2, final2, twin2, sum_sem.at[pl.ds(10, 10)])
    small = SmallSum(place, eparts, eslots, sum_sem.at[pl.ds(20, 10)])

    for load in loads[0:5]:
        load.wait()
    pack_block(coarse_ref, row_src_ref, row_frac_ref, col_src_ref, col_frac_ref, lines_ref, pack_ref)
    pl.semaphore_wait(barrier, len(partners))
    packs.start()
    loads[5].wait()
    gather_columns(cot_ref, colpack_ref)
    columns.start()

    nb_ref[4] = pack_ref[...]
    for load in loads[6:9]:
        load.wait()
    spread_taps(conv2_ref, w2t_ref, True)
    spread_own(cot_ref, c3_ref)
    apart(back_inside, c3_ref, w2t_ref, back_ref)
    spread_taps(conv1_ref, w1_ref, False)
    spread_taps(conv2_ref, w2_ref, False)
    spread_taps(conv1_ref, w1t_ref, True)
    embed_ref[...] = jnp.zeros_like(embed_ref)
    embed_ref[pl.ds(0, embed_in_ref.shape[0]), :] = embed_in_ref[...]
    down_ref[...] = jnp.zeros_like(down_ref)

    packs.arrive()
    corners.start()
    rows.start()
    coarse_setup(lat, lon, nb_ref, cells_ref, rowmix_ref, colmix_ref)
    apart(lift_and_hide, lat, embed_ref, cells_ref, rowmix_ref, colmix_ref, w1_ref, l3_ref, h3_ref, slope_ref)
    columns.arrive()
    close_columns(cot_ref, colhalo_ref, c3_ref)
    apart(weight_grad, h3_ref, 0, c3_ref, 2, part2)
    sum2.step_pair()
    corners.arrive()
    rows.arrive()
    close_rows(lat, rowhalo_ref, colhalo_ref, c3_ref)
    apart(back_around, c3_ref, w2t_ref, back_ref)
    sum2.step_scatter()
    apart(delta_and_grad, back_ref, slope_ref, d3_ref, l3_ref, part1)
    sum1.step_pair()
    apart(back_to_embed, 0, 8, d3_ref, w1t_ref, cot_ref, rowmix_ref, colmix_ref, down_ref)
    sum1.step_scatter()
    apart(back_to_embed, 8, 8, d3_ref, w1t_ref, cot_ref, rowmix_ref, colmix_ref, down_ref)
    embed_grad(cells_ref, down_ref, eparts.at[0])
    small.begin()
    shift_hidden(h3_ref)
    done = [
        pltpu.make_async_copy(feat_ref.at[pl.ds(n * 16, 16)], feat_out.at[pl.ds(n * 16, 16)], out_sem.at[n])
        for n in range(2)
    ]
    small.pass_on(0)
    apart(features_of, 0, 8, h3_ref, l3_ref, w2_ref, feat_ref)
    done[0].start()
    sum2.step_column()
    apart(features_of, 8, 8, h3_ref, l3_ref, w2_ref, feat_ref)
    done[1].start()
    sum1.step_column()
    small.pass_on(1)
    sum2.step_gather()
    sum1.step_gather()
    small.pass_on(2)
    sum2.step_swap(g2_ref, g2_out, out_sem.at[pl.ds(2, 2)], scale)
    small.pass_on(3)
    sum1.step_swap(g1_ref, g1_out, out_sem.at[pl.ds(5, 2)], scale)
    sum2.finish(g2_ref, scale)
    small.finish(gemb_ref, scale)
    done.append(pltpu.make_async_copy(gemb_ref, gemb_out, out_sem.at[4]))
    done[2].start()
    sum1.finish(g1_ref, scale)
    for exchange in (packs, columns, rows, corners):
        exchange.sent()
    for copy in done:
        copy.wait()
    sum2.drain()
    sum1.drain()


def write_out(*refs):
    copies = [pltpu.make_async_copy(refs[n], refs[n + 4], refs[-1].at[n]) for n in range(4)]
    for copy in copies:
        copy.start()
    for copy in copies:
        copy.wait()


RESULTS = [
    ((ROWS, COLS, HID), BF),
    ((EMBED_TILES, 16, HID), F32),
    ((TILES, 16, HID), F32),
    ((TILES, 16, HID), F32),
]


def scratch_list(channels=73):
    dma = pltpu.SemaphoreType.DMA
    line = lambda n, kind: pltpu.VMEM((1, n), kind)
    tiles = lambda *n: pltpu.VMEM((*n, 16, HID), BF)
    grad = [
        tiles(TILES), tiles(HALF), tiles(HALF), tiles(15 * PIECE),
        tiles(PIECE), tiles(3, PIECE), tiles(HALF), tiles(HALF),
    ]
    return (
        [pltpu.VMEM(shape, kind) for shape, kind in RESULTS]
        + [dma((7,))]
        + [
            pltpu.VMEM((CELLS, channels), BF),
            line(ROWS, jnp.int32), line(ROWS, F32), line(COLS, jnp.int32), line(COLS, F32),
            pltpu.VMEM((channels, HID), BF),
            pltpu.VMEM((3, 3, HID, HID), BF),
            pltpu.VMEM((3, 3, HID, HID), BF),
            pltpu.VMEM((ROWS, COLS, HID), BF),
            pltpu.VMEM((16, HID), F32),
            pltpu.VMEM((PACK, HID), BF),
            pltpu.VMEM((HID, HID), BF),
            pltpu.VMEM((9, PACK, HID), BF),
            pltpu.VMEM((2, 2, COLS, HID), BF),
            tiles(2, 4),
            tiles(2, 6),
            pltpu.VMEM((12, 24, HID), F32),
            pltpu.VMEM((8, HID), F32),
            pltpu.VMEM((64, 2 * HID), BF),
            pltpu.VMEM((12, 32, HID), F32),
        ]
        + [pltpu.VMEM((12 * HID, 2 * HID), BF)] * 4
        + [pltpu.VMEM((18, 2, WIDE, 3 * HID), BF)] * 2
        + [pltpu.VMEM((17, 2, WIDE, 3 * HID), BF)] * 2
        + [pltpu.VMEM((17, WIDE, 2 * HID), F32)] * 2
        + grad
        + grad
        + [tiles(5, EMBED_TILES), tiles(11, EMBED_TILES)]
        + [dma((9,))]
        + [dma((8,)), dma((30,))]
    )


def on_device(coarse, row_src, row_frac, col_src, col_frac, embed_weight, conv1_weight, conv2_weight, cotangent):
    channels = coarse.shape[0]
    cells = jnp.transpose(coarse, (1, 2, 0)).reshape(CELLS, channels)
    lines = [v.reshape(1, -1) for v in (row_src, row_frac, col_src, col_frac)]
    results = pl.pallas_call(
        kernel,
        out_shape=[pltpu.VMEM(shape, kind) for shape, kind in RESULTS],
        in_specs=[pl.BlockSpec(memory_space=pl.ANY)] * 9,
        out_specs=[pl.BlockSpec(memory_space=pl.ANY)] * 4,
        scratch_shapes=scratch_list(channels),
        compiler_params=pltpu.CompilerParams(
            collective_id=0, has_side_effects=True, vmem_limit_bytes=56 * 2**20
        ),
    )(cells, *lines, embed_weight, conv1_weight, conv2_weight, cotangent)
    features, grad_embed, grad_conv1, grad_conv2 = pl.pallas_call(
        write_out,
        out_shape=[jax.ShapeDtypeStruct(shape, kind) for shape, kind in RESULTS],
        in_specs=[pl.BlockSpec(memory_space=pl.ANY)] * 4,
        out_specs=[pl.BlockSpec(memory_space=pl.ANY)] * 4,
        scratch_shapes=[pltpu.SemaphoreType.DMA((4,))],
    )(*[pltpu.with_memory_space_constraint(r, pltpu.VMEM) for r in results])
    taps = (3, 3, HID, HID)
    grad_embed = grad_embed.reshape(EMBED_TILES * 16, HID)[:channels]
    return (features, grad_embed, grad_conv1.reshape(taps), grad_conv2.reshape(taps))


def solution(mesh):
    in_specs = (
        P(None, "lat", "lon"),
        P("lat"),
        P("lat"),
        P("lon"),
        P("lon"),
        P(),
        P(),
        P(),
        P("lat", "lon", None),
    )
    out_specs = (P("lat", "lon", None), P(), P(), P())
    return jax.shard_map(
        on_device, mesh=mesh, in_specs=in_specs, out_specs=out_specs, check_vma=False
    )
```

```python
import functools
import math

import jax
import jax.numpy as jnp
from jax import lax
from jax.experimental import pallas as pl
from jax.experimental.pallas import tpu as pltpu
from jax.sharding import PartitionSpec as P

MESH = pl.DeviceIdType.MESH
BF = jnp.bfloat16
F32 = jnp.float32

ROWS = 32
COLS = 128
WIDE = 144
HID = 128
CROW = 4
CCOL = 8
CELLS = CROW * CCOL
PACK = 48
TILES = 72
HALF = 36
PIECE = 3
OWNERS = 12


def owner_rank(plane):
    x, y = plane // 4, lax.rem(plane, 4)
    return x != y, jnp.minimum(x * 3 + y - (y > x).astype(jnp.int32), OWNERS - 1)

EMBED_TILES = 5
DIRS = [(dy, dx) for dy in (-1, 0, 1) for dx in (-1, 0, 1) if (dy, dx) != (0, 0)]


def dot(a, b):
    return jnp.dot(a, b, preferred_element_type=F32)


def dot_t(a, b):
    return lax.dot_general(a, b, (((0,), (0,)), ((), ())), preferred_element_type=F32)


def halves(x):
    hi = x.astype(BF)
    return hi, (x - hi.astype(F32)).astype(BF)


def spread_taps(w_ref, out_ref, back):
    zero = jnp.zeros((HID, HID), BF)
    for b in range(3):
        for a in range(3):
            block = w_ref[2 - a, 2 - b].T if back else w_ref[a, b]
            for s in range(2):
                k = a + s
                out_ref[pl.ds((k * 3 + b) * HID, HID), pl.ds(s * HID, HID)] = block
        out_ref[pl.ds(b * HID, HID), pl.ds(HID, HID)] = zero
        out_ref[pl.ds((9 + b) * HID, HID), pl.ds(0, HID)] = zero


def store_shifted(ref, pair, side, x):
    axis = x.ndim - 2
    ref[pair, side, :, pl.ds(HID, HID)] = x.astype(BF)
    ref[pair, side, :, pl.ds(0, HID)] = pltpu.roll(x, 1, axis).astype(BF)
    ref[pair, side, :, pl.ds(2 * HID, HID)] = pltpu.roll(x, WIDE - 1, axis).astype(BF)


def four_rows(ref, first, count, width, start=0):
    rows = [
        ref[pl.ds(first + k // 2, count), k % 2, pl.ds(start, width), :].reshape(count * width, 3 * HID)
        for k in range(4)
    ]
    return jnp.concatenate(rows, axis=-1)


def coarse_setup(lat, lon, nb_ref, cells_ref, rowmix_ref, colmix_ref):
    for block in range(9):
        dy, dx = block // 3, block % 3
        cells_ref[pl.ds(dy * CROW, CROW), pl.ds(dx * CCOL, CCOL), :] = (
            nb_ref[block, pl.ds(0, CELLS), :].astype(F32).reshape(CROW, CCOL, HID)
        )

    def line(block):
        return nb_ref[block, pl.ds(CELLS, 16), :].astype(F32)

    lane = lax.broadcasted_iota(jnp.int32, (16, HID), 1)
    rows = jnp.where(
        lane < 2,
        pltpu.roll(line(1), 98, 1),
        jnp.where(lane < 34, pltpu.roll(line(4), 2, 1), pltpu.roll(line(7), 34, 1)),
    )
    lane = lane[0:1]
    frac = rows[1:2] + rows[2:3] + rows[3:4]
    start = ((lane + 30) // 8 - 1).astype(F32)
    place = rows[0:1] - (lat * CROW - CROW).astype(F32) - start
    fine_row = lat * ROWS + lane - 2
    inside = ((fine_row >= 0) & (fine_row < 8 * ROWS)).astype(F32)
    for m in range(4):
        weight = jnp.where(place == float(m), 1.0 - frac, 0.0) + jnp.where(
            place == float(m - 1), frac, 0.0
        )
        rowmix_ref[pl.ds(m, 1), :] = weight * inside

    lane = lax.broadcasted_iota(jnp.int32, (16, HID), 1)
    edge = jnp.where(lane < 8, line(5), pltpu.roll(line(3), 16, 1))
    tables = []
    for part in (line(4), edge):
        frac = part[5:6] + part[6:7] + part[7:8]
        spot = part[4:5] - (lon * CCOL - CCOL).astype(F32)
        spot = jnp.where(spot < 0.0, spot + 128.0, spot)
        spot = jnp.where(spot >= 128.0, spot - 128.0, spot)
        cell = lax.broadcasted_iota(jnp.int32, (32, HID), 0).astype(F32)
        tables.append(
            jnp.where(cell == spot, 1.0 - frac, 0.0) + jnp.where(cell == spot + 1.0, frac, 0.0)
        )
    hi, lo = halves(jnp.concatenate(tables, axis=-1))
    colmix_ref[pl.ds(0, 32), :] = hi
    colmix_ref[pl.ds(32, 32), :] = lo


def spread_own(cot_ref, c3_ref):
    def step(q, carry):
        for t in range(2):
            x = cot_ref[2 * q + t].astype(F32)
            own = pl.ds(0, COLS)
            c3_ref[q + 1, t, own, pl.ds(HID, HID)] = cot_ref[2 * q + t]
            c3_ref[q + 1, t, own, pl.ds(0, HID)] = pltpu.roll(x, 1, 0).astype(BF)
            c3_ref[q + 1, t, own, pl.ds(2 * HID, HID)] = pltpu.roll(x, COLS - 1, 0).astype(BF)
        return carry

    lax.fori_loop(0, ROWS // 2, step, 0)


def gather_columns(cot_ref, colpack_ref):
    spot = lax.broadcasted_iota(jnp.int32, (16, HID), 0) // 2
    for side, start in ((0, 0), (1, COLS - 16)):
        for g in range(ROWS // 8):
            total = None
            for n in range(8):
                x = cot_ref[8 * g + n, pl.ds(start, 16)].astype(F32)
                shift = (2 * n + 2 * side) % 16
                x = pltpu.roll(x, shift, 0) if shift else x
                total = x if n == 0 else jnp.where(spot == n, x, total)
            colpack_ref[side, g] = total.astype(BF)


def beside(colhalo_ref, tile, n):
    near = lax.broadcasted_iota(jnp.int32, (16, HID), 0) < 8
    right = colhalo_ref[1, tile].astype(F32)
    left = colhalo_ref[0, tile].astype(F32)
    right = pltpu.roll(right, 16 - 2 * n, 0) if n else right
    left = pltpu.roll(left, 14 - 2 * n, 0) if n < 7 else left
    return jnp.where(near, right, left)


def close_columns(cot_ref, colhalo_ref, c3_ref):
    def step(g, carry):
        for n in range(8):
            r = 8 * g + n
            last = cot_ref[r, pl.ds(COLS - 16, 16)].astype(F32)
            first = cot_ref[r, pl.ds(0, 16)].astype(F32)
            x = jnp.concatenate([last, beside(colhalo_ref, g, n), first], axis=0)
            west = pltpu.roll(x, 1, 0).astype(BF)
            east = pltpu.roll(x, 47, 0).astype(BF)
            wide = pl.ds(COLS, 16)
            q, t = 4 * g + n // 2 + 1, n % 2
            c3_ref[q, t, wide, pl.ds(HID, HID)] = x[16:32].astype(BF)
            c3_ref[q, t, wide, pl.ds(0, HID)] = west[16:32]
            c3_ref[q, t, pl.ds(0, 16), pl.ds(0, HID)] = west[32:48]
            c3_ref[q, t, pl.ds(COLS - 16, 32), pl.ds(2 * HID, HID)] = east[0:32]
        return carry

    lax.fori_loop(0, ROWS // 8, step, 0)


def close_rows(lat, rowhalo_ref, colhalo_ref, c3_ref):
    top = (lat > 0).astype(F32)
    bottom = (lat < 7).astype(F32)
    for t in range(2):
        x = jnp.concatenate([rowhalo_ref[0, t].astype(F32), beside(colhalo_ref, 4, 6 + t)], axis=0)
        store_shifted(c3_ref, 0, t, x * top)
        x = jnp.concatenate([rowhalo_ref[1, t].astype(F32), beside(colhalo_ref, 5, t)], axis=0)
        store_shifted(c3_ref, 17, t, x * bottom)


def back_inside(c3_ref, w2t_ref, back_ref):
    y = dot(four_rows(c3_ref, 1, 15, 96, 16), w2t_ref[...])
    back_ref[pl.ds(1, 15), pl.ds(16, 96), :] = y.reshape(15, 96, 2 * HID)


def back_beside(c3_ref, w2t_ref, back_ref):
    parts = [four_rows(c3_ref, 1, 15, 16, 0), four_rows(c3_ref, 1, 15, 32, COLS - 16)]
    y = dot(jnp.concatenate(parts, axis=0), w2t_ref[...])
    back_ref[pl.ds(1, 15), pl.ds(0, 16), :] = y[0:240].reshape(15, 16, 2 * HID)
    back_ref[pl.ds(1, 15), pl.ds(COLS - 16, 32), :] = y[240:720].reshape(15, 32, 2 * HID)


def back_ends(c3_ref, w2t_ref, back_ref):
    parts = [four_rows(c3_ref, 0, 1, WIDE), four_rows(c3_ref, 16, 1, WIDE)]
    y = dot(jnp.concatenate(parts, axis=0), w2t_ref[...])
    back_ref[0] = y[0:WIDE]
    back_ref[16] = y[WIDE : 2 * WIDE]


def lift_and_hide(lat, embed_ref, cells_ref, rowmix_ref, colmix_ref, w1_ref, l3_ref, h3_ref, slope_ref):
    hi, lo = colmix_ref[pl.ds(0, 32), :], colmix_ref[pl.ds(32, 32), :]
    mixer = jnp.concatenate([hi, lo, hi], axis=0).T[0:WIDE]
    mix = rowmix_ref[...]
    step = 6

    def lift(start):
        rows = []
        for i in range(start, start + step):
            first = (i + 30) // 8 - 1
            total = None
            for m in range(4):
                term = mix[m : m + 1, i : i + 1] * cells_ref[first + m]
                total = term if total is None else total + term
            rows.append(total)
        wide = jnp.concatenate(rows, axis=-1)
        wide = jnp.concatenate([wide, jnp.zeros((8, step * HID), F32)], axis=0)
        hi, lo = halves(wide)
        fine = dot(mixer, jnp.concatenate([hi, hi, lo], axis=0)).astype(BF)
        fine = jnp.concatenate([fine[:, n * HID : (n + 1) * HID] for n in range(step)], axis=0)
        lifted = dot(fine, embed_ref[...])
        for n in range(step):
            i = start + n
            store_shifted(l3_ref, i // 2, i % 2, lifted[n * WIDE : (n + 1) * WIDE])

    def finish(pre_all, first, count):
        for p in range(count):
            for s in range(2):
                pre = pre_all[p * WIDE : (p + 1) * WIDE, s * HID : (s + 1) * HID]
                sig = 0.5 + 0.5 * jnp.tanh(0.5 * pre)
                hidden = pre * sig
                slope = sig + hidden * (1.0 - sig)
                if first + p == 0 and s == 0:
                    inside = (lat > 0).astype(F32)
                    hidden, slope = hidden * inside, slope * inside
                if first + p == 16 and s == 1:
                    inside = (lat < 7).astype(F32)
                    hidden, slope = hidden * inside, slope * inside
                h3_ref[first + p, s, :, pl.ds(HID, HID)] = hidden.astype(BF)
                slope_ref[first + p, :, pl.ds(s * HID, HID)] = slope

    waiting = None
    lift(0)
    lift(step)
    for first in range(0, 17, 3):
        count = min(3, 17 - first)
        pre_all = dot(four_rows(l3_ref, first, count, WIDE), w1_ref[...])
        if 2 * first + 2 * step < ROWS + 4:
            lift(2 * first + 2 * step)
        if waiting is not None:
            finish(*waiting)
        waiting = (pre_all, first, count)
    finish(*waiting)


def shift_hidden(h3_ref):
    def step(p, carry):
        for s in range(2):
            x = h3_ref[p, s, :, pl.ds(HID, HID)].astype(F32)
            h3_ref[p, s, :, pl.ds(0, HID)] = pltpu.roll(x, 1, 0).astype(BF)
            h3_ref[p, s, :, pl.ds(2 * HID, HID)] = pltpu.roll(x, WIDE - 1, 0).astype(BF)
        return carry

    lax.fori_loop(0, 17, step, 0)


def make_delta(back_ref, slope_ref, d3_ref, first, count):
    for p in range(first, first + count):
        for s in range(2):
            lanes = pl.ds(s * HID, HID)
            store_shifted(d3_ref, p, s, back_ref[p, :, lanes] * slope_ref[p, :, lanes])


def rows_from(ref, start, lanes, count=ROWS):
    q, odd, half = start // 2, start % 2, count // 2
    if odd == 0:
        return ref[pl.ds(q, half), :, pl.ds(0, COLS), lanes].reshape(count * COLS, -1)
    parts = [
        ref[pl.ds(q, half), 1, pl.ds(0, COLS), lanes],
        ref[pl.ds(q + 1, half), 0, pl.ds(0, COLS), lanes],
    ]
    return jnp.stack(parts, axis=1).reshape(count * COLS, -1)


def tap_products(v_ref, u_ref, runs):
    left, right = [[], [], []], []
    left_two, right_two = [[], [], [], []], [[], []]
    for v_start, u_start, count in runs:
        turned = []
        for n in range(v_start, v_start + count + 2):
            turned.append(v_ref[n // 2, n % 2, pl.ds(0, COLS), pl.ds(HID, HID)].T)
        for a in range(3):
            left[a] += turned[a : a + count]
        for a in range(4):
            left_two[a] += turned[a : a + count : 2]
        right.append(rows_from(u_ref, u_start, pl.ds(0, 2 * HID), count))
        for s in range(2):
            n = u_start + s
            rows = u_ref[pl.ds(n // 2, count // 2), n % 2, pl.ds(0, COLS), pl.ds(2 * HID, HID)]
            right_two[s].append(rows.reshape(count // 2 * COLS, HID))

    def stack(lines):
        return jnp.concatenate([jnp.concatenate(line, axis=1) for line in lines], axis=0)

    wide = dot(stack(left), jnp.concatenate(right, axis=0))
    last = dot(stack(left_two), jnp.concatenate([jnp.concatenate(x, axis=0) for x in right_two], axis=-1))
    blocks = []
    for a in range(3):
        line = wide[a * HID : (a + 1) * HID]
        third = last[a * HID : (a + 1) * HID, 0:HID] + last[(a + 1) * HID : (a + 2) * HID, HID : 2 * HID]
        blocks.append([line[:, 0:HID], line[:, HID : 2 * HID], third])
    return blocks


def store_taps(blocks, out_ref):
    for a in range(3):
        for b in range(3):
            out_ref[pl.ds((a * 3 + b) * 8, 8)] = blocks[a][2 - b].reshape(8, 16, HID).astype(BF)


def weight_grad(v_ref, v_start, u_ref, u_start, out_ref):
    store_taps(tap_products(v_ref, u_ref, [(v_start, u_start, ROWS)]), out_ref)


def delta_inside(back_ref, slope_ref, d3_ref, l3_ref, held_ref):
    make_delta(back_ref, slope_ref, d3_ref, 1, 9)
    blocks = tap_products(l3_ref, d3_ref, [(3, 3, 16)])
    make_delta(back_ref, slope_ref, d3_ref, 10, 6)
    for a in range(3):
        for n in range(3):
            held_ref[a, n] = blocks[a][n]


def delta_ends(back_ref, slope_ref, d3_ref, l3_ref, held_ref, out_ref):
    make_delta(back_ref, slope_ref, d3_ref, 0, 1)
    make_delta(back_ref, slope_ref, d3_ref, 16, 1)
    blocks = tap_products(l3_ref, d3_ref, [(1, 1, 2), (19, 19, 14)])
    store_taps([[blocks[a][n] + held_ref[a, n] for n in range(3)] for a in range(3)], out_ref)


def back_to_embed(first, count, d3_ref, w1t_ref, cot_ref, rowmix_ref, colmix_ref, down_ref):
    y = dot(four_rows(d3_ref, first, count, COLS), w1t_ref[...])
    rows = []
    for p in range(count):
        for s in range(2):
            part = y[p * COLS : (p + 1) * COLS, s * HID : (s + 1) * HID]
            rows.append((cot_ref[2 * (first + p) + s].astype(F32) + part).astype(BF))
    low = dot(colmix_ref[:, pl.ds(0, COLS)], jnp.concatenate(rows, axis=-1))
    low = low[0:32] + low[32:64]
    mix = rowmix_ref[...]
    sums = {}
    for n in range(2 * count):
        i = 2 * first + n + 2
        base = (i + 30) // 8 - 1
        part = low[:, n * HID : (n + 1) * HID]
        for m in range(4):
            term = mix[m : m + 1, i : i + 1] * part
            sums[base + m] = term if base + m not in sums else sums[base + m] + term
    for j, value in sums.items():
        down_ref[j] = down_ref[j] + value


def embed_grad(cells_ref, down_ref, out_ref):
    window = cells_ref[...].reshape(12 * 24, HID).astype(BF)
    down = jnp.concatenate([down_ref[j, pl.ds(0, 24), :] for j in range(12)], axis=0)
    hi, lo = halves(down)
    grad = dot_t(window, hi) + dot_t(window, lo)
    out_ref[...] = grad[0 : EMBED_TILES * 16].reshape(EMBED_TILES, 16, HID).astype(BF)


def features_of(first, count, h3_ref, l3_ref, w2_ref, feat_ref):
    y = dot(four_rows(h3_ref, first, count, COLS), w2_ref[...])
    for p in range(count):
        for s in range(2):
            part = y[p * COLS : (p + 1) * COLS, s * HID : (s + 1) * HID]
            own = l3_ref[first + p + 1, s, pl.ds(0, COLS), pl.ds(HID, HID)].astype(F32)
            feat_ref[2 * (first + p) + s] = (own + part).astype(BF)


class Place:
    def __init__(self):
        self.lat = lax.axis_index("lat")
        self.lon = lax.axis_index("lon")
        self.core = lax.rem(self.lon, 2)
        self.z = lax.rem(self.lat, 2) * 2 + lax.rem(self.lon // 2, 2)
        self.plane = self.lon // 4 * 4 + self.lat // 2
        self.mate = (self.lat, self.lon + 1 - 2 * self.core)
        self.planes = [lax.rem(self.plane + d, 16) for d in range(1, 16)]
        self.plane_mates = [self.spot(q, self.z) for q in self.planes]
        x, y = self.plane // 4, lax.rem(self.plane, 4)
        self.x_mates = [self.spot(lax.rem(x + d, 4) * 4 + y, self.z) for d in range(1, 4)]
        self.y_mates = [self.spot(x * 4 + lax.rem(y + d, 4), self.z) for d in range(1, 4)]
        self.z_mates = [self.spot(self.plane, lax.rem(self.z + d, 4)) for d in range(1, 4)]
        self.around = [(lax.rem(self.lat + dy + 8, 8), lax.rem(self.lon + dx + 16, 16)) for dy, dx in DIRS]

    def spot(self, plane, z):
        return (lax.rem(plane, 4) * 2 + z // 2, plane // 4 * 4 + lax.rem(z, 2) * 2 + self.core)


class Exchange:
    def __init__(self, copies, span, sems):
        self.copies = copies
        self.whole = [pltpu.make_async_copy(span, span, sem) for sem in sems]

    def start(self):
        for c in self.copies:
            c.start()

    def arrive(self):
        self.whole[1].wait()

    def sent(self):
        self.whole[0].wait()


def remote(src, dst, sems, target):
    return pltpu.make_async_remote_copy(
        src_ref=src, dst_ref=dst, send_sem=sems[0], recv_sem=sems[1], device_id=target, device_id_type=MESH
    )


class GradSum:
    def __init__(self, place, part, paired, half, got, mine, other, final, twin, sems):
        self.part, self.paired, self.half, self.got = part, paired, half, got
        self.mine, self.other, self.final, self.twin = mine, other, final, twin
        pairs = [(sems.at[2 * n], sems.at[2 * n + 1]) for n in range(5)]
        self.place = place
        self.owner, rank = owner_rank(place.plane)
        self.keep = place.core * HALF
        self.own = pl.ds(rank * PIECE, PIECE)
        away = part.at[pl.ds(HALF - self.keep, HALF)]
        self.pair = Exchange([remote(away, paired, pairs[0], place.mate)], paired, pairs[0])
        self.scatter_sems, self.gather_sems = pairs[1], pairs[3]
        self.column = Exchange(
            [remote(mine, other.at[n], pairs[2], t) for n, t in enumerate(place.z_mates)], other, pairs[2]
        )
        self.swap = Exchange([remote(final, twin, pairs[4], place.mate)], twin, pairs[4])

    def take(self, ref, count, sem):
        span = ref.at[pl.ds(0, count * PIECE)]
        pltpu.make_async_copy(span, span, sem).wait()

    def take_others(self, ref, sem):
        @pl.when(self.owner)
        def _():
            self.take(ref, OWNERS - 1, sem)

        @pl.when(jnp.logical_not(self.owner))
        def _():
            self.take(ref, OWNERS, sem)

    def step_pair(self):
        self.pair.start()

    def step_scatter(self):
        self.pair.arrive()
        total = self.part[pl.ds(self.keep, HALF)].astype(F32) + self.paired[...].astype(F32)
        self.half[...] = total.astype(BF)
        for n, (q, t) in enumerate(zip(self.place.planes, self.place.plane_mates)):
            owner, rank = owner_rank(q)

            @pl.when(owner)
            def _():
                piece = self.half.at[pl.ds(rank * PIECE, PIECE)]
                remote(piece, self.got.at[pl.ds(n * PIECE, PIECE)], self.scatter_sems, t).start()

    def step_column(self):
        @pl.when(self.owner)
        def _():
            self.take(self.got, 15, self.scatter_sems[1])
            total = self.half[self.own].astype(F32)
            for n in range(15):
                total = total + self.got[pl.ds(n * PIECE, PIECE)].astype(F32)
            self.mine[...] = total.astype(BF)
            self.column.start()

    def step_gather(self):
        @pl.when(self.owner)
        def _():
            self.column.arrive()
            total = self.mine[...].astype(F32)
            for n in range(3):
                total = total + self.other[n].astype(F32)
            self.final[self.own] = total.astype(BF)
            for t in self.place.plane_mates:
                remote(self.final.at[self.own], self.final.at[self.own], self.gather_sems, t).start()

    def step_swap(self, full_ref, out_ref, sem, scale):
        self.take_others(self.final, self.gather_sems[1])
        self.swap.start()
        self.outs = [
            pltpu.make_async_copy(full_ref.at[part], out_ref.at[part], sem.at[n])
            for n, part in enumerate((pl.ds(self.keep, HALF), pl.ds(HALF - self.keep, HALF)))
        ]
        full_ref[pl.ds(self.keep, HALF)] = self.final[...].astype(F32) * scale
        self.outs[0].start()

    def finish(self, full_ref, scale):
        self.swap.arrive()
        full_ref[pl.ds(HALF - self.keep, HALF)] = self.twin[...].astype(F32) * scale
        self.outs[1].start()

    def drain(self):
        self.pair.sent()
        self.swap.sent()
        self.take_others(self.half, self.scatter_sems[0])

        @pl.when(self.owner)
        def _():
            self.column.sent()
            self.take(self.got, 15, self.gather_sems[0])

        for out in self.outs:
            out.wait()


class SmallSum:
    def __init__(self, place, parts, slots, sems):
        self.parts, self.slots = parts, slots
        self.keep = pl.ds(place.core * 2, 3)
        self.away = pl.ds(2 - place.core * 2, 3)
        self.steps = []
        base = 0
        for g, targets in enumerate([[place.mate], place.z_mates, place.x_mates, place.y_mates, [place.mate]]):
            size = EMBED_TILES if g == 0 else 3
            pair = (sems.at[2 * g], sems.at[2 * g + 1])
            copies = []
            for n, t in enumerate(targets, base):
                copies.append(remote(parts.at[g, pl.ds(0, size)], slots.at[n, pl.ds(0, size)], pair, t))
            span = slots.at[pl.ds(base, len(targets)), pl.ds(0, size)]
            self.steps.append((base, len(targets), Exchange(copies, span, pair)))
            base += len(targets)

    def begin(self):
        self.steps[0][2].start()

    def pass_on(self, g):
        base, count, exchange = self.steps[g]
        exchange.arrive()
        here = self.keep if g == 0 else pl.ds(0, 3)
        total = self.parts[g, here].astype(F32)
        for n in range(count):
            total = total + self.slots[base + n, here].astype(F32)
        self.parts[g + 1, pl.ds(0, 3)] = total.astype(BF)
        self.steps[g + 1][2].start()

    def finish(self, out_ref, scale):
        base, _, exchange = self.steps[4]
        exchange.arrive()
        out_ref[self.away] = self.slots[base, pl.ds(0, 3)].astype(F32) * scale
        out_ref[self.keep] = self.parts[4, pl.ds(0, 3)].astype(F32) * scale
        for _, _, exchange in self.steps:
            exchange.sent()


def pack_block(coarse_ref, row_src_ref, row_frac_ref, col_src_ref, col_frac_ref, lines_ref, pack_ref):
    pack_ref[...] = jnp.zeros_like(pack_ref)
    pack_ref[pl.ds(0, CELLS), pl.ds(0, coarse_ref.shape[1])] = coarse_ref[...]
    lines_ref[...] = jnp.zeros_like(lines_ref)
    for row, src_ref, frac_ref in ((0, row_src_ref, row_frac_ref), (4, col_src_ref, col_frac_ref)):
        lanes = pl.ds(0, src_ref.shape[1])
        lines_ref[pl.ds(row, 1), lanes] = src_ref[...].astype(F32)
        left = frac_ref[...]
        for n in range(1, 4):
            term = left.astype(BF).astype(F32)
            lines_ref[pl.ds(row + n, 1), lanes] = term
            left = left - term
    pack_ref[pl.ds(CELLS, 16), :] = lines_ref[...].astype(BF)


def kernel(
    coarse_hbm, row_src_hbm, row_frac_hbm, col_src_hbm, col_frac_hbm, embed_hbm, conv1_hbm, conv2_hbm, cot_hbm,
    feat_out, gemb_out, g1_out, g2_out,
    feat_ref, gemb_ref, g1_ref, g2_ref, out_sem,
    coarse_ref, row_src_ref, row_frac_ref, col_src_ref, col_frac_ref, embed_in_ref, conv1_ref, conv2_ref, cot_ref,
    lines_ref, pack_ref, embed_ref,
    nb_ref, rowhalo_ref, colpack_ref, colhalo_ref, cells_ref, rowmix_ref, colmix_ref, down_ref,
    w1_ref, w2_ref, w1t_ref, w2t_ref, l3_ref, c3_ref, h3_ref, d3_ref, back_ref, slope_ref, held_ref,
    part1, paired1, half1, got1, mine1, other1, final1, twin1,
    part2, paired2, half2, got2, mine2, other2, final2, twin2, eparts, eslots,
    load_sem, halo_sem, sum_sem,
):
    place = Place()
    lat, lon = place.lat, place.lon
    scale = 1.0 / math.sqrt(8 * ROWS * 16 * COLS)

    def apart(stage, *args):
        @pl.when(lat < 8)
        def _():
            stage(*args)

    barrier = pltpu.get_barrier_semaphore()
    partners = [place.mate] + place.around + place.z_mates + place.plane_mates
    for spot in partners:
        pl.semaphore_signal(barrier, inc=1, device_id=spot, device_id_type=MESH)

    pairs = [
        (coarse_hbm, coarse_ref), (row_src_hbm, row_src_ref), (row_frac_hbm, row_frac_ref),
        (col_src_hbm, col_src_ref), (col_frac_hbm, col_frac_ref), (cot_hbm, cot_ref),
        (conv2_hbm, conv2_ref), (conv1_hbm, conv1_ref), (embed_hbm, embed_in_ref),
    ]
    loads = [pltpu.make_async_copy(src, dst, load_sem.at[n]) for n, (src, dst) in enumerate(pairs)]
    for load in loads:
        load.start()

    packs, columns, rows, corners = [], [], [], []
    pairs = [(halo_sem.at[2 * n], halo_sem.at[2 * n + 1]) for n in range(4)]
    for n, (dy, dx) in enumerate(DIRS):
        slot = (1 - dy) * 3 + 1 - dx
        packs.append(remote(pack_ref, nb_ref.at[slot], pairs[0], place.around[n]))
        if dx == 0:
            src = cot_ref.at[pl.ds(0 if dy == -1 else ROWS - 2, 2)]
            rows.append(remote(src, rowhalo_ref.at[0 if dy == 1 else 1], pairs[2], place.around[n]))
        else:
            side = 0 if dx == -1 else 1
            src = colpack_ref.at[side, {-1: pl.ds(0, 1), 0: pl.ds(0, 4), 1: pl.ds(3, 1)}[dy]]
            dst = colhalo_ref.at[1 - side, {1: pl.ds(4, 1), 0: pl.ds(0, 4), -1: pl.ds(5, 1)}[dy]]
            if dy == 0:
                columns.append(remote(src, dst, pairs[1], place.around[n]))
            else:
                corners.append(remote(src, dst, pairs[3], place.around[n]))
    packs = Exchange(packs, nb_ref.at[pl.ds(0, 8)], pairs[0])
    columns = Exchange(columns, colhalo_ref.at[:, pl.ds(0, 4)], pairs[1])
    rows = Exchange(rows, rowhalo_ref, pairs[2])
    corners = Exchange(corners, colhalo_ref.at[:, pl.ds(4, 2)], pairs[3])
    sum1 = GradSum(place, part1, paired1, half1, got1, mine1, other1, final1, twin1, sum_sem.at[pl.ds(0, 10)])
    sum2 = GradSum(place, part2, paired2, half2, got2, mine2, other2, final2, twin2, sum_sem.at[pl.ds(10, 10)])
    small = SmallSum(place, eparts, eslots, sum_sem.at[pl.ds(20, 10)])

    for load in loads[0:5]:
        load.wait()
    pack_block(coarse_ref, row_src_ref, row_frac_ref, col_src_ref, col_frac_ref, lines_ref, pack_ref)
    pl.semaphore_wait(barrier, len(partners))
    packs.start()
    loads[5].wait()
    gather_columns(cot_ref, colpack_ref)
    columns.start()

    nb_ref[4] = pack_ref[...]
    for load in loads[6:9]:
        load.wait()
    spread_taps(conv2_ref, w2t_ref, True)
    spread_own(cot_ref, c3_ref)
    apart(back_inside, c3_ref, w2t_ref, back_ref)
    spread_taps(conv1_ref, w1_ref, False)
    spread_taps(conv2_ref, w2_ref, False)
    spread_taps(conv1_ref, w1t_ref, True)
    embed_ref[...] = jnp.zeros_like(embed_ref)
    embed_ref[pl.ds(0, embed_in_ref.shape[0]), :] = embed_in_ref[...]
    down_ref[...] = jnp.zeros_like(down_ref)

    columns.arrive()
    close_columns(cot_ref, colhalo_ref, c3_ref)
    apart(back_beside, c3_ref, w2t_ref, back_ref)
    packs.arrive()
    corners.start()
    rows.start()
    coarse_setup(lat, lon, nb_ref, cells_ref, rowmix_ref, colmix_ref)
    apart(lift_and_hide, lat, embed_ref, cells_ref, rowmix_ref, colmix_ref, w1_ref, l3_ref, h3_ref, slope_ref)
    apart(weight_grad, h3_ref, 0, c3_ref, 2, part2)
    sum2.step_pair()
    apart(delta_inside, back_ref, slope_ref, d3_ref, l3_ref, held_ref)
    sum2.step_scatter()
    corners.arrive()
    rows.arrive()
    close_rows(lat, rowhalo_ref, colhalo_ref, c3_ref)
    apart(back_ends, c3_ref, w2t_ref, back_ref)
    apart(delta_ends, back_ref, slope_ref, d3_ref, l3_ref, held_ref, part1)
    sum1.step_pair()
    apart(back_to_embed, 0, 8, d3_ref, w1t_ref, cot_ref, rowmix_ref, colmix_ref, down_ref)
    sum1.step_scatter()
    apart(back_to_embed, 8, 8, d3_ref, w1t_ref, cot_ref, rowmix_ref, colmix_ref, down_ref)
    embed_grad(cells_ref, down_ref, eparts.at[0])
    small.begin()
    shift_hidden(h3_ref)
    done = [
        pltpu.make_async_copy(feat_ref.at[pl.ds(n * 16, 16)], feat_out.at[pl.ds(n * 16, 16)], out_sem.at[n])
        for n in range(2)
    ]
    small.pass_on(0)
    apart(features_of, 0, 8, h3_ref, l3_ref, w2_ref, feat_ref)
    done[0].start()
    sum2.step_column()
    apart(features_of, 8, 8, h3_ref, l3_ref, w2_ref, feat_ref)
    done[1].start()
    sum1.step_column()
    small.pass_on(1)
    sum2.step_gather()
    sum1.step_gather()
    small.pass_on(2)
    sum2.step_swap(g2_ref, g2_out, out_sem.at[pl.ds(2, 2)], scale)
    small.pass_on(3)
    sum1.step_swap(g1_ref, g1_out, out_sem.at[pl.ds(5, 2)], scale)
    sum2.finish(g2_ref, scale)
    small.finish(gemb_ref, scale)
    done.append(pltpu.make_async_copy(gemb_ref, gemb_out, out_sem.at[4]))
    done[2].start()
    sum1.finish(g1_ref, scale)
    for exchange in (packs, columns, rows, corners):
        exchange.sent()
    for copy in done:
        copy.wait()
    sum2.drain()
    sum1.drain()


def write_out(*refs):
    copies = [pltpu.make_async_copy(refs[n], refs[n + 4], refs[-1].at[n]) for n in range(4)]
    for copy in copies:
        copy.start()
    for copy in copies:
        copy.wait()


RESULTS = [
    ((ROWS, COLS, HID), BF),
    ((EMBED_TILES, 16, HID), F32),
    ((TILES, 16, HID), F32),
    ((TILES, 16, HID), F32),
]


def scratch_list(channels=73):
    dma = pltpu.SemaphoreType.DMA
    line = lambda n, kind: pltpu.VMEM((1, n), kind)
    tiles = lambda *n: pltpu.VMEM((*n, 16, HID), BF)
    grad = [
        tiles(TILES), tiles(HALF), tiles(HALF), tiles(15 * PIECE),
        tiles(PIECE), tiles(3, PIECE), tiles(HALF), tiles(HALF),
    ]
    return (
        [pltpu.VMEM(shape, kind) for shape, kind in RESULTS]
        + [dma((7,))]
        + [
            pltpu.VMEM((CELLS, channels), BF),
            line(ROWS, jnp.int32), line(ROWS, F32), line(COLS, jnp.int32), line(COLS, F32),
            pltpu.VMEM((channels, HID), BF),
            pltpu.VMEM((3, 3, HID, HID), BF),
            pltpu.VMEM((3, 3, HID, HID), BF),
            pltpu.VMEM((ROWS, COLS, HID), BF),
            pltpu.VMEM((16, HID), F32),
            pltpu.VMEM((PACK, HID), BF),
            pltpu.VMEM((HID, HID), BF),
            pltpu.VMEM((9, PACK, HID), BF),
            pltpu.VMEM((2, 2, COLS, HID), BF),
            tiles(2, 4),
            tiles(2, 6),
            pltpu.VMEM((12, 24, HID), F32),
            pltpu.VMEM((8, HID), F32),
            pltpu.VMEM((64, 2 * HID), BF),
            pltpu.VMEM((12, 32, HID), F32),
        ]
        + [pltpu.VMEM((12 * HID, 2 * HID), BF)] * 4
        + [pltpu.VMEM((18, 2, WIDE, 3 * HID), BF)] * 2
        + [pltpu.VMEM((17, 2, WIDE, 3 * HID), BF)] * 2
        + [pltpu.VMEM((17, WIDE, 2 * HID), F32)] * 2
        + [pltpu.VMEM((3, 3, HID, HID), F32)]
        + grad
        + grad
        + [tiles(5, EMBED_TILES), tiles(11, EMBED_TILES)]
        + [dma((9,))]
        + [dma((8,)), dma((30,))]
    )


def on_device(coarse, row_src, row_frac, col_src, col_frac, embed_weight, conv1_weight, conv2_weight, cotangent):
    channels = coarse.shape[0]
    cells = jnp.transpose(coarse, (1, 2, 0)).reshape(CELLS, channels)
    lines = [v.reshape(1, -1) for v in (row_src, row_frac, col_src, col_frac)]
    results = pl.pallas_call(
        kernel,
        out_shape=[pltpu.VMEM(shape, kind) for shape, kind in RESULTS],
        in_specs=[pl.BlockSpec(memory_space=pl.ANY)] * 9,
        out_specs=[pl.BlockSpec(memory_space=pl.ANY)] * 4,
        scratch_shapes=scratch_list(channels),
        compiler_params=pltpu.CompilerParams(
            collective_id=0, has_side_effects=True, vmem_limit_bytes=56 * 2**20
        ),
    )(cells, *lines, embed_weight, conv1_weight, conv2_weight, cotangent)
    features, grad_embed, grad_conv1, grad_conv2 = pl.pallas_call(
        write_out,
        out_shape=[jax.ShapeDtypeStruct(shape, kind) for shape, kind in RESULTS],
        in_specs=[pl.BlockSpec(memory_space=pl.ANY)] * 4,
        out_specs=[pl.BlockSpec(memory_space=pl.ANY)] * 4,
        scratch_shapes=[pltpu.SemaphoreType.DMA((4,))],
    )(*[pltpu.with_memory_space_constraint(r, pltpu.VMEM) for r in results])
    taps = (3, 3, HID, HID)
    grad_embed = grad_embed.reshape(EMBED_TILES * 16, HID)[:channels]
    return (features, grad_embed, grad_conv1.reshape(taps), grad_conv2.reshape(taps))


def solution(mesh):
    in_specs = (
        P(None, "lat", "lon"),
        P("lat"),
        P("lat"),
        P("lon"),
        P("lon"),
        P(),
        P(),
        P(),
        P("lat", "lon", None),
    )
    out_specs = (P("lat", "lon", None), P(), P(), P())
    return jax.shard_map(
        on_device, mesh=mesh, in_specs=in_specs, out_specs=out_specs, check_vma=False
    )
```

```python
import functools
import math

import jax
import jax.numpy as jnp
from jax import lax
from jax.experimental import pallas as pl
from jax.experimental.pallas import tpu as pltpu
from jax.sharding import PartitionSpec as P

MESH = pl.DeviceIdType.MESH
BF = jnp.bfloat16
F32 = jnp.float32

ROWS = 32
COLS = 128
WIDE = 144
HID = 128
CROW = 4
CCOL = 8
CELLS = CROW * CCOL
PACK = 48
TILES = 72
HALF = 36
PIECE = 3
OWNERS = 12


def owner_rank(plane):
    x, y = plane // 4, lax.rem(plane, 4)
    return x != y, jnp.minimum(x * 3 + y - (y > x).astype(jnp.int32), OWNERS - 1)

EMBED_TILES = 5
DIRS = [(-1, -1), (-1, 1), (1, -1), (1, 1), (-1, 0), (1, 0), (0, -1), (0, 1)]
FAR_FIRST = [(d // 4, d % 4) for d in range(1, 16)]
FAR_FIRST.sort(key=lambda s: -min(s[0], 4 - s[0]) - min(s[1], 4 - s[1]))


def dot(a, b):
    return jnp.dot(a, b, preferred_element_type=F32)


def dot_t(a, b):
    return lax.dot_general(a, b, (((0,), (0,)), ((), ())), preferred_element_type=F32)


def halves(x):
    hi = x.astype(BF)
    return hi, (x - hi.astype(F32)).astype(BF)


def spread_taps(w_ref, out_ref, back):
    zero = jnp.zeros((HID, HID), BF)
    for b in range(3):
        for a in range(3):
            block = w_ref[2 - a, 2 - b].T if back else w_ref[a, b]
            for s in range(2):
                k = a + s
                out_ref[pl.ds((k * 3 + b) * HID, HID), pl.ds(s * HID, HID)] = block
        out_ref[pl.ds(b * HID, HID), pl.ds(HID, HID)] = zero
        out_ref[pl.ds((9 + b) * HID, HID), pl.ds(0, HID)] = zero


def store_shifted(ref, pair, side, x):
    axis = x.ndim - 2
    ref[pair, side, :, pl.ds(HID, HID)] = x.astype(BF)
    ref[pair, side, :, pl.ds(0, HID)] = pltpu.roll(x, 1, axis).astype(BF)
    ref[pair, side, :, pl.ds(2 * HID, HID)] = pltpu.roll(x, WIDE - 1, axis).astype(BF)


def four_rows(ref, first, count, width, start=0):
    rows = [
        ref[pl.ds(first + k // 2, count), k % 2, pl.ds(start, width), :].reshape(count * width, 3 * HID)
        for k in range(4)
    ]
    return jnp.concatenate(rows, axis=-1)


def coarse_setup(lat, lon, nb_ref, cells_ref, rowmix_ref, colmix_ref):
    for block in range(9):
        dy, dx = block // 3, block % 3
        cells_ref[pl.ds(dy * CROW, CROW), pl.ds(dx * CCOL, CCOL), :] = (
            nb_ref[block, pl.ds(0, CELLS), :].astype(F32).reshape(CROW, CCOL, HID)
        )

    def line(block):
        return nb_ref[block, pl.ds(CELLS, 16), :].astype(F32)

    lane = lax.broadcasted_iota(jnp.int32, (16, HID), 1)
    rows = jnp.where(
        lane < 2,
        pltpu.roll(line(1), 98, 1),
        jnp.where(lane < 34, pltpu.roll(line(4), 2, 1), pltpu.roll(line(7), 34, 1)),
    )
    lane = lane[0:1]
    frac = rows[1:2] + rows[2:3] + rows[3:4]
    start = ((lane + 30) // 8 - 1).astype(F32)
    place = rows[0:1] - (lat * CROW - CROW).astype(F32) - start
    fine_row = lat * ROWS + lane - 2
    inside = ((fine_row >= 0) & (fine_row < 8 * ROWS)).astype(F32)
    for m in range(4):
        weight = jnp.where(place == float(m), 1.0 - frac, 0.0) + jnp.where(
            place == float(m - 1), frac, 0.0
        )
        rowmix_ref[pl.ds(m, 1), :] = weight * inside

    lane = lax.broadcasted_iota(jnp.int32, (16, HID), 1)
    edge = jnp.where(lane < 8, line(5), pltpu.roll(line(3), 16, 1))
    tables = []
    for part in (line(4), edge):
        frac = part[5:6] + part[6:7] + part[7:8]
        spot = part[4:5] - (lon * CCOL - CCOL).astype(F32)
        spot = jnp.where(spot < 0.0, spot + 128.0, spot)
        spot = jnp.where(spot >= 128.0, spot - 128.0, spot)
        cell = lax.broadcasted_iota(jnp.int32, (32, HID), 0).astype(F32)
        tables.append(
            jnp.where(cell == spot, 1.0 - frac, 0.0) + jnp.where(cell == spot + 1.0, frac, 0.0)
        )
    hi, lo = halves(jnp.concatenate(tables, axis=-1))
    colmix_ref[pl.ds(0, 32), :] = hi
    colmix_ref[pl.ds(32, 32), :] = lo


def spread_own(cot_ref, c3_ref):
    def step(q, carry):
        for t in range(2):
            x = cot_ref[2 * q + t].astype(F32)
            own = pl.ds(0, COLS)
            c3_ref[q + 1, t, own, pl.ds(HID, HID)] = cot_ref[2 * q + t]
            c3_ref[q + 1, t, own, pl.ds(0, HID)] = pltpu.roll(x, 1, 0).astype(BF)
            c3_ref[q + 1, t, own, pl.ds(2 * HID, HID)] = pltpu.roll(x, COLS - 1, 0).astype(BF)
        return carry

    lax.fori_loop(0, ROWS // 2, step, 0)


def gather_columns(cot_ref, colpack_ref):
    spot = lax.broadcasted_iota(jnp.int32, (16, HID), 0) // 2
    for side, start in ((0, 0), (1, COLS - 16)):
        for g in range(ROWS // 8):
            total = None
            for n in range(8):
                x = cot_ref[8 * g + n, pl.ds(start, 16)].astype(F32)
                shift = (2 * n + 2 * side) % 16
                x = pltpu.roll(x, shift, 0) if shift else x
                total = x if n == 0 else jnp.where(spot == n, x, total)
            colpack_ref[side, g] = total.astype(BF)


def beside(colhalo_ref, tile, n):
    near = lax.broadcasted_iota(jnp.int32, (16, HID), 0) < 8
    right = colhalo_ref[1, tile].astype(F32)
    left = colhalo_ref[0, tile].astype(F32)
    right = pltpu.roll(right, 16 - 2 * n, 0) if n else right
    left = pltpu.roll(left, 14 - 2 * n, 0) if n < 7 else left
    return jnp.where(near, right, left)


def close_columns(cot_ref, colhalo_ref, c3_ref):
    def step(g, carry):
        for n in range(8):
            r = 8 * g + n
            last = cot_ref[r, pl.ds(COLS - 16, 16)].astype(F32)
            first = cot_ref[r, pl.ds(0, 16)].astype(F32)
            x = jnp.concatenate([last, beside(colhalo_ref, g, n), first], axis=0)
            west = pltpu.roll(x, 1, 0).astype(BF)
            east = pltpu.roll(x, 47, 0).astype(BF)
            wide = pl.ds(COLS, 16)
            q, t = 4 * g + n // 2 + 1, n % 2
            c3_ref[q, t, wide, pl.ds(HID, HID)] = x[16:32].astype(BF)
            c3_ref[q, t, wide, pl.ds(0, HID)] = west[16:32]
            c3_ref[q, t, pl.ds(0, 16), pl.ds(0, HID)] = west[32:48]
            c3_ref[q, t, pl.ds(COLS - 16, 32), pl.ds(2 * HID, HID)] = east[0:32]
        return carry

    lax.fori_loop(0, ROWS // 8, step, 0)


def close_rows(lat, rowhalo_ref, colhalo_ref, c3_ref):
    top = (lat > 0).astype(F32)
    bottom = (lat < 7).astype(F32)
    for t in range(2):
        x = jnp.concatenate([rowhalo_ref[0, t].astype(F32), beside(colhalo_ref, 4, 6 + t)], axis=0)
        store_shifted(c3_ref, 0, t, x * top)
        x = jnp.concatenate([rowhalo_ref[1, t].astype(F32), beside(colhalo_ref, 5, t)], axis=0)
        store_shifted(c3_ref, 17, t, x * bottom)


def back_inside(c3_ref, w2t_ref, back_ref):
    y = dot(four_rows(c3_ref, 1, 15, 96, 16), w2t_ref[...])
    back_ref[pl.ds(1, 15), pl.ds(16, 96), :] = y.reshape(15, 96, 2 * HID)


def back_beside(c3_ref, w2t_ref, back_ref):
    parts = [four_rows(c3_ref, 1, 15, 16, 0), four_rows(c3_ref, 1, 15, 32, COLS - 16)]
    y = dot(jnp.concatenate(parts, axis=0), w2t_ref[...])
    back_ref[pl.ds(1, 15), pl.ds(0, 16), :] = y[0:240].reshape(15, 16, 2 * HID)
    back_ref[pl.ds(1, 15), pl.ds(COLS - 16, 32), :] = y[240:720].reshape(15, 32, 2 * HID)


def back_ends(c3_ref, w2t_ref, back_ref):
    parts = [four_rows(c3_ref, 0, 1, WIDE), four_rows(c3_ref, 16, 1, WIDE)]
    y = dot(jnp.concatenate(parts, axis=0), w2t_ref[...])
    back_ref[0] = y[0:WIDE]
    back_ref[16] = y[WIDE : 2 * WIDE]


def lift_and_hide(lat, embed_ref, cells_ref, rowmix_ref, colmix_ref, w1_ref, l3_ref, h3_ref, slope_ref):
    hi, lo = colmix_ref[pl.ds(0, 32), :], colmix_ref[pl.ds(32, 32), :]
    mixer = jnp.concatenate([hi, lo, hi], axis=0).T[0:WIDE]
    mix = rowmix_ref[...]
    step = 6

    def lift(start):
        rows = []
        for i in range(start, start + step):
            first = (i + 30) // 8 - 1
            total = None
            for m in range(4):
                term = mix[m : m + 1, i : i + 1] * cells_ref[first + m]
                total = term if total is None else total + term
            rows.append(total)
        wide = jnp.concatenate(rows, axis=-1)
        wide = jnp.concatenate([wide, jnp.zeros((8, step * HID), F32)], axis=0)
        hi, lo = halves(wide)
        fine = dot(mixer, jnp.concatenate([hi, hi, lo], axis=0)).astype(BF)
        fine = jnp.concatenate([fine[:, n * HID : (n + 1) * HID] for n in range(step)], axis=0)
        lifted = dot(fine, embed_ref[...])
        for n in range(step):
            i = start + n
            store_shifted(l3_ref, i // 2, i % 2, lifted[n * WIDE : (n + 1) * WIDE])

    def finish(pre_all, first, count):
        for p in range(count):
            for s in range(2):
                pre = pre_all[p * WIDE : (p + 1) * WIDE, s * HID : (s + 1) * HID]
                sig = 0.5 + 0.5 * jnp.tanh(0.5 * pre)
                hidden = pre * sig
                slope = sig + hidden * (1.0 - sig)
                if first + p == 0 and s == 0:
                    inside = (lat > 0).astype(F32)
                    hidden, slope = hidden * inside, slope * inside
                if first + p == 16 and s == 1:
                    inside = (lat < 7).astype(F32)
                    hidden, slope = hidden * inside, slope * inside
                h3_ref[first + p, s, :, pl.ds(HID, HID)] = hidden.astype(BF)
                slope_ref[first + p, :, pl.ds(s * HID, HID)] = slope

    waiting = None
    lift(0)
    lift(step)
    for first in range(0, 17, 3):
        count = min(3, 17 - first)
        pre_all = dot(four_rows(l3_ref, first, count, WIDE), w1_ref[...])
        if 2 * first + 2 * step < ROWS + 4:
            lift(2 * first + 2 * step)
        if waiting is not None:
            finish(*waiting)
        waiting = (pre_all, first, count)
    finish(*waiting)


def shift_hidden(h3_ref):
    def step(p, carry):
        for s in range(2):
            x = h3_ref[p, s, :, pl.ds(HID, HID)].astype(F32)
            h3_ref[p, s, :, pl.ds(0, HID)] = pltpu.roll(x, 1, 0).astype(BF)
            h3_ref[p, s, :, pl.ds(2 * HID, HID)] = pltpu.roll(x, WIDE - 1, 0).astype(BF)
        return carry

    lax.fori_loop(0, 17, step, 0)


def make_delta(back_ref, slope_ref, d3_ref, first, count):
    for p in range(first, first + count):
        for s in range(2):
            lanes = pl.ds(s * HID, HID)
            store_shifted(d3_ref, p, s, back_ref[p, :, lanes] * slope_ref[p, :, lanes])


def rows_from(ref, start, lanes, count=ROWS):
    q, odd, half = start // 2, start % 2, count // 2
    if odd == 0:
        return ref[pl.ds(q, half), :, pl.ds(0, COLS), lanes].reshape(count * COLS, -1)
    parts = [
        ref[pl.ds(q, half), 1, pl.ds(0, COLS), lanes],
        ref[pl.ds(q + 1, half), 0, pl.ds(0, COLS), lanes],
    ]
    return jnp.stack(parts, axis=1).reshape(count * COLS, -1)


def tap_products(v_ref, u_ref, runs):
    left, right = [[], [], []], []
    left_two, right_two = [[], [], [], []], [[], []]
    for v_start, u_start, count in runs:
        turned = []
        for n in range(v_start, v_start + count + 2):
            turned.append(v_ref[n // 2, n % 2, pl.ds(0, COLS), pl.ds(HID, HID)].T)
        for a in range(3):
            left[a] += turned[a : a + count]
        for a in range(4):
            left_two[a] += turned[a : a + count : 2]
        right.append(rows_from(u_ref, u_start, pl.ds(0, 2 * HID), count))
        for s in range(2):
            n = u_start + s
            rows = u_ref[pl.ds(n // 2, count // 2), n % 2, pl.ds(0, COLS), pl.ds(2 * HID, HID)]
            right_two[s].append(rows.reshape(count // 2 * COLS, HID))

    def stack(lines):
        return jnp.concatenate([jnp.concatenate(line, axis=1) for line in lines], axis=0)

    wide = dot(stack(left), jnp.concatenate(right, axis=0))
    last = dot(stack(left_two), jnp.concatenate([jnp.concatenate(x, axis=0) for x in right_two], axis=-1))
    blocks = []
    for a in range(3):
        line = wide[a * HID : (a + 1) * HID]
        third = last[a * HID : (a + 1) * HID, 0:HID] + last[(a + 1) * HID : (a + 2) * HID, HID : 2 * HID]
        blocks.append([line[:, 0:HID], line[:, HID : 2 * HID], third])
    return blocks


def store_taps(blocks, out_ref):
    for a in range(3):
        for b in range(3):
            out_ref[pl.ds((a * 3 + b) * 8, 8)] = blocks[a][2 - b].reshape(8, 16, HID).astype(BF)


def weight_grad(v_ref, v_start, u_ref, u_start, out_ref):
    store_taps(tap_products(v_ref, u_ref, [(v_start, u_start, ROWS)]), out_ref)


def delta_inside(back_ref, slope_ref, d3_ref, l3_ref, held_ref):
    make_delta(back_ref, slope_ref, d3_ref, 1, 9)
    blocks = tap_products(l3_ref, d3_ref, [(3, 3, 16)])
    make_delta(back_ref, slope_ref, d3_ref, 10, 6)
    for a in range(3):
        for n in range(3):
            held_ref[a, n] = blocks[a][n]


def delta_ends(back_ref, slope_ref, d3_ref, l3_ref, held_ref, out_ref):
    make_delta(back_ref, slope_ref, d3_ref, 0, 1)
    make_delta(back_ref, slope_ref, d3_ref, 16, 1)
    blocks = tap_products(l3_ref, d3_ref, [(1, 1, 2), (19, 19, 14)])
    store_taps([[blocks[a][n] + held_ref[a, n] for n in range(3)] for a in range(3)], out_ref)


def back_to_embed(first, count, d3_ref, w1t_ref, cot_ref, rowmix_ref, colmix_ref, down_ref):
    y = dot(four_rows(d3_ref, first, count, COLS), w1t_ref[...])
    rows = []
    for p in range(count):
        for s in range(2):
            part = y[p * COLS : (p + 1) * COLS, s * HID : (s + 1) * HID]
            rows.append((cot_ref[2 * (first + p) + s].astype(F32) + part).astype(BF))
    low = dot(colmix_ref[:, pl.ds(0, COLS)], jnp.concatenate(rows, axis=-1))
    low = low[0:32] + low[32:64]
    mix = rowmix_ref[...]
    sums = {}
    for n in range(2 * count):
        i = 2 * first + n + 2
        base = (i + 30) // 8 - 1
        part = low[:, n * HID : (n + 1) * HID]
        for m in range(4):
            term = mix[m : m + 1, i : i + 1] * part
            sums[base + m] = term if base + m not in sums else sums[base + m] + term
    for j, value in sums.items():
        down_ref[j] = down_ref[j] + value


def embed_grad(cells_ref, down_ref, out_ref):
    window = cells_ref[...].reshape(12 * 24, HID).astype(BF)
    down = jnp.concatenate([down_ref[j, pl.ds(0, 24), :] for j in range(12)], axis=0)
    hi, lo = halves(down)
    grad = dot_t(window, hi) + dot_t(window, lo)
    out_ref[...] = grad[0 : EMBED_TILES * 16].reshape(EMBED_TILES, 16, HID).astype(BF)


def features_of(first, count, h3_ref, l3_ref, w2_ref, feat_ref):
    y = dot(four_rows(h3_ref, first, count, COLS), w2_ref[...])
    for p in range(count):
        for s in range(2):
            part = y[p * COLS : (p + 1) * COLS, s * HID : (s + 1) * HID]
            own = l3_ref[first + p + 1, s, pl.ds(0, COLS), pl.ds(HID, HID)].astype(F32)
            feat_ref[2 * (first + p) + s] = (own + part).astype(BF)


class Place:
    def __init__(self):
        self.lat = lax.axis_index("lat")
        self.lon = lax.axis_index("lon")
        self.core = lax.rem(self.lon, 2)
        self.z = lax.rem(self.lat, 2) * 2 + lax.rem(self.lon // 2, 2)
        self.plane = self.lon // 4 * 4 + self.lat // 2
        self.mate = (self.lat, self.lon + 1 - 2 * self.core)
        x, y = self.plane // 4, lax.rem(self.plane, 4)
        self.planes = [lax.rem(x + a, 4) * 4 + lax.rem(y + b, 4) for a, b in FAR_FIRST]
        self.plane_mates = [self.spot(q, self.z) for q in self.planes]
        self.x_mates = [self.spot(lax.rem(x + d, 4) * 4 + y, self.z) for d in range(1, 4)]
        self.y_mates = [self.spot(x * 4 + lax.rem(y + d, 4), self.z) for d in range(1, 4)]
        self.z_mates = [self.spot(self.plane, lax.rem(self.z + d, 4)) for d in range(1, 4)]
        self.around = [(lax.rem(self.lat + dy + 8, 8), lax.rem(self.lon + dx + 16, 16)) for dy, dx in DIRS]

    def spot(self, plane, z):
        return (lax.rem(plane, 4) * 2 + z // 2, plane // 4 * 4 + lax.rem(z, 2) * 2 + self.core)


class Exchange:
    def __init__(self, copies, span, sems):
        self.copies = copies
        self.whole = [pltpu.make_async_copy(span, span, sem) for sem in sems]

    def start(self):
        for c in self.copies:
            c.start()

    def arrive(self):
        self.whole[1].wait()

    def sent(self):
        self.whole[0].wait()


def remote(src, dst, sems, target):
    return pltpu.make_async_remote_copy(
        src_ref=src, dst_ref=dst, send_sem=sems[0], recv_sem=sems[1], device_id=target, device_id_type=MESH
    )


class GradSum:
    def __init__(self, place, part, paired, half, got, mine, other, final, twin, sems):
        self.part, self.paired, self.half, self.got = part, paired, half, got
        self.mine, self.other, self.final, self.twin = mine, other, final, twin
        pairs = [(sems.at[2 * n], sems.at[2 * n + 1]) for n in range(5)]
        self.place = place
        self.owner, rank = owner_rank(place.plane)
        self.keep = place.core * HALF
        self.own = pl.ds(rank * PIECE, PIECE)
        away = part.at[pl.ds(HALF - self.keep, HALF)]
        self.pair = Exchange([remote(away, paired, pairs[0], place.mate)], paired, pairs[0])
        self.scatter_sems, self.gather_sems = pairs[1], pairs[3]
        self.column = Exchange(
            [remote(mine, other.at[n], pairs[2], t) for n, t in enumerate(place.z_mates)], other, pairs[2]
        )
        self.swap = Exchange([remote(final, twin, pairs[4], place.mate)], twin, pairs[4])

    def take(self, ref, count, sem):
        span = ref.at[pl.ds(0, count * PIECE)]
        pltpu.make_async_copy(span, span, sem).wait()

    def take_others(self, ref, sem):
        @pl.when(self.owner)
        def _():
            self.take(ref, OWNERS - 1, sem)

        @pl.when(jnp.logical_not(self.owner))
        def _():
            self.take(ref, OWNERS, sem)

    def step_pair(self):
        self.pair.start()

    def step_scatter(self):
        self.pair.arrive()
        total = self.part[pl.ds(self.keep, HALF)].astype(F32) + self.paired[...].astype(F32)
        self.half[...] = total.astype(BF)
        for n, (q, t) in enumerate(zip(self.place.planes, self.place.plane_mates)):
            owner, rank = owner_rank(q)

            @pl.when(owner)
            def _():
                piece = self.half.at[pl.ds(rank * PIECE, PIECE)]
                remote(piece, self.got.at[pl.ds(n * PIECE, PIECE)], self.scatter_sems, t).start()

    def step_column(self):
        @pl.when(self.owner)
        def _():
            self.take(self.got, 15, self.scatter_sems[1])
            total = self.half[self.own].astype(F32)
            for n in range(15):
                total = total + self.got[pl.ds(n * PIECE, PIECE)].astype(F32)
            self.mine[...] = total.astype(BF)
            self.column.start()

    def step_gather(self):
        @pl.when(self.owner)
        def _():
            self.column.arrive()
            total = self.mine[...].astype(F32)
            for n in range(3):
                total = total + self.other[n].astype(F32)
            self.final[self.own] = total.astype(BF)
            for t in self.place.plane_mates:
                remote(self.final.at[self.own], self.final.at[self.own], self.gather_sems, t).start()

    def step_swap(self, full_ref, out_ref, sem, scale):
        self.take_others(self.final, self.gather_sems[1])
        self.swap.start()
        self.outs = [
            pltpu.make_async_copy(full_ref.at[part], out_ref.at[part], sem.at[n])
            for n, part in enumerate((pl.ds(self.keep, HALF), pl.ds(HALF - self.keep, HALF)))
        ]
        full_ref[pl.ds(self.keep, HALF)] = self.final[...].astype(F32) * scale
        self.outs[0].start()

    def finish(self, full_ref, scale):
        self.swap.arrive()
        full_ref[pl.ds(HALF - self.keep, HALF)] = self.twin[...].astype(F32) * scale
        self.outs[1].start()

    def drain(self):
        self.pair.sent()
        self.swap.sent()
        self.take_others(self.half, self.scatter_sems[0])

        @pl.when(self.owner)
        def _():
            self.column.sent()
            self.take(self.got, 15, self.gather_sems[0])

        for out in self.outs:
            out.wait()


class SmallSum:
    def __init__(self, place, parts, slots, sems):
        self.parts, self.slots = parts, slots
        self.keep = pl.ds(place.core * 2, 3)
        self.away = pl.ds(2 - place.core * 2, 3)
        self.steps = []
        base = 0
        for g, targets in enumerate([[place.mate], place.z_mates, place.x_mates, place.y_mates, [place.mate]]):
            size = EMBED_TILES if g == 0 else 3
            pair = (sems.at[2 * g], sems.at[2 * g + 1])
            copies = []
            for n, t in enumerate(targets, base):
                copies.append(remote(parts.at[g, pl.ds(0, size)], slots.at[n, pl.ds(0, size)], pair, t))
            span = slots.at[pl.ds(base, len(targets)), pl.ds(0, size)]
            self.steps.append((base, len(targets), Exchange(copies, span, pair)))
            base += len(targets)

    def begin(self):
        self.steps[0][2].start()

    def pass_on(self, g):
        base, count, exchange = self.steps[g]
        exchange.arrive()
        here = self.keep if g == 0 else pl.ds(0, 3)
        total = self.parts[g, here].astype(F32)
        for n in range(count):
            total = total + self.slots[base + n, here].astype(F32)
        self.parts[g + 1, pl.ds(0, 3)] = total.astype(BF)
        self.steps[g + 1][2].start()

    def finish(self, out_ref, scale):
        base, _, exchange = self.steps[4]
        exchange.arrive()
        out_ref[self.away] = self.slots[base, pl.ds(0, 3)].astype(F32) * scale
        out_ref[self.keep] = self.parts[4, pl.ds(0, 3)].astype(F32) * scale
        for _, _, exchange in self.steps:
            exchange.sent()


def pack_block(coarse_ref, row_src_ref, row_frac_ref, col_src_ref, col_frac_ref, lines_ref, pack_ref):
    pack_ref[...] = jnp.zeros_like(pack_ref)
    pack_ref[pl.ds(0, CELLS), pl.ds(0, coarse_ref.shape[1])] = coarse_ref[...]
    lines_ref[...] = jnp.zeros_like(lines_ref)
    for row, src_ref, frac_ref in ((0, row_src_ref, row_frac_ref), (4, col_src_ref, col_frac_ref)):
        lanes = pl.ds(0, src_ref.shape[1])
        lines_ref[pl.ds(row, 1), lanes] = src_ref[...].astype(F32)
        left = frac_ref[...]
        for n in range(1, 4):
            term = left.astype(BF).astype(F32)
            lines_ref[pl.ds(row + n, 1), lanes] = term
            left = left - term
    pack_ref[pl.ds(CELLS, 16), :] = lines_ref[...].astype(BF)


def kernel(
    coarse_hbm, row_src_hbm, row_frac_hbm, col_src_hbm, col_frac_hbm, embed_hbm, conv1_hbm, conv2_hbm, cot_hbm,
    feat_out, gemb_out, g1_out, g2_out,
    feat_ref, gemb_ref, g1_ref, g2_ref, out_sem,
    coarse_ref, row_src_ref, row_frac_ref, col_src_ref, col_frac_ref, embed_in_ref, conv1_ref, conv2_ref, cot_ref,
    lines_ref, pack_ref, embed_ref,
    nb_ref, rowhalo_ref, colpack_ref, colhalo_ref, cells_ref, rowmix_ref, colmix_ref, down_ref,
    w1_ref, w2_ref, w1t_ref, w2t_ref, l3_ref, c3_ref, h3_ref, d3_ref, back_ref, slope_ref, held_ref,
    part1, paired1, half1, got1, mine1, other1, final1, twin1,
    part2, paired2, half2, got2, mine2, other2, final2, twin2, eparts, eslots,
    load_sem, halo_sem, sum_sem,
):
    place = Place()
    lat, lon = place.lat, place.lon
    scale = 1.0 / math.sqrt(8 * ROWS * 16 * COLS)

    def apart(stage, *args):
        @pl.when(lat < 8)
        def _():
            stage(*args)

    barrier = pltpu.get_barrier_semaphore()
    partners = [place.mate] + place.around + place.z_mates + place.plane_mates
    for spot in partners:
        pl.semaphore_signal(barrier, inc=1, device_id=spot, device_id_type=MESH)

    pairs = [
        (coarse_hbm, coarse_ref), (row_src_hbm, row_src_ref), (row_frac_hbm, row_frac_ref),
        (col_src_hbm, col_src_ref), (col_frac_hbm, col_frac_ref), (cot_hbm, cot_ref),
        (conv2_hbm, conv2_ref), (conv1_hbm, conv1_ref), (embed_hbm, embed_in_ref),
    ]
    loads = [pltpu.make_async_copy(src, dst, load_sem.at[n]) for n, (src, dst) in enumerate(pairs)]
    for load in loads:
        load.start()

    packs, columns, rows, corners = [], [], [], []
    pairs = [(halo_sem.at[2 * n], halo_sem.at[2 * n + 1]) for n in range(4)]
    for n, (dy, dx) in enumerate(DIRS):
        slot = (1 - dy) * 3 + 1 - dx
        packs.append(remote(pack_ref, nb_ref.at[slot], pairs[0], place.around[n]))
        if dx == 0:
            src = cot_ref.at[pl.ds(0 if dy == -1 else ROWS - 2, 2)]
            rows.append(remote(src, rowhalo_ref.at[0 if dy == 1 else 1], pairs[2], place.around[n]))
        else:
            side = 0 if dx == -1 else 1
            src = colpack_ref.at[side, {-1: pl.ds(0, 1), 0: pl.ds(0, 4), 1: pl.ds(3, 1)}[dy]]
            dst = colhalo_ref.at[1 - side, {1: pl.ds(4, 1), 0: pl.ds(0, 4), -1: pl.ds(5, 1)}[dy]]
            if dy == 0:
                columns.append(remote(src, dst, pairs[1], place.around[n]))
            else:
                corners.append(remote(src, dst, pairs[3], place.around[n]))
    packs = Exchange(packs, nb_ref.at[pl.ds(0, 8)], pairs[0])
    columns = Exchange(columns, colhalo_ref.at[:, pl.ds(0, 4)], pairs[1])
    rows = Exchange(rows, rowhalo_ref, pairs[2])
    corners = Exchange(corners, colhalo_ref.at[:, pl.ds(4, 2)], pairs[3])
    sum1 = GradSum(place, part1, paired1, half1, got1, mine1, other1, final1, twin1, sum_sem.at[pl.ds(0, 10)])
    sum2 = GradSum(place, part2, paired2, half2, got2, mine2, other2, final2, twin2, sum_sem.at[pl.ds(10, 10)])
    small = SmallSum(place, eparts, eslots, sum_sem.at[pl.ds(20, 10)])

    for load in loads[0:5]:
        load.wait()
    pack_block(coarse_ref, row_src_ref, row_frac_ref, col_src_ref, col_frac_ref, lines_ref, pack_ref)
    pl.semaphore_wait(barrier, len(partners))
    packs.start()
    loads[5].wait()
    gather_columns(cot_ref, colpack_ref)
    columns.start()

    nb_ref[4] = pack_ref[...]
    for load in loads[6:9]:
        load.wait()
    spread_taps(conv2_ref, w2t_ref, True)
    spread_own(cot_ref, c3_ref)
    apart(back_inside, c3_ref, w2t_ref, back_ref)
    spread_taps(conv1_ref, w1_ref, False)
    spread_taps(conv2_ref, w2_ref, False)
    spread_taps(conv1_ref, w1t_ref, True)
    embed_ref[...] = jnp.zeros_like(embed_ref)
    embed_ref[pl.ds(0, embed_in_ref.shape[0]), :] = embed_in_ref[...]
    down_ref[...] = jnp.zeros_like(down_ref)

    columns.arrive()
    close_columns(cot_ref, colhalo_ref, c3_ref)
    apart(back_beside, c3_ref, w2t_ref, back_ref)
    packs.arrive()
    corners.start()
    rows.start()
    coarse_setup(lat, lon, nb_ref, cells_ref, rowmix_ref, colmix_ref)
    apart(lift_and_hide, lat, embed_ref, cells_ref, rowmix_ref, colmix_ref, w1_ref, l3_ref, h3_ref, slope_ref)
    apart(weight_grad, h3_ref, 0, c3_ref, 2, part2)
    sum2.step_pair()
    apart(delta_inside, back_ref, slope_ref, d3_ref, l3_ref, held_ref)
    sum2.step_scatter()
    corners.arrive()
    rows.arrive()
    close_rows(lat, rowhalo_ref, colhalo_ref, c3_ref)
    apart(back_ends, c3_ref, w2t_ref, back_ref)
    apart(delta_ends, back_ref, slope_ref, d3_ref, l3_ref, held_ref, part1)
    sum1.step_pair()
    apart(back_to_embed, 0, 8, d3_ref, w1t_ref, cot_ref, rowmix_ref, colmix_ref, down_ref)
    sum1.step_scatter()
    apart(back_to_embed, 8, 8, d3_ref, w1t_ref, cot_ref, rowmix_ref, colmix_ref, down_ref)
    embed_grad(cells_ref, down_ref, eparts.at[0])
    small.begin()
    shift_hidden(h3_ref)
    done = [
        pltpu.make_async_copy(feat_ref.at[pl.ds(n * 16, 16)], feat_out.at[pl.ds(n * 16, 16)], out_sem.at[n])
        for n in range(2)
    ]
    small.pass_on(0)
    apart(features_of, 0, 8, h3_ref, l3_ref, w2_ref, feat_ref)
    done[0].start()
    sum2.step_column()
    apart(features_of, 8, 8, h3_ref, l3_ref, w2_ref, feat_ref)
    done[1].start()
    sum1.step_column()
    small.pass_on(1)
    sum2.step_gather()
    sum1.step_gather()
    small.pass_on(2)
    sum2.step_swap(g2_ref, g2_out, out_sem.at[pl.ds(2, 2)], scale)
    small.pass_on(3)
    sum1.step_swap(g1_ref, g1_out, out_sem.at[pl.ds(5, 2)], scale)
    sum2.finish(g2_ref, scale)
    small.finish(gemb_ref, scale)
    done.append(pltpu.make_async_copy(gemb_ref, gemb_out, out_sem.at[4]))
    done[2].start()
    sum1.finish(g1_ref, scale)
    for exchange in (packs, columns, rows, corners):
        exchange.sent()
    for copy in done:
        copy.wait()
    sum2.drain()
    sum1.drain()


def write_out(*refs):
    copies = [pltpu.make_async_copy(refs[n], refs[n + 4], refs[-1].at[n]) for n in range(4)]
    for copy in copies:
        copy.start()
    for copy in copies:
        copy.wait()


RESULTS = [
    ((ROWS, COLS, HID), BF),
    ((EMBED_TILES, 16, HID), F32),
    ((TILES, 16, HID), F32),
    ((TILES, 16, HID), F32),
]


def scratch_list(channels=73):
    dma = pltpu.SemaphoreType.DMA
    line = lambda n, kind: pltpu.VMEM((1, n), kind)
    tiles = lambda *n: pltpu.VMEM((*n, 16, HID), BF)
    grad = [
        tiles(TILES), tiles(HALF), tiles(HALF), tiles(15 * PIECE),
        tiles(PIECE), tiles(3, PIECE), tiles(HALF), tiles(HALF),
    ]
    return (
        [pltpu.VMEM(shape, kind) for shape, kind in RESULTS]
        + [dma((7,))]
        + [
            pltpu.VMEM((CELLS, channels), BF),
            line(ROWS, jnp.int32), line(ROWS, F32), line(COLS, jnp.int32), line(COLS, F32),
            pltpu.VMEM((channels, HID), BF),
            pltpu.VMEM((3, 3, HID, HID), BF),
            pltpu.VMEM((3, 3, HID, HID), BF),
            pltpu.VMEM((ROWS, COLS, HID), BF),
            pltpu.VMEM((16, HID), F32),
            pltpu.VMEM((PACK, HID), BF),
            pltpu.VMEM((HID, HID), BF),
            pltpu.VMEM((9, PACK, HID), BF),
            pltpu.VMEM((2, 2, COLS, HID), BF),
            tiles(2, 4),
            tiles(2, 6),
            pltpu.VMEM((12, 24, HID), F32),
            pltpu.VMEM((8, HID), F32),
            pltpu.VMEM((64, 2 * HID), BF),
            pltpu.VMEM((12, 32, HID), F32),
        ]
        + [pltpu.VMEM((12 * HID, 2 * HID), BF)] * 4
        + [pltpu.VMEM((18, 2, WIDE, 3 * HID), BF)] * 2
        + [pltpu.VMEM((17, 2, WIDE, 3 * HID), BF)] * 2
        + [pltpu.VMEM((17, WIDE, 2 * HID), F32)] * 2
        + [pltpu.VMEM((3, 3, HID, HID), F32)]
        + grad
        + grad
        + [tiles(5, EMBED_TILES), tiles(11, EMBED_TILES)]
        + [dma((9,))]
        + [dma((8,)), dma((30,))]
    )


def on_device(coarse, row_src, row_frac, col_src, col_frac, embed_weight, conv1_weight, conv2_weight, cotangent):
    channels = coarse.shape[0]
    cells = jnp.transpose(coarse, (1, 2, 0)).reshape(CELLS, channels)
    lines = [v.reshape(1, -1) for v in (row_src, row_frac, col_src, col_frac)]
    results = pl.pallas_call(
        kernel,
        out_shape=[pltpu.VMEM(shape, kind) for shape, kind in RESULTS],
        in_specs=[pl.BlockSpec(memory_space=pl.ANY)] * 9,
        out_specs=[pl.BlockSpec(memory_space=pl.ANY)] * 4,
        scratch_shapes=scratch_list(channels),
        compiler_params=pltpu.CompilerParams(
            collective_id=0, has_side_effects=True, vmem_limit_bytes=56 * 2**20
        ),
    )(cells, *lines, embed_weight, conv1_weight, conv2_weight, cotangent)
    features, grad_embed, grad_conv1, grad_conv2 = pl.pallas_call(
        write_out,
        out_shape=[jax.ShapeDtypeStruct(shape, kind) for shape, kind in RESULTS],
        in_specs=[pl.BlockSpec(memory_space=pl.ANY)] * 4,
        out_specs=[pl.BlockSpec(memory_space=pl.ANY)] * 4,
        scratch_shapes=[pltpu.SemaphoreType.DMA((4,))],
    )(*[pltpu.with_memory_space_constraint(r, pltpu.VMEM) for r in results])
    taps = (3, 3, HID, HID)
    grad_embed = grad_embed.reshape(EMBED_TILES * 16, HID)[:channels]
    return (features, grad_embed, grad_conv1.reshape(taps), grad_conv2.reshape(taps))


def solution(mesh):
    in_specs = (
        P(None, "lat", "lon"),
        P("lat"),
        P("lat"),
        P("lon"),
        P("lon"),
        P(),
        P(),
        P(),
        P("lat", "lon", None),
    )
    out_specs = (P("lat", "lon", None), P(), P(), P())
    return jax.shard_map(
        on_device, mesh=mesh, in_specs=in_specs, out_specs=out_specs, check_vma=False
    )
```
